32 devices in a mesh: gx: 4 (over z), gy: 8 (over y, x, core).
Axes of the slice: x: 2, y: 2, z: 4, core: 2. Of those that a mesh axis runs over, the one named last changes fastest.
Arguments:
- embeddings: bfloat16 [32768, 768], P(('gx', 'gy')), may hold values from -30 to 30, as said below
- members: int32 [32768], P(('gx', 'gy')), may hold values from 0 to 32767, as said below
- sizes: int32 [4, 25], P('gx'), may hold values from 1 to 4096, as said below
Outputs:
- nearest: float32 [32768], P(('gx', 'gy'))
The draws below stay inside these ranges and needn't reach their ends.
Inputs may be any that keep to these rules, and one draw needn't show every extreme that they name: `members`: a permutation of all images; the 1024 slots of each device hold exactly 32 images stored on each device. `sizes`: each row sums to 8192; its largest entry is exactly 4096. `embeddings`: finite values.
All inputs are finite; a program needn't handle non-finite values.
Results may differ from the reference program's by a relative error of at most 0.00055.
Values may be sent and summed in bfloat16 or wider, within the bound.
No kernel may reach another device: no remote copies, remote signals or barrier semaphores. Data moves between devices by JAX's collectives and lax.ppermute only.
A program may use at most 128 MiB of HBM per device.

```python
import jax
import jax.numpy as jnp
from jax import lax

D = 768
ROWS = 1024
CL_G = 25
GROUPS = 4
OWNERS = 32
SLOTS_G = 8192
MOST = 4096
IMAGES = 32768


def layout(key):
    key_sizes, key_perm, key_shuffle = jax.random.split(key, 3)
    rest = SLOTS_G - MOST

    def one_group(group_key):
        key_cut, key_roll = jax.random.split(group_key)
        cuts = jnp.sort(jax.random.permutation(key_cut, rest - 1)[:CL_G - 2] + 1).astype(jnp.int32)
        bounds = jnp.concatenate([jnp.zeros((1,), jnp.int32), cuts, jnp.full((1,), rest, jnp.int32)])
        parts = bounds[1:] - bounds[:-1]
        counts = jnp.concatenate([jnp.full((1,), MOST, jnp.int32), parts])
        offset = jax.random.randint(key_roll, (), 0, CL_G)
        return jnp.roll(counts, offset)
    sizes = jax.vmap(one_group)(jax.random.split(key_sizes, GROUPS))
    quota = ROWS // OWNERS
    local = jax.vmap(lambda k: jax.random.permutation(k, ROWS))(jax.random.split(key_perm, OWNERS))
    ids = (local + (jnp.arange(OWNERS, dtype=jnp.int32) * ROWS)[:, None]).astype(jnp.int32)
    per_device = jnp.transpose(ids.reshape(OWNERS, OWNERS, quota), (1, 0, 2)).reshape(OWNERS, ROWS)
    shuffle = jax.vmap(lambda k: jax.random.permutation(k, ROWS))(jax.random.split(key_shuffle, OWNERS))
    members = jnp.take_along_axis(per_device, shuffle, axis=1).reshape(IMAGES).astype(jnp.int32)
    return (sizes.astype(jnp.int32), members)


def draw_members(key, part):
    sizes, members = layout(key)
    return members


def draw_sizes(key, part):
    sizes, members = layout(key)
    return sizes


def draw_embeddings(key, part):
    sizes, members = layout(key)
    key = jax.random.fold_in(key, 7)
    key_anchor, key_noise, key_strength = jax.random.split(key, 3)
    ends = jnp.cumsum(sizes, axis=1).astype(jnp.int32)
    starts = ends - sizes
    slot = jnp.arange(IMAGES, dtype=jnp.int32)
    group = slot // SLOTS_G
    within = slot % SLOTS_G
    cluster = jnp.sum((within[:, None] >= ends[group]).astype(jnp.int32), axis=1)
    first = starts[group, cluster]
    count = sizes[group, cluster]
    anchor = group * SLOTS_G + first + jax.random.randint(key_anchor, (IMAGES,), 0, count)
    noise = jnp.clip(jax.random.normal(key_noise, (IMAGES, D), jnp.float32), -5.0, 5.0)
    strength = jax.random.uniform(key_strength, (IMAGES, 1), jnp.float32, 0.0, 2.5)
    rows = noise + strength * noise[anchor]
    placed = jnp.zeros((IMAGES, D), jnp.float32).at[members].set(rows)
    return placed.astype(jnp.bfloat16)


def setup_inputs(seed: int = 0) -> dict:
    keys = jax.random.split(jax.random.key(seed), 4)
    return {
        "embeddings": draw_embeddings(jax.random.fold_in(keys[3], 71), 0),
        "members": draw_members(jax.random.fold_in(keys[3], 71), 0),
        "sizes": draw_sizes(jax.random.fold_in(keys[3], 71), 0),
    }


def cluster_of(position, ends):
    return lax.optimization_barrier(jnp.sum((position[:, None] >= ends[None, :]).astype(jnp.int32), axis=1)).astype(jnp.int32)

def reference(embeddings, members, sizes):
    values = embeddings.astype(jnp.float32)
    squared = lax.optimization_barrier(jnp.sum(values * values, axis=1, keepdims=True))
    unit = (values * lax.rsqrt(squared + 1e-06)).astype(jnp.bfloat16)
    count_tiles = SLOTS_G // ROWS

    def group_part(group):
        ids = lax.dynamic_slice_in_dim(members, (group * SLOTS_G).astype(jnp.int32), SLOTS_G)
        gathered = unit[ids]
        ends = jnp.cumsum(sizes[group]).astype(jnp.int32)
        cluster = cluster_of(jnp.arange(SLOTS_G, dtype=jnp.int32), ends)

        def row_tile(row_index):
            start_row = (row_index * ROWS).astype(jnp.int32)
            left = lax.dynamic_slice_in_dim(gathered, start_row, ROWS)
            left_cl = lax.dynamic_slice_in_dim(cluster, start_row, ROWS)
            left_pos = start_row + jnp.arange(ROWS, dtype=jnp.int32)

            def column(col_index, best):
                start_col = (col_index * ROWS).astype(jnp.int32)
                right = lax.dynamic_slice_in_dim(gathered, start_col, ROWS)
                right_cl = lax.dynamic_slice_in_dim(cluster, start_col, ROWS)
                right_pos = start_col + jnp.arange(ROWS, dtype=jnp.int32)

                def compute(current):
                    sims = lax.dot_general(left, right, (((1,), (1,)), ((), ())), preferred_element_type=jnp.float32)
                    keep = (left_cl[:, None] == right_cl[None, :]) & (left_pos[:, None] != right_pos[None, :])
                    return jnp.maximum(current, lax.optimization_barrier(jnp.max(jnp.where(keep, sims, -1.0), axis=1)))
                touch = (left_cl[0] <= right_cl[-1]) & (right_cl[0] <= left_cl[-1])
                return lax.cond(touch, compute, lambda current: current, best)
            return lax.fori_loop(0, count_tiles, column, jnp.full((ROWS,), -1.0, jnp.float32))
        return lax.map(row_tile, jnp.arange(count_tiles, dtype=jnp.int32)).reshape(SLOTS_G)
    return lax.map(group_part, jnp.arange(GROUPS, dtype=jnp.int32)).reshape(IMAGES)
```

```python
import functools

import jax
import jax.numpy as jnp
from jax import lax
from jax.experimental import pallas as pl
from jax.experimental.pallas import tpu as pltpu
from jax.sharding import PartitionSpec as P

F32 = jnp.float32
BF16 = jnp.bfloat16
I32 = jnp.int32
META = 16
KEYS = 4
BLOCK = 256
VMEM = 48 * 1024 * 1024


def iota(shape, dim):
    return lax.broadcasted_iota(I32, shape, dim)


def dot_nt(a, b):
    return lax.dot_general(a, b, (((1,), (1,)), ((), ())), preferred_element_type=F32)


def dot_nn(a, b):
    return lax.dot_general(a, b, (((1,), (0,)), ((), ())), preferred_element_type=F32)


def one_hot(mask):
    return jnp.where(mask, 1.0, 0.0).astype(BF16)


def log2(value):
    assert value & (value - 1) == 0
    return value.bit_length() - 1


def params(scale=1):
    return pltpu.CompilerParams(vmem_limit_bytes=VMEM)


def request_kernel(dims, place_ref, sizes_ref, members_ref, asked_ref, home_ref):
    n_gx, n_gy, rows, quota = dims
    owners = n_gx * n_gy
    member = members_ref[...]
    owner = lax.shift_right_logical(member, log2(rows))
    row = member & (rows - 1)
    slot = place_ref[1] * rows + iota((1, rows), 1)
    cluster = jnp.zeros((1, rows), I32)
    end = jnp.int32(0)
    for c in range(sizes_ref.shape[1]):
        end = end + sizes_ref[0, c]
        cluster = cluster + (slot >= end).astype(I32)
    mask = iota((owners, rows), 0) == owner
    hot = one_hot(mask)
    before = one_hot(iota((128, 128), 0) < iota((128, 128), 1))
    count = jnp.zeros((owners, 1), F32)
    ranks = []
    for b in range(rows // 128):
        part = hot[:, b * 128:(b + 1) * 128]
        rank = dot_nn(part, before) + count
        part32 = part.astype(F32)
        ranks.append(jnp.sum(part32 * rank, axis=0, keepdims=True))
        count = count + jnp.sum(part32, axis=1, keepdims=True)
    rank = jnp.concatenate(ranks, axis=1).astype(I32)
    place = one_hot(iota((quota, rows), 0) == rank)
    low = (row & 255).astype(F32)
    high = lax.shift_right_logical(row, 8).astype(F32)
    zero = jnp.zeros((owners, rows), F32)

    def pick(value):
        return dot_nt(jnp.where(mask, value, zero).astype(BF16), place)

    asked = pick(low) + 256.0 * pick(high) + float(rows) * pick(cluster.astype(F32))
    asked = asked.astype(I32)
    for o in range(owners):
        asked_ref[o] = asked[o:o + 1, :]
    plane = lax.shift_right_logical(owner, log2(n_gy))
    step = (place_ref[0] - plane) & (n_gx - 1)
    home_ref[0:1, :] = owner & (n_gy - 1)
    home_ref[1:2, :] = step * quota + rank


def select_kernel(dims, pieces, place_ref, asked_ref, unit_ref, *out_refs):
    n_gx, n_gy, rows, quota = dims
    chunk = n_gy * quota
    pick = one_hot((iota((chunk, quota), 0) & (quota - 1)) == iota((chunk, quota), 1))
    block = lax.shift_right_logical(iota((chunk, n_gy), 0), log2(quota))
    own_col = block == iota((chunk, n_gy), 1)
    block_row = lax.shift_right_logical(iota((n_gy, chunk), 1), log2(quota))
    own_row = block_row == iota((n_gy, chunk), 0)
    at = 0
    for step, cuts in pieces:
        plane = (place_ref[0] + step) & (n_gx - 1)
        wanted = jnp.concatenate([asked_ref[plane * n_gy + d] for d in range(n_gy)], axis=0)
        row = wanted & (rows - 1)
        cluster = lax.shift_right_logical(wanted, log2(rows)).astype(F32).astype(BF16)
        low = (row & 255).astype(F32).astype(BF16)
        high = lax.shift_right_logical(row, 8).astype(F32).astype(BF16)
        index = dot_nt(pick, low) + 256.0 * dot_nt(pick, high)
        index = jnp.sum(jnp.where(own_col, index, 0.0), axis=1, keepdims=True).astype(I32)
        flat = jnp.sum(jnp.where(own_row, dot_nt(cluster, pick), 0.0), axis=0, keepdims=True)
        hot = one_hot(iota((chunk, rows), 1) == index)
        found = dot_nn(hot, unit_ref[...]).astype(BF16)
        size = chunk // cuts
        for c in range(cuts):
            ref = out_refs[at]
            ref[0:size, :] = found[c * size:(c + 1) * size, :]
            meta = jnp.zeros((META, unit_ref.shape[1]), F32)
            part = flat[:, c * size:(c + 1) * size]
            fill = jnp.zeros((1, unit_ref.shape[1] - size), F32)
            line = jnp.concatenate([part, fill], axis=1)
            meta = jnp.where(iota(meta.shape, 0) == 0, line, 0.0)
            ref[size:size + META, :] = meta.astype(BF16)
            at += 1


def column(line):
    parts = []
    for b in range(line.shape[1] // 128):
        wide = jnp.broadcast_to(line[:, b * 128:(b + 1) * 128], (128, 128))
        parts.append(wide.T)
    return jnp.concatenate(parts, axis=0)


def wide(col, lanes):
    return jnp.concatenate([col] * (lanes // 128), axis=1)


def step_kernel(size, n_query, olds, last, dims, *refs):
    refs = list(refs)
    new_keys = [refs.pop(0) for _ in range(KEYS)]
    new_queries = [new_keys[0]] + [refs.pop(0) for _ in range(n_query - 1)]
    old = [tuple(refs.pop(0) for _ in range(5)) for _ in olds]
    if last:
        send_ref = refs.pop(0)
    else:
        best_out = [refs.pop(0) for _ in olds]
        keys_out, key_line_out, queries_out, query_line_out, best_new = (refs.pop(0) for _ in range(5))
    if last:
        best_out = [refs.pop(0) for _ in olds]
        keys_out, key_line_out, queries_out, query_line_out, best_new = (refs.pop(0) for _ in range(5))
    key_col, query_col, total = refs

    def place(sources, rows_ref, line_ref, col_ref):
        lines = []
        for t, ref in enumerate(sources):
            rows_ref[t * size:(t + 1) * size, :] = ref[0:size, :]
            lines.append(ref[size:size + META, 0:size].astype(F32)[0:1, :])
        line = jnp.concatenate(lines, axis=1)
        col_ref[...] = column(line)
        for b in range(line.shape[1] // BLOCK):
            line_ref[b] = line[:, b * BLOCK:(b + 1) * BLOCK]

    place(new_keys, keys_out, key_line_out, key_col)
    place(new_queries, queries_out, query_line_out, query_col)
    n_new_q = n_query * size
    n_new_k = KEYS * size

    total[...] = jnp.full(total.shape, -1.0, F32)

    def against(keys_ref, line_ref, own):
        def body(b, carry):
            at = pl.multiple_of(b * BLOCK, BLOCK)
            keys = keys_ref[pl.ds(at, BLOCK), :]
            line = line_ref[b]
            for m in range(n_new_q // BLOCK):
                span = slice(m * BLOCK, (m + 1) * BLOCK)
                sims = dot_nt(queries_out[span, :], keys)
                keep = wide(query_col[span, :], BLOCK) == line
                if own:
                    me = m * BLOCK + iota((BLOCK, BLOCK), 0)
                    it = at + iota((BLOCK, BLOCK), 1)
                    keep = keep & ((me != it) | (me >= size))
                sims = jnp.where(keep, sims, -1.0)
                best = total[span, :]
                for v in range(BLOCK // 128):
                    best = jnp.maximum(best, sims[:, v * 128:(v + 1) * 128])
                total[span, :] = best
            return carry
        lax.fori_loop(0, keys_ref.shape[0] // BLOCK, body, 0)

    against(keys_out, key_line_out, True)
    for keys_ref, line_ref, _, _, _ in old:
        against(keys_ref, line_ref, False)
    parts = []
    for b in range(n_new_q // 128):
        parts.append(jnp.max(total[b * 128:(b + 1) * 128, :].T, axis=0, keepdims=True))
    line = jnp.concatenate(parts, axis=1)
    for b in range(n_new_q // BLOCK):
        best_new[b] = line[:, b * BLOCK:(b + 1) * BLOCK]

    for (_, _, queries_ref, line_ref, best_ref), out_ref in zip(old, best_out):
        def body(b, carry, queries_ref=queries_ref, line_ref=line_ref, best_ref=best_ref, out_ref=out_ref):
            at = pl.multiple_of(b * BLOCK, BLOCK)
            queries = queries_ref[pl.ds(at, BLOCK), :]
            line = line_ref[b]
            best = best_ref[b]
            for m in range(n_new_k // BLOCK):
                span = slice(m * BLOCK, (m + 1) * BLOCK)
                sims = dot_nt(keys_out[span, :], queries)
                keep = wide(key_col[span, :], BLOCK) == line
                sims = jnp.where(keep, sims, -1.0)
                best = jnp.maximum(best, jnp.max(sims, axis=0, keepdims=True))
            out_ref[b] = best
            return carry
        lax.fori_loop(0, queries_ref.shape[0] // BLOCK, body, 0)

    if last:
        n_gx, n_gy, rows, quota = dims
        spread = []
        for q in range(n_query):
            acc = jnp.zeros((n_gy, 128), F32)
            pieces = [(o, r) for o, r in zip(olds, best_out)] + [(last, best_new)]
            for (c, step, first), ref in pieces:
                flat = jnp.concatenate([ref[b] for b in range(ref.shape[0])], axis=1)
                flat = flat[:, q * c:(q + 1) * c]
                block = lax.shift_right_logical(iota((n_gy, c), 1) + first, log2(quota))
                held = jnp.where(block == iota((n_gy, c), 0), flat, 0.0)
                fold = held[:, 0:128]
                for v in range(1, c // 128):
                    fold = fold + held[:, v * 128:(v + 1) * 128]
                shift = 64
                while shift >= quota:
                    fold = fold + pltpu.roll(fold, shift, 1)
                    shift //= 2
                here = lax.shift_right_logical(iota((n_gy, 128), 1), log2(quota)) == step
                acc = acc + jnp.where(here, fold, 0.0)
            spread.append(acc)
        spread = jnp.concatenate(spread, axis=1)
        for d in range(n_gy):
            send_ref[d] = spread[d:d + 1, :]


def finish_kernel(dims, home_ref, back_ref, out_ref):
    n_gx, n_gy, rows, quota = dims
    n_query = n_gy // KEYS
    lines = []
    for q in range(n_gy):
        best = None
        for m in range(n_query):
            part = back_ref[q ^ (KEYS * m)][:, m * 128:(m + 1) * 128]
            best = part if best is None else jnp.maximum(best, part)
        lines.append(best)
    found = jnp.concatenate(lines, axis=0)
    high = found.astype(BF16)
    rest = found - high.astype(F32)
    mid = rest.astype(BF16)
    low = (rest - mid.astype(F32)).astype(BF16)
    here = one_hot(iota((128, rows), 0) == home_ref[1:2, :])
    value = (dot_nn(high, here) + dot_nn(mid, here)) + dot_nn(low, here)
    own = iota((n_gy, rows), 0) == home_ref[0:1, :]
    out_ref[...] = jnp.sum(jnp.where(own, value, 0.0), axis=0, keepdims=True)


def shape(dims, dtype):
    return jax.ShapeDtypeStruct(dims, dtype)


def per_device(embeddings, members, sizes):
    rows = members.shape[0]
    width = embeddings.shape[1]
    n_gx = lax.axis_size("gx")
    n_gy = lax.axis_size("gy")
    owners = n_gx * n_gy
    quota = rows // owners
    chunk = n_gy * quota
    n_query = n_gy // KEYS
    dims = (n_gx, n_gy, rows, quota)
    in_vmem = pl.BlockSpec(memory_space=pltpu.VMEM)
    in_smem = pl.BlockSpec(memory_space=pltpu.SMEM)
    place = jnp.stack([lax.axis_index("gx"), lax.axis_index("gy")]).astype(I32)

    asked, home = pl.pallas_call(
        functools.partial(request_kernel, dims),
        out_shape=(shape((owners, 1, quota), I32), shape((2, rows), I32)),
        in_specs=[in_smem, in_smem, in_vmem],
        out_specs=(in_vmem, in_vmem),
        compiler_params=params(),
        name="request",
    )(place, sizes, members.reshape(1, rows))
    asked = lax.all_to_all(asked, ("gx", "gy"), split_axis=0, concat_axis=0, tiled=True)

    values = embeddings.astype(F32)
    squared = jnp.sum(values * values, axis=1, keepdims=True)
    unit = (values * lax.rsqrt(squared + 1e-06)).astype(BF16)

    order = sorted(range(n_gx), key=lambda k: (min(k, n_gx - k), k))
    pieces = [(k, 2 if k == order[-1] and chunk > 128 else 1) for k in order]
    parts = []
    for k, cuts in pieces:
        size = chunk // cuts
        parts += [(size, k, c * size) for c in range(cuts)]
    found = pl.pallas_call(
        functools.partial(select_kernel, dims, pieces),
        out_shape=[shape((size + META, width), BF16) for size, _, _ in parts],
        in_specs=[in_smem, in_vmem, in_vmem],
        out_specs=[in_vmem] * len(parts),
        compiler_params=params(),
        name="select",
    )(place, asked, unit)

    def across(array, step):
        return lax.ppermute(array, "gx", [(i, (i + step) % n_gx) for i in range(n_gx)])

    def swap(array, mask):
        return lax.ppermute(array, "gy", [(i, i ^ mask) for i in range(n_gy)])

    tiles = []
    for (size, k, first), array in zip(parts, found):
        tile = array if k == 0 else across(array, k)
        other = swap(tile, 2)
        far = [swap(tile, KEYS * m) for m in range(1, n_query)]
        tiles.append(([tile, swap(tile, 1), other, swap(other, 1)], far))

    state = []
    for s, (size, k, first) in enumerate(parts):
        keys, far = tiles[s]
        last = s == len(parts) - 1
        flat_old = [a for group in state for a in group]
        nk, nq = KEYS * size, n_query * size
        new_shapes = [
            shape((nk, width), BF16),
            shape((nk // BLOCK, 1, BLOCK), F32),
            shape((nq, width), BF16),
            shape((nq // BLOCK, 1, BLOCK), F32),
            shape((nq // BLOCK, 1, BLOCK), F32),
        ]
        best_shapes = [shape(group[4].shape, F32) for group in state]
        scratch = [
            pltpu.VMEM((nk, 128), F32),
            pltpu.VMEM((nq, 128), F32),
            pltpu.VMEM((nq, 128), F32),
        ]
        if last:
            kept = best_shapes + new_shapes
            scratch = [pltpu.VMEM(a.shape, a.dtype) for a in kept] + scratch
            out_shapes = [shape((n_gy, 1, n_query * 128), F32)]
        else:
            out_shapes = best_shapes + new_shapes
        out = pl.pallas_call(
            functools.partial(step_kernel, size, n_query, parts[:s], parts[s] if last else None, dims),
            out_shape=out_shapes,
            in_specs=[in_vmem] * (len(keys) + len(far) + len(flat_old)),
            out_specs=[in_vmem] * len(out_shapes),
            scratch_shapes=scratch,
            compiler_params=params(),
            name=f"step{s}",
        )(*keys, *far, *flat_old)
        if last:
            send = out[0]
        else:
            state = [group[:4] + (best,) for group, best in zip(state, out[:s])] + [tuple(out[s:])]

    back = lax.all_to_all(send, "gy", split_axis=0, concat_axis=0, tiled=True)
    out = pl.pallas_call(
        functools.partial(finish_kernel, dims),
        out_shape=shape((1, rows), F32),
        in_specs=[in_vmem, in_vmem],
        out_specs=in_vmem,
        compiler_params=params(),
        name="finish",
    )(home, back)
    return out.reshape(rows)


def solution(mesh):
    return jax.shard_map(
        per_device,
        mesh=mesh,
        in_specs=(P(("gx", "gy"), None), P(("gx", "gy")), P("gx", None)),
        out_specs=P(("gx", "gy")),
        check_vma=False,
    )
```

```python
import functools

import jax
import jax.numpy as jnp
from jax import lax
from jax.experimental import pallas as pl
from jax.experimental.pallas import tpu as pltpu
from jax.sharding import PartitionSpec as P

F32 = jnp.float32
BF16 = jnp.bfloat16
I32 = jnp.int32
META = 16
KEYS = 4
BLOCK = 256
VMEM = 24 * 1024 * 1024


def iota(shape, dim):
    return lax.broadcasted_iota(I32, shape, dim)


def dot_nt(a, b):
    return lax.dot_general(a, b, (((1,), (1,)), ((), ())), preferred_element_type=F32)


def dot_nn(a, b):
    return lax.dot_general(a, b, (((1,), (0,)), ((), ())), preferred_element_type=F32)


def one_hot(mask):
    return jnp.where(mask, 1.0, 0.0).astype(BF16)


def log2(value):
    assert value & (value - 1) == 0
    return value.bit_length() - 1


def params():
    return pltpu.CompilerParams(vmem_limit_bytes=VMEM)


def cost(flops, size):
    return pl.CostEstimate(flops=flops, bytes_accessed=size, transcendentals=0)


def request_kernel(dims, place_ref, sizes_ref, members_ref, asked_ref, home_ref):
    n_gx, n_gy, rows, quota = dims
    owners = n_gx * n_gy
    member = members_ref[...]
    owner = lax.shift_right_logical(member, log2(rows))
    row = member & (rows - 1)
    slot = place_ref[1] * rows + iota((1, rows), 1)
    cluster = jnp.zeros((1, rows), I32)
    end = jnp.int32(0)
    for c in range(sizes_ref.shape[1]):
        end = end + sizes_ref[0, c]
        cluster = cluster + (slot >= end).astype(I32)
    mask = iota((owners, rows), 0) == owner
    hot = one_hot(mask)
    before = one_hot(iota((128, 128), 0) < iota((128, 128), 1))
    count = jnp.zeros((owners, 1), F32)
    ranks = []
    for b in range(rows // 128):
        part = hot[:, b * 128:(b + 1) * 128]
        rank = dot_nn(part, before) + count
        part32 = part.astype(F32)
        ranks.append(jnp.sum(part32 * rank, axis=0, keepdims=True))
        count = count + jnp.sum(part32, axis=1, keepdims=True)
    rank = jnp.concatenate(ranks, axis=1).astype(I32)
    place = one_hot(iota((quota, rows), 0) == rank)
    low = (row & 255).astype(F32)
    high = lax.shift_right_logical(row, 8).astype(F32)
    zero = jnp.zeros((owners, rows), F32)

    def pick(value):
        return dot_nt(jnp.where(mask, value, zero).astype(BF16), place)

    asked = pick(low) + 256.0 * pick(high) + float(rows) * pick(cluster.astype(F32))
    asked = asked.astype(I32)
    for o in range(owners):
        asked_ref[o] = asked[o:o + 1, :]
    plane = lax.shift_right_logical(owner, log2(n_gy))
    step = (place_ref[0] - plane) & (n_gx - 1)
    home_ref[0:1, :] = owner & (n_gy - 1)
    home_ref[1:2, :] = step * quota + rank


def select_kernel(dims, pieces, place_ref, asked_ref, unit_ref, *out_refs):
    n_gx, n_gy, rows, quota = dims
    chunk = n_gy * quota
    pick = one_hot((iota((chunk, quota), 0) & (quota - 1)) == iota((chunk, quota), 1))
    block = lax.shift_right_logical(iota((chunk, n_gy), 0), log2(quota))
    own_col = block == iota((chunk, n_gy), 1)
    block_row = lax.shift_right_logical(iota((n_gy, chunk), 1), log2(quota))
    own_row = block_row == iota((n_gy, chunk), 0)
    at = 0
    for step, cuts in pieces:
        plane = (place_ref[0] + step) & (n_gx - 1)
        wanted = jnp.concatenate([asked_ref[plane * n_gy + d] for d in range(n_gy)], axis=0)
        row = wanted & (rows - 1)
        cluster = lax.shift_right_logical(wanted, log2(rows)).astype(F32).astype(BF16)
        low = (row & 255).astype(F32).astype(BF16)
        high = lax.shift_right_logical(row, 8).astype(F32).astype(BF16)
        index = dot_nt(pick, low) + 256.0 * dot_nt(pick, high)
        index = jnp.sum(jnp.where(own_col, index, 0.0), axis=1, keepdims=True).astype(I32)
        flat = jnp.sum(jnp.where(own_row, dot_nt(cluster, pick), 0.0), axis=0, keepdims=True)
        hot = one_hot(iota((chunk, rows), 1) == index)
        found = dot_nn(hot, unit_ref[...]).astype(BF16)
        size = chunk // cuts
        for c in range(cuts):
            ref = out_refs[at]
            ref[0:size, :] = found[c * size:(c + 1) * size, :]
            meta = jnp.zeros((META, unit_ref.shape[1]), F32)
            part = flat[:, c * size:(c + 1) * size]
            fill = jnp.zeros((1, unit_ref.shape[1] - size), F32)
            line = jnp.concatenate([part, fill], axis=1)
            meta = jnp.where(iota(meta.shape, 0) == 0, line, 0.0)
            ref[size:size + META, :] = meta.astype(BF16)
            at += 1


def column(line):
    parts = []
    for b in range(line.shape[1] // 128):
        wide = jnp.broadcast_to(line[:, b * 128:(b + 1) * 128], (128, 128))
        parts.append(wide.T)
    return jnp.concatenate(parts, axis=0)


def wide(col, lanes):
    return jnp.concatenate([col] * (lanes // 128), axis=1)


def step_kernel(size, n_query, olds, last, dims, *refs):
    refs = list(refs)
    new_keys = [refs.pop(0) for _ in range(KEYS)]
    new_queries = [new_keys[0]] + [refs.pop(0) for _ in range(n_query - 1)]
    old = [tuple(refs.pop(0) for _ in range(5)) for _ in olds]
    if last:
        send_ref = refs.pop(0)
    else:
        best_out = [refs.pop(0) for _ in olds]
        keys_out, key_line_out, queries_out, query_line_out, best_new = (refs.pop(0) for _ in range(5))
    if last:
        best_out = [refs.pop(0) for _ in olds]
        keys_out, key_line_out, queries_out, query_line_out, best_new = (refs.pop(0) for _ in range(5))
    key_col, query_col, total = refs

    def place(sources, rows_ref, line_ref, col_ref):
        lines = []
        for t, ref in enumerate(sources):
            rows_ref[t * size:(t + 1) * size, :] = ref[0:size, :]
            lines.append(ref[size:size + META, 0:size].astype(F32)[0:1, :])
        line = jnp.concatenate(lines, axis=1)
        col_ref[...] = column(line)
        for b in range(line.shape[1] // BLOCK):
            line_ref[b] = line[:, b * BLOCK:(b + 1) * BLOCK]

    place(new_keys, keys_out, key_line_out, key_col)
    place(new_queries, queries_out, query_line_out, query_col)
    n_new_q = n_query * size
    n_new_k = KEYS * size

    total[...] = jnp.full(total.shape, -1.0, F32)

    def against(keys_ref, line_ref, own):
        n_keys = keys_ref.shape[0]
        sims = dot_nt(queries_out[...], keys_ref[...])
        line = jnp.concatenate([line_ref[b] for b in range(n_keys // BLOCK)], axis=1)
        keep = wide(query_col[...], n_keys) == line
        if own:
            me = iota((n_new_q, n_keys), 0)
            it = iota((n_new_q, n_keys), 1)
            keep = keep & ((me != it) | (me >= size))
        sims = jnp.where(keep, sims, -1.0)
        best = total[...]
        for v in range(n_keys // 128):
            best = jnp.maximum(best, sims[:, v * 128:(v + 1) * 128])
        total[...] = best

    against(keys_out, key_line_out, True)
    for keys_ref, line_ref, _, _, _ in old:
        against(keys_ref, line_ref, False)
    parts = []
    for b in range(n_new_q // 128):
        parts.append(jnp.max(total[b * 128:(b + 1) * 128, :].T, axis=0, keepdims=True))
    line = jnp.concatenate(parts, axis=1)
    for b in range(n_new_q // BLOCK):
        best_new[b] = line[:, b * BLOCK:(b + 1) * BLOCK]

    for (_, _, queries_ref, line_ref, best_ref), out_ref in zip(old, best_out):
        n_queries = queries_ref.shape[0]
        sims = dot_nt(keys_out[...], queries_ref[...])
        line = jnp.concatenate([line_ref[b] for b in range(n_queries // BLOCK)], axis=1)
        keep = wide(key_col[...], n_queries) == line
        best = jnp.max(jnp.where(keep, sims, -1.0), axis=0, keepdims=True)
        for b in range(n_queries // BLOCK):
            out_ref[b] = jnp.maximum(best_ref[b], best[:, b * BLOCK:(b + 1) * BLOCK])

    if last:
        n_gx, n_gy, rows, quota = dims
        spread = []
        for q in range(n_query):
            acc = jnp.zeros((n_gy, 128), F32)
            pieces = [(o, r) for o, r in zip(olds, best_out)] + [(last, best_new)]
            for (c, step, first), ref in pieces:
                flat = jnp.concatenate([ref[b] for b in range(ref.shape[0])], axis=1)
                flat = flat[:, q * c:(q + 1) * c]
                block = lax.shift_right_logical(iota((n_gy, c), 1) + first, log2(quota))
                held = jnp.where(block == iota((n_gy, c), 0), flat, 0.0)
                fold = held[:, 0:128]
                for v in range(1, c // 128):
                    fold = fold + held[:, v * 128:(v + 1) * 128]
                shift = 64
                while shift >= quota:
                    fold = fold + pltpu.roll(fold, shift, 1)
                    shift //= 2
                here = lax.shift_right_logical(iota((n_gy, 128), 1), log2(quota)) == step
                acc = acc + jnp.where(here, fold, 0.0)
            spread.append(acc)
        spread = jnp.concatenate(spread, axis=1)
        for d in range(n_gy):
            send_ref[d] = spread[d:d + 1, :]


def finish_kernel(dims, home_ref, back_ref, out_ref):
    n_gx, n_gy, rows, quota = dims
    n_query = n_gy // KEYS
    lines = []
    for q in range(n_gy):
        best = None
        for m in range(n_query):
            part = back_ref[q ^ (KEYS * m)][:, m * 128:(m + 1) * 128]
            best = part if best is None else jnp.maximum(best, part)
        lines.append(best)
    found = jnp.concatenate(lines, axis=0)
    high = found.astype(BF16)
    rest = found - high.astype(F32)
    mid = rest.astype(BF16)
    low = (rest - mid.astype(F32)).astype(BF16)
    here = one_hot(iota((128, rows), 0) == home_ref[1:2, :])
    value = (dot_nn(high, here) + dot_nn(mid, here)) + dot_nn(low, here)
    own = iota((n_gy, rows), 0) == home_ref[0:1, :]
    out_ref[...] = jnp.sum(jnp.where(own, value, 0.0), axis=0, keepdims=True)


def shape(dims, dtype):
    return jax.ShapeDtypeStruct(dims, dtype)


def per_device(embeddings, members, sizes):
    rows = members.shape[0]
    width = embeddings.shape[1]
    n_gx = lax.axis_size("gx")
    n_gy = lax.axis_size("gy")
    owners = n_gx * n_gy
    quota = rows // owners
    chunk = n_gy * quota
    n_query = n_gy // KEYS
    dims = (n_gx, n_gy, rows, quota)
    in_vmem = pl.BlockSpec(memory_space=pltpu.VMEM)
    in_smem = pl.BlockSpec(memory_space=pltpu.SMEM)
    place = jnp.stack([lax.axis_index("gx"), lax.axis_index("gy")]).astype(I32)

    asked, home = pl.pallas_call(
        functools.partial(request_kernel, dims),
        out_shape=(shape((owners, 1, quota), I32), shape((2, rows), I32)),
        in_specs=[in_smem, in_smem, in_vmem],
        out_specs=(in_vmem, in_vmem),
        compiler_params=params(),
        name="request",
    )(place, sizes, members.reshape(1, rows))
    asked = lax.all_to_all(asked, ("gx", "gy"), split_axis=0, concat_axis=0, tiled=True)

    values = embeddings.astype(F32)
    squared = jnp.sum(values * values, axis=1, keepdims=True)
    unit = (values * lax.rsqrt(squared + 1e-06)).astype(BF16)

    order = sorted(range(n_gx), key=lambda k: (min(k, n_gx - k), k))
    pieces = [(k, 2 if k == order[-1] and chunk > 128 else 1) for k in order]
    parts = []
    for k, cuts in pieces:
        size = chunk // cuts
        parts += [(size, k, c * size) for c in range(cuts)]
    found = pl.pallas_call(
        functools.partial(select_kernel, dims, pieces),
        out_shape=[shape((size + META, width), BF16) for size, _, _ in parts],
        in_specs=[in_smem, in_vmem, in_vmem],
        out_specs=[in_vmem] * len(parts),
        compiler_params=params(),
        name="select",
    )(place, asked, unit)

    def across(array, step):
        return lax.ppermute(array, "gx", [(i, (i + step) % n_gx) for i in range(n_gx)])

    def swap(array, mask):
        return lax.ppermute(array, "gy", [(i, i ^ mask) for i in range(n_gy)])

    tiles = []
    for (size, k, first), array in zip(parts, found):
        tile = array if k == 0 else across(array, k)
        other = swap(tile, 2)
        far = [swap(tile, KEYS * m) for m in range(1, n_query)]
        tiles.append(([tile, swap(tile, 1), other, swap(other, 1)], far))

    state = []
    for s, (size, k, first) in enumerate(parts):
        keys, far = tiles[s]
        last = s == len(parts) - 1
        flat_old = [a for group in state for a in group]
        nk, nq = KEYS * size, n_query * size
        new_shapes = [
            shape((nk, width), BF16),
            shape((nk // BLOCK, 1, BLOCK), F32),
            shape((nq, width), BF16),
            shape((nq // BLOCK, 1, BLOCK), F32),
            shape((nq // BLOCK, 1, BLOCK), F32),
        ]
        best_shapes = [shape(group[4].shape, F32) for group in state]
        scratch = [
            pltpu.VMEM((nk, 128), F32),
            pltpu.VMEM((nq, 128), F32),
            pltpu.VMEM((nq, 128), F32),
        ]
        if last:
            kept = best_shapes + new_shapes
            scratch = [pltpu.VMEM(a.shape, a.dtype) for a in kept] + scratch
            out_shapes = [shape((n_gy, 1, n_query * 128), F32)]
        else:
            out_shapes = best_shapes + new_shapes
        out = pl.pallas_call(
            functools.partial(step_kernel, size, n_query, parts[:s], parts[s] if last else None, dims),
            out_shape=out_shapes,
            in_specs=[in_vmem] * (len(keys) + len(far) + len(flat_old)),
            out_specs=[in_vmem] * len(out_shapes),
            scratch_shapes=scratch,
            cost_estimate=cost(2 * width * (nq * nk + sum(nq * a[0].shape[0] + nk * a[2].shape[0] for a in state)), nk * width),
            compiler_params=params(),
            name=f"step{s}",
        )(*keys, *far, *flat_old)
        if last:
            send = out[0]
        else:
            state = [group[:4] + (best,) for group, best in zip(state, out[:s])] + [tuple(out[s:])]

    back = lax.all_to_all(send, "gy", split_axis=0, concat_axis=0, tiled=True)
    out = pl.pallas_call(
        functools.partial(finish_kernel, dims),
        out_shape=shape((1, rows), F32),
        in_specs=[in_vmem, in_vmem],
        out_specs=in_vmem,
        compiler_params=params(),
        name="finish",
    )(home, back)
    return out.reshape(rows)


def solution(mesh):
    return jax.shard_map(
        per_device,
        mesh=mesh,
        in_specs=(P(("gx", "gy"), None), P(("gx", "gy")), P("gx", None)),
        out_specs=P(("gx", "gy")),
        check_vma=False,
    )
```

```python
import functools

import jax
import jax.numpy as jnp
from jax import lax
from jax.experimental import pallas as pl
from jax.experimental.pallas import tpu as pltpu
from jax.sharding import PartitionSpec as P

F32 = jnp.float32
BF16 = jnp.bfloat16
I32 = jnp.int32
META = 16
KEYS = 4
VMEM = 24 * 1024 * 1024


def iota(shape, dim):
    return lax.broadcasted_iota(I32, shape, dim)


def dot_nt(a, b):
    return lax.dot_general(a, b, (((1,), (1,)), ((), ())), preferred_element_type=F32)


def dot_nn(a, b):
    return lax.dot_general(a, b, (((1,), (0,)), ((), ())), preferred_element_type=F32)


def one_hot(mask):
    return jnp.where(mask, 1.0, 0.0).astype(BF16)


def log2(value):
    assert value & (value - 1) == 0
    return value.bit_length() - 1


def params():
    return pltpu.CompilerParams(vmem_limit_bytes=VMEM)


def cost(flops, size):
    return pl.CostEstimate(flops=flops, bytes_accessed=size, transcendentals=0)


def request_kernel(dims, place_ref, sizes_ref, members_ref, asked_ref, home_ref):
    n_gx, n_gy, rows, quota = dims
    owners = n_gx * n_gy
    member = members_ref[...]
    owner = lax.shift_right_logical(member, log2(rows))
    row = member & (rows - 1)
    slot = place_ref[1] * rows + iota((1, rows), 1)
    cluster = jnp.zeros((1, rows), I32)
    end = jnp.int32(0)
    for c in range(sizes_ref.shape[1]):
        end = end + sizes_ref[0, c]
        cluster = cluster + (slot >= end).astype(I32)
    mask = iota((owners, rows), 0) == owner
    hot = one_hot(mask)
    before = one_hot(iota((128, 128), 0) < iota((128, 128), 1))
    count = jnp.zeros((owners, 1), F32)
    ranks = []
    for b in range(rows // 128):
        part = hot[:, b * 128:(b + 1) * 128]
        rank = dot_nn(part, before) + count
        part32 = part.astype(F32)
        ranks.append(jnp.sum(part32 * rank, axis=0, keepdims=True))
        count = count + jnp.sum(part32, axis=1, keepdims=True)
    rank = jnp.concatenate(ranks, axis=1).astype(I32)
    place = one_hot(iota((quota, rows), 0) == rank)
    low = (row & 255).astype(F32)
    high = lax.shift_right_logical(row, 8).astype(F32)
    zero = jnp.zeros((owners, rows), F32)

    def pick(value):
        return dot_nt(jnp.where(mask, value, zero).astype(BF16), place)

    asked = pick(low) + 256.0 * pick(high) + float(rows) * pick(cluster.astype(F32))
    asked = asked.astype(I32)
    for o in range(owners):
        asked_ref[o] = asked[o:o + 1, :]
    plane = lax.shift_right_logical(owner, log2(n_gy))
    step = (place_ref[0] - plane) & (n_gx - 1)
    home_ref[0:1, :] = owner & (n_gy - 1)
    home_ref[1:2, :] = step * quota + rank


def select_kernel(dims, steps, place_ref, asked_ref, unit_ref, *out_refs):
    n_gx, n_gy, rows, quota = dims
    chunk = n_gy * quota
    pick = one_hot((iota((chunk, quota), 0) & (quota - 1)) == iota((chunk, quota), 1))
    block = lax.shift_right_logical(iota((chunk, n_gy), 0), log2(quota))
    own_col = block == iota((chunk, n_gy), 1)
    block_row = lax.shift_right_logical(iota((n_gy, chunk), 1), log2(quota))
    own_row = block_row == iota((n_gy, chunk), 0)
    for step, ref in zip(steps, out_refs):
        plane = (place_ref[0] + step) & (n_gx - 1)
        wanted = jnp.concatenate([asked_ref[plane * n_gy + d] for d in range(n_gy)], axis=0)
        row = wanted & (rows - 1)
        cluster = lax.shift_right_logical(wanted, log2(rows)).astype(F32).astype(BF16)
        low = (row & 255).astype(F32).astype(BF16)
        high = lax.shift_right_logical(row, 8).astype(F32).astype(BF16)
        index = dot_nt(pick, low) + 256.0 * dot_nt(pick, high)
        index = jnp.sum(jnp.where(own_col, index, 0.0), axis=1, keepdims=True).astype(I32)
        flat = jnp.sum(jnp.where(own_row, dot_nt(cluster, pick), 0.0), axis=0, keepdims=True)
        hot = one_hot(iota((chunk, rows), 1) == index)
        ref[0:chunk, :] = dot_nn(hot, unit_ref[...]).astype(BF16)
        width = unit_ref.shape[1]
        line = jnp.concatenate([flat, jnp.zeros((1, width - chunk), F32)], axis=1)
        ref[chunk:chunk + META, :] = jnp.where(iota((META, width), 0) == 0, line, 0.0).astype(BF16)


def column(line):
    parts = []
    for b in range(line.shape[1] // 128):
        wide = jnp.broadcast_to(line[:, b * 128:(b + 1) * 128], (128, 128))
        parts.append(wide.T)
    return jnp.concatenate(parts, axis=0)


def wide(col, lanes):
    return jnp.concatenate([col] * (lanes // 128), axis=1)


def cluster_line(ref, size, chunk):
    block = ref[size:size + META, 0:chunk].astype(F32)
    return jnp.concatenate([block[r:r + 1, :] for r in range(size // chunk)], axis=1)


def pack_kernel(groups, sizes, chunk, *refs):
    refs = list(refs)
    outs = refs[sum(len(g) for g in groups):]
    for group, out_ref in zip(groups, outs):
        at = 0
        total = sum(sizes[n] for n in group)
        width = out_ref.shape[1]
        meta = jnp.zeros((META, width), F32)
        for name in group:
            ref, size = refs.pop(0), sizes[name]
            out_ref[at:at + size, :] = ref[0:size, :]
            lines = ref[size:size + META, :].astype(F32)
            for r in range(size // chunk):
                meta = jnp.where(iota((META, width), 0) == at // chunk + r, lines[r:r + 1, :], meta)
            at += size
        out_ref[total:total + META, :] = meta.astype(BF16)


def product_kernel(pairs, sizes, chunk, started, close, *refs):
    names = sorted({n for q, ks in pairs for n in [q] + ks})
    queries = [q for q, _ in pairs]
    refs = list(refs)
    rows = {n: refs.pop(0) for n in names}
    state = {q: (refs.pop(0), refs.pop(0)) for q in queries if q in started}
    for q, keys in pairs:
        n_q = sizes[q]
        if close:
            out_ref = refs.pop(0)
        else:
            col_ref, out_ref = refs.pop(0), refs.pop(0)
        if q in started:
            col = state[q][0][...]
            best = state[q][1][...]
        else:
            col = column(cluster_line(rows[q], n_q, chunk))
            best = jnp.full((n_q, 128), -1.0, F32)
        if not close:
            col_ref[...] = col
        for k in keys:
            n_k = sizes[k]
            sims = dot_nt(rows[q][0:n_q, :], rows[k][0:n_k, :])
            keep = wide(col, n_k) == cluster_line(rows[k], n_k, chunk)
            if k == q:
                keep = keep & (iota((n_q, n_k), 0) != iota((n_q, n_k), 1))
            sims = jnp.where(keep, sims, -1.0)
            for v in range(n_k // 128):
                best = jnp.maximum(best, sims[:, v * 128:(v + 1) * 128])
        if close:
            parts = [jnp.max(best[b * 128:(b + 1) * 128, :].T, axis=0, keepdims=True) for b in range(n_q // 128)]
            out_ref[...] = jnp.concatenate(parts, axis=1)
        else:
            out_ref[...] = best


def last_kernel(dims, queries, size, *refs):
    n_gx, n_gy, rows, quota = dims
    chunk = n_gy * quota
    refs = list(refs)
    key_ref = refs.pop(0)
    send_ref = refs.pop()
    keys = key_ref[0:size, :]
    col = column(cluster_line(key_ref, size, chunk))
    spread = {}
    for (m, steps, n_q), row_ref, best_ref in zip(queries, refs[0::2], refs[1::2]):
        sims = dot_nt(keys, row_ref[0:n_q, :])
        keep = wide(col, n_q) == cluster_line(row_ref, n_q, chunk)
        line = jnp.max(jnp.where(keep, sims, -1.0), axis=0, keepdims=True)
        line = jnp.maximum(line, best_ref[...])
        for c, step in enumerate(steps):
            flat = line[:, c * chunk:(c + 1) * chunk]
            block = lax.shift_right_logical(iota((n_gy, chunk), 1), log2(quota))
            held = jnp.where(block == iota((n_gy, chunk), 0), flat, 0.0)
            fold = held[:, 0:128]
            for v in range(1, chunk // 128):
                fold = fold + held[:, v * 128:(v + 1) * 128]
            shift = 64
            while shift >= quota:
                fold = fold + pltpu.roll(fold, shift, 1)
                shift //= 2
            here = lax.shift_right_logical(iota((n_gy, 128), 1), log2(quota)) == step
            fold = jnp.where(here, fold, 0.0)
            spread[m] = spread[m] + fold if m in spread else fold
    spread = jnp.concatenate([spread[m] for m in sorted(spread)], axis=1)
    for d in range(n_gy):
        send_ref[d] = spread[d:d + 1, :]


def finish_kernel(dims, home_ref, back_ref, out_ref):
    n_gx, n_gy, rows, quota = dims
    n_query = n_gy // KEYS
    lines = []
    for q in range(n_gy):
        best = None
        for m in range(n_query):
            part = back_ref[q ^ (KEYS * m)][:, m * 128:(m + 1) * 128]
            best = part if best is None else jnp.maximum(best, part)
        lines.append(best)
    found = jnp.concatenate(lines, axis=0)
    high = found.astype(BF16)
    rest = found - high.astype(F32)
    mid = rest.astype(BF16)
    low = (rest - mid.astype(F32)).astype(BF16)
    here = one_hot(iota((128, rows), 0) == home_ref[1:2, :])
    value = (dot_nn(high, here) + dot_nn(mid, here)) + dot_nn(low, here)
    own = iota((n_gy, rows), 0) == home_ref[0:1, :]
    out_ref[...] = jnp.sum(jnp.where(own, value, 0.0), axis=0, keepdims=True)


def shape(dims, dtype):
    return jax.ShapeDtypeStruct(dims, dtype)


def per_device(embeddings, members, sizes):
    rows = members.shape[0]
    width = embeddings.shape[1]
    n_gx = lax.axis_size("gx")
    n_gy = lax.axis_size("gy")
    owners = n_gx * n_gy
    quota = rows // owners
    chunk = n_gy * quota
    n_query = n_gy // KEYS
    dims = (n_gx, n_gy, rows, quota)
    in_vmem = pl.BlockSpec(memory_space=pltpu.VMEM)
    in_smem = pl.BlockSpec(memory_space=pltpu.SMEM)
    place = jnp.stack([lax.axis_index("gx"), lax.axis_index("gy")]).astype(I32)

    asked, home = pl.pallas_call(
        functools.partial(request_kernel, dims),
        out_shape=(shape((owners, 1, quota), I32), shape((2, rows), I32)),
        in_specs=[in_smem, in_smem, in_vmem],
        out_specs=(in_vmem, in_vmem),
        compiler_params=params(),
        name="request",
    )(place, sizes, members.reshape(1, rows))
    asked = lax.all_to_all(asked, ("gx", "gy"), split_axis=0, concat_axis=0, tiled=True)

    values = embeddings.astype(F32)
    squared = jnp.sum(values * values, axis=1, keepdims=True)
    unit = (values * lax.rsqrt(squared + 1e-06)).astype(BF16)

    stages = [[0], [1, n_gx - 1], list(range(2, n_gx - 1))]

    def select(steps, unit):
        found = pl.pallas_call(
            functools.partial(select_kernel, dims, steps),
            out_shape=[shape((chunk + (2 if k else 1) * META, width), BF16) for k in steps],
            in_specs=[in_smem, in_vmem, in_vmem],
            out_specs=[in_vmem] * len(steps),
            cost_estimate=cost(2 * len(steps) * chunk * rows * width, rows * width),
            compiler_params=params(),
            name="select",
        )(place, asked, unit)
        return dict(zip(steps, found))

    def meet(*arrays):
        return lax.optimization_barrier(arrays)

    found = select(stages[1], unit)
    unit, *first = meet(unit, *found.values())
    found = {**dict(zip(found, first)), **select(stages[0] + stages[2], unit)}

    def across(array, step):
        return lax.ppermute(array, "gx", [(i, (i + step) % n_gx) for i in range(n_gx)])

    def swap(array, mask):
        return lax.ppermute(array, "gy", [(i, i ^ mask) for i in range(n_gy)])

    far = ["Y%d" % m for m in range(1, n_query)]
    edge = stages[1]
    rest = [k for k in stages[2]]
    names = ["%d" % k for k in stages[0] + stages[1]] + ["b"]
    piece = {}
    size = {}
    state = {}
    for n in names:
        for kind in ["T", "N", "X", "Z"] + far:
            size[kind + n] = chunk * (len(rest) if n == "b" else 1)
    for k in range(n_gx):
        size["z%d" % k] = chunk

    def pack(groups):
        flat = [n for g in groups.values() for n in g]
        for name, group in groups.items():
            size[name] = sum(size[n] for n in group)
        out = pl.pallas_call(
            functools.partial(pack_kernel, list(groups.values()), size, chunk),
            out_shape=[shape((size[n] + META, width), BF16) for n in groups],
            in_specs=[in_vmem] * len(flat),
            out_specs=[in_vmem] * len(groups),
            cost_estimate=cost(0, 4 * sum(size[n] for n in flat) * width),
            compiler_params=params(),
            name="pack",
        )(*[piece[n] for n in flat])
        piece.update(zip(groups, out))

    def near(n):
        piece["X" + n] = swap(piece["T" + n], 2)
        for m, kind in enumerate(far):
            piece[kind + n] = swap(piece["T" + n], KEYS * (m + 1))

    def join(names):
        arrays = [piece[n] for n in names] + [a for q in state for a in state[q]]
        arrays = list(meet(*arrays))
        for name in names:
            piece[name] = arrays.pop(0)
        for q in state:
            state[q] = (arrays.pop(0), arrays.pop(0))

    def kinds(kinds, names):
        return [k + n for n in names for k in kinds]

    for k in edge:
        piece["z%d" % k] = across(found[k], k)
    piece["T0"] = found[0]
    near("0")
    piece["N0"] = swap(piece["T0"], 1)
    for k in rest:
        piece["f%d" % k] = found[k]
    join(["z%d" % k for k in edge] + ["f%d" % k for k in rest] + kinds(["T", "X", "N"] + far, ["0"]))
    for k in rest:
        piece["z%d" % k] = across(piece["f%d" % k], k)
    pack({"T%d" % k: ["z%d" % k] for k in edge})
    for k in edge:
        near("%d" % k)

    def products(pairs, close=False):
        names = sorted({n for q, ks in pairs for n in [q] + ks})
        queries = [q for q, _ in pairs]
        started = [q for q in queries if q in state]
        inputs = [piece[n] for n in names] + [a for q in started for a in state[q]]
        outs = []
        for q in queries:
            if close:
                outs.append(shape((1, size[q]), F32))
            else:
                outs += [shape((size[q], 128), F32)] * 2
        flops = sum(2 * width * size[q] * size[k] for q, ks in pairs for k in ks)
        out = pl.pallas_call(
            functools.partial(product_kernel, pairs, size, chunk, started, close),
            out_shape=outs,
            in_specs=[in_vmem] * len(inputs),
            out_specs=[in_vmem] * len(outs),
            cost_estimate=cost(flops, 0),
            compiler_params=params(),
            name="products",
        )(*inputs)
        for i, q in enumerate(queries):
            state[q] = out[i] if close else (out[2 * i], out[2 * i + 1])

    one = ["0"] + ["%d" % k for k in edge]
    side = one[1:]
    tops = kinds(["T"], one) + kinds(far, ["0"])
    keys = ["N0", "X0"] + kinds(["T"], one)
    products([(q, keys) for q in tops])
    join(["z%d" % k for k in rest] + kinds(["T", "X"] + far, side))
    pack({"Tb": ["z%d" % k for k in rest], "P": kinds(["T"], side) + kinds(["X"], one)})
    near("b")
    piece["Nb"] = swap(piece["Tb"], 1)
    piece["Q"] = swap(piece["P"], 1)
    size["Q"] = size["P"]
    late = kinds(far, side)
    sides = kinds(["X"], side)
    products(
        [(q, sides + ["Tb"]) for q in tops]
        + [(q, keys + sides + ["Tb"]) for q in late + ["Tb"]]
    )
    before = tops + late + ["Tb"]
    products([(q, ["Q", "Nb"]) for q in before])
    join(["Tb", "Xb", "Nb", "Q"] + kinds(far, ["b"]))
    piece["Zb"] = swap(piece["Xb"], 1)
    products([(q, ["Xb"]) for q in before] + [(q, keys + sides + ["Tb", "Q", "Nb", "Xb"]) for q in kinds(far, ["b"])], close=True)

    order = []
    inputs = []
    for n in names:
        for m, kind in enumerate(["T"] + far):
            q = kind + n
            order.append((m, rest if n == "b" else [int(n)], size[q]))
            inputs += [piece[q], state[q]]
    send = pl.pallas_call(
        functools.partial(last_kernel, dims, order, size["Zb"]),
        out_shape=shape((n_gy, 1, n_query * 128), F32),
        in_specs=[in_vmem] * (1 + len(inputs)),
        out_specs=in_vmem,
        cost_estimate=cost(2 * width * size["Zb"] * n_query * rows, 0),
        compiler_params=params(),
        name="last",
    )(piece["Zb"], *inputs)

    back = lax.all_to_all(send, "gy", split_axis=0, concat_axis=0, tiled=True)
    out = pl.pallas_call(
        functools.partial(finish_kernel, dims),
        out_shape=shape((1, rows), F32),
        in_specs=[in_vmem, in_vmem],
        out_specs=in_vmem,
        compiler_params=params(),
        name="finish",
    )(home, back)
    return out.reshape(rows)


def solution(mesh):
    return jax.shard_map(
        per_device,
        mesh=mesh,
        in_specs=(P(("gx", "gy"), None), P(("gx", "gy")), P("gx", None)),
        out_specs=P(("gx", "gy")),
        check_vma=False,
    )
```

```python
import functools

import jax
import jax.numpy as jnp
from jax import lax
from jax.experimental import pallas as pl
from jax.experimental.pallas import tpu as pltpu
from jax.sharding import PartitionSpec as P

F32 = jnp.float32
BF16 = jnp.bfloat16
I32 = jnp.int32
SPARE = 8
KEYS = 4
VMEM = 24 * 1024 * 1024


def iota(shape, dim):
    return lax.broadcasted_iota(I32, shape, dim)


def dot_nt(a, b):
    return lax.dot_general(a, b, (((1,), (1,)), ((), ())), preferred_element_type=F32)


def dot_nn(a, b):
    return lax.dot_general(a, b, (((1,), (0,)), ((), ())), preferred_element_type=F32)


def one_hot(mask):
    return jnp.where(mask, 1.0, 0.0).astype(BF16)


def log2(value):
    assert value & (value - 1) == 0
    return value.bit_length() - 1


def params(limit=VMEM):
    return pltpu.CompilerParams(vmem_limit_bytes=limit)


def cost(flops, size):
    return pl.CostEstimate(flops=flops, bytes_accessed=size, transcendentals=0)


def request_kernel(dims, sizes_hbm, members_hbm, asked_ref, home_ref, sizes_ref, members_ref, sems):
    n_gx, n_gy, rows, quota = dims
    copies = [
        pltpu.make_async_copy(members_hbm, members_ref, sems.at[0]),
        pltpu.make_async_copy(sizes_hbm, sizes_ref, sems.at[1]),
    ]
    for copy in copies:
        copy.start()
    for copy in copies:
        copy.wait()
    owners = n_gx * n_gy
    member = members_ref[...]
    owner = lax.shift_right_logical(member, log2(rows))
    row = member & (rows - 1)
    slot = lax.axis_index("gy") * rows + iota((1, rows), 1)
    cluster = jnp.zeros((1, rows), I32)
    end = jnp.int32(0)
    for c in range(sizes_ref.shape[1]):
        end = end + sizes_ref[0, c]
        cluster = cluster + (slot >= end).astype(I32)
    mask = iota((owners, rows), 0) == owner
    hot = one_hot(mask)
    before = one_hot(iota((128, 128), 0) < iota((128, 128), 1))
    count = jnp.zeros((owners, 1), F32)
    ranks = []
    for b in range(rows // 128):
        part = hot[:, b * 128:(b + 1) * 128]
        rank = dot_nn(part, before) + count
        part32 = part.astype(F32)
        ranks.append(jnp.sum(part32 * rank, axis=0, keepdims=True))
        count = count + jnp.sum(part32, axis=1, keepdims=True)
    rank = jnp.concatenate(ranks, axis=1).astype(I32)
    place = one_hot(iota((quota, rows), 0) == rank)
    low = (row & 255).astype(F32)
    high = lax.shift_right_logical(row, 8).astype(F32)
    zero = jnp.zeros((owners, rows), F32)

    def pick(value):
        return dot_nt(jnp.where(mask, value, zero).astype(BF16), place)

    asked = pick(low) + 256.0 * pick(high) + float(rows) * pick(cluster.astype(F32))
    asked = asked.astype(I32)
    for o in range(owners):
        asked_ref[o] = asked[o:o + 1, :]
    plane = lax.shift_right_logical(owner, log2(n_gy))
    step = (lax.axis_index("gx") - plane) & (n_gx - 1)
    home_ref[0:1, :] = owner & (n_gy - 1)
    home_ref[1:2, :] = step * quota + rank


def select_kernel(dims, steps, asked_ref, unit_ref, *out_refs):
    n_gx, n_gy, rows, quota = dims
    chunk = n_gy * quota
    pick = one_hot((iota((chunk, quota), 0) & (quota - 1)) == iota((chunk, quota), 1))
    block = lax.shift_right_logical(iota((chunk, n_gy), 0), log2(quota))
    own_col = block == iota((chunk, n_gy), 1)
    block_row = lax.shift_right_logical(iota((n_gy, chunk), 1), log2(quota))
    own_row = block_row == iota((n_gy, chunk), 0)
    for step, ref in zip(steps, out_refs):
        plane = (lax.axis_index("gx") + step) & (n_gx - 1)
        wanted = jnp.concatenate([asked_ref[plane * n_gy + d] for d in range(n_gy)], axis=0)
        row = wanted & (rows - 1)
        cluster = lax.shift_right_logical(wanted, log2(rows)).astype(F32).astype(BF16)
        low = (row & 255).astype(F32).astype(BF16)
        high = lax.shift_right_logical(row, 8).astype(F32).astype(BF16)
        index = dot_nt(pick, low) + 256.0 * dot_nt(pick, high)
        index = jnp.sum(jnp.where(own_col, index, 0.0), axis=1, keepdims=True).astype(I32)
        flat = jnp.sum(jnp.where(own_row, dot_nt(cluster, pick), 0.0), axis=0, keepdims=True)
        hot = one_hot(iota((chunk, rows), 1) == index)
        ref[0:chunk, :] = dot_nn(hot, unit_ref[...]).astype(BF16)
        width = unit_ref.shape[1]
        line = jnp.concatenate([flat, jnp.zeros((1, width - chunk), F32)], axis=1)
        ref[chunk:chunk + SPARE, :] = jnp.where(iota((SPARE, width), 0) == 0, line, 0.0).astype(BF16)


def column(line):
    parts = []
    for b in range(line.shape[1] // 128):
        wide = jnp.broadcast_to(line[:, b * 128:(b + 1) * 128], (128, 128))
        parts.append(wide.T)
    return jnp.concatenate(parts, axis=0)


def wide(col, lanes):
    return jnp.concatenate([col] * (lanes // 128), axis=1)


def more(chunks):
    return -(-chunks // SPARE) * SPARE


def cluster_line(ref, size, chunk):
    block = ref[size:size + more(size // chunk), 0:chunk].astype(F32)
    return jnp.concatenate([block[r:r + 1, :] for r in range(size // chunk)], axis=1)


def pack_kernel(groups, sizes, chunk, *refs):
    refs = list(refs)
    outs = refs[sum(len(g) for g in groups):]
    for group, out_ref in zip(groups, outs):
        at = 0
        total = sum(sizes[n] for n in group)
        width = out_ref.shape[1]
        extra = more(total // chunk)
        meta = jnp.zeros((extra, width), F32)
        for name in group:
            ref, size = refs.pop(0), sizes[name]
            out_ref[at:at + size, :] = ref[0:size, :]
            lines = ref[size:size + more(size // chunk), :].astype(F32)
            for r in range(size // chunk):
                meta = jnp.where(iota((extra, width), 0) == at // chunk + r, lines[r:r + 1, :], meta)
            at += size
        out_ref[total:total + extra, :] = meta.astype(BF16)


def product_kernel(pairs, sizes, chunk, started, close, *refs):
    names = sorted({n for q, ks in pairs for n in [q] + ks})
    queries = [q for q, _ in pairs]
    refs = list(refs)
    rows = {n: refs.pop(0) for n in names}
    state = {q: (refs.pop(0), refs.pop(0)) for q in queries if q in started}
    for q, keys in pairs:
        n_q = sizes[q]
        if close:
            out_ref = refs.pop(0)
        else:
            col_ref, out_ref = refs.pop(0), refs.pop(0)
        if q in started:
            col = state[q][0][...]
            best = state[q][1][...]
        else:
            col = column(cluster_line(rows[q], n_q, chunk))
            best = jnp.full((n_q, 128), -1.0, F32)
        if not close:
            col_ref[...] = col
        for k in keys:
            n_k = sizes[k]
            sims = dot_nt(rows[q][0:n_q, :], rows[k][0:n_k, :])
            keep = wide(col, n_k) == cluster_line(rows[k], n_k, chunk)
            if k == q:
                keep = keep & (iota((n_q, n_k), 0) != iota((n_q, n_k), 1))
            sims = jnp.where(keep, sims, -1.0)
            for v in range(n_k // 128):
                best = jnp.maximum(best, sims[:, v * 128:(v + 1) * 128])
        if close:
            parts = [jnp.max(best[b * 128:(b + 1) * 128, :].T, axis=0, keepdims=True) for b in range(n_q // 128)]
            out_ref[...] = jnp.concatenate(parts, axis=1)
        else:
            out_ref[...] = best


def last_kernel(dims, queries, size, *refs):
    n_gx, n_gy, rows, quota = dims
    chunk = n_gy * quota
    refs = list(refs)
    key_ref = refs.pop(0)
    send_ref = refs.pop()
    keys = key_ref[0:size, :]
    col = column(cluster_line(key_ref, size, chunk))
    spread = {}
    for (m, steps, n_q), row_ref, best_ref in zip(queries, refs[0::2], refs[1::2]):
        sims = dot_nt(keys, row_ref[0:n_q, :])
        keep = wide(col, n_q) == cluster_line(row_ref, n_q, chunk)
        line = jnp.max(jnp.where(keep, sims, -1.0), axis=0, keepdims=True)
        line = jnp.maximum(line, best_ref[...])
        for c, step in enumerate(steps):
            flat = line[:, c * chunk:(c + 1) * chunk]
            block = lax.shift_right_logical(iota((n_gy, chunk), 1), log2(quota))
            held = jnp.where(block == iota((n_gy, chunk), 0), flat, 0.0)
            fold = held[:, 0:128]
            for v in range(1, chunk // 128):
                fold = fold + held[:, v * 128:(v + 1) * 128]
            shift = 64
            while shift >= quota:
                fold = fold + pltpu.roll(fold, shift, 1)
                shift //= 2
            here = lax.shift_right_logical(iota((n_gy, 128), 1), log2(quota)) == step
            fold = jnp.where(here, fold, 0.0)
            spread[m] = spread[m] + fold if m in spread else fold
    spread = jnp.concatenate([spread[m] for m in sorted(spread)], axis=1)
    for d in range(n_gy):
        send_ref[d] = spread[d:d + 1, :]


def finish_kernel(dims, home_ref, back_ref, out_ref):
    n_gx, n_gy, rows, quota = dims
    n_query = n_gy // KEYS
    lines = []
    for q in range(n_gy):
        best = None
        for m in range(n_query):
            part = back_ref[q ^ (KEYS * m)][:, m * 128:(m + 1) * 128]
            best = part if best is None else jnp.maximum(best, part)
        lines.append(best)
    found = jnp.concatenate(lines, axis=0)
    high = found.astype(BF16)
    rest = found - high.astype(F32)
    mid = rest.astype(BF16)
    low = (rest - mid.astype(F32)).astype(BF16)
    here = one_hot(iota((128, rows), 0) == home_ref[1:2, :])
    value = (dot_nn(high, here) + dot_nn(mid, here)) + dot_nn(low, here)
    own = iota((n_gy, rows), 0) == home_ref[0:1, :]
    out_ref[...] = jnp.sum(jnp.where(own, value, 0.0), axis=0, keepdims=True)


def shape(dims, dtype):
    return jax.ShapeDtypeStruct(dims, dtype)


def per_device(embeddings, members, sizes):
    rows = members.shape[0]
    width = embeddings.shape[1]
    n_gx = lax.axis_size("gx")
    n_gy = lax.axis_size("gy")
    owners = n_gx * n_gy
    quota = rows // owners
    chunk = n_gy * quota
    n_query = n_gy // KEYS
    dims = (n_gx, n_gy, rows, quota)
    in_vmem = pl.BlockSpec(memory_space=pltpu.VMEM)

    in_hbm = pl.BlockSpec(memory_space=pltpu.HBM)
    asked, home = pl.pallas_call(
        functools.partial(request_kernel, dims),
        out_shape=(shape((owners, 1, quota), I32), shape((2, rows), I32)),
        in_specs=[in_hbm, in_hbm],
        out_specs=(in_vmem, in_vmem),
        scratch_shapes=[
            pltpu.SMEM(sizes.shape, I32),
            pltpu.VMEM((1, rows), I32),
            pltpu.SemaphoreType.DMA((2,)),
        ],
        compiler_params=params(56 * 1024 * 1024),
        name="request",
    )(sizes, members.reshape(1, rows))
    asked = lax.all_to_all(asked, ("gx", "gy"), split_axis=0, concat_axis=0, tiled=True)

    values = embeddings.astype(F32)
    squared = jnp.sum(values * values, axis=1, keepdims=True)
    unit = (values * lax.rsqrt(squared + 1e-06)).astype(BF16)

    stages = [[0], [1, n_gx - 1], list(range(2, n_gx - 1))]

    def meet(*arrays):
        return lax.optimization_barrier(arrays)

    found = {}
    for steps in [stages[1][:1], stages[0], stages[1][1:] + stages[2]]:
        out = pl.pallas_call(
            functools.partial(select_kernel, dims, steps),
            out_shape=[shape((chunk + (2 if k else 1) * SPARE, width), BF16) for k in steps],
            in_specs=[in_vmem, in_vmem],
            out_specs=[in_vmem] * len(steps),
            cost_estimate=cost(2 * len(steps) * chunk * rows * width, rows * width),
            compiler_params=params(),
            name="select",
        )(asked, unit)
        unit, *out = meet(unit, *out)
        found.update(zip(steps, out))

    def across(array, step):
        return lax.ppermute(array, "gx", [(i, (i + step) % n_gx) for i in range(n_gx)])

    def swap(array, mask):
        return lax.ppermute(array, "gy", [(i, i ^ mask) for i in range(n_gy)])

    far = ["Y%d" % m for m in range(1, n_query)]
    edge = stages[1]
    rest = [k for k in stages[2]]
    names = ["%d" % k for k in stages[0] + stages[1]] + ["b"]
    piece = {}
    size = {}
    state = {}
    for n in names:
        for kind in ["T", "N", "X", "Z"] + far:
            size[kind + n] = chunk * (len(rest) if n == "b" else 1)
    for k in range(n_gx):
        size["z%d" % k] = chunk

    def pack(groups):
        flat = [n for g in groups.values() for n in g]
        for name, group in groups.items():
            size[name] = sum(size[n] for n in group)
        out = pl.pallas_call(
            functools.partial(pack_kernel, list(groups.values()), size, chunk),
            out_shape=[shape((size[n] + more(size[n] // chunk), width), BF16) for n in groups],
            in_specs=[in_vmem] * len(flat),
            out_specs=[in_vmem] * len(groups),
            cost_estimate=cost(0, 4 * sum(size[n] for n in flat) * width),
            compiler_params=params(),
            name="pack",
        )(*[piece[n] for n in flat])
        piece.update(zip(groups, out))

    def near(n):
        piece["X" + n] = swap(piece["T" + n], 2)
        for m, kind in enumerate(far):
            piece[kind + n] = swap(piece["T" + n], KEYS * (m + 1))

    def join(names):
        arrays = [piece[n] for n in names] + [a for q in state for a in state[q]]
        arrays = list(meet(*arrays))
        for name in names:
            piece[name] = arrays.pop(0)
        for q in state:
            state[q] = (arrays.pop(0), arrays.pop(0))

    def kinds(kinds, names):
        return [k + n for n in names for k in kinds]

    def products(pairs, close=False):
        names = sorted({n for q, ks in pairs for n in [q] + ks})
        queries = [q for q, _ in pairs]
        started = [q for q in queries if q in state]
        inputs = [piece[n] for n in names] + [a for q in started for a in state[q]]
        outs = []
        for q in queries:
            if close:
                outs.append(shape((1, size[q]), F32))
            else:
                outs += [shape((size[q], 128), F32)] * 2
        flops = sum(2 * width * size[q] * size[k] for q, ks in pairs for k in ks)
        out = pl.pallas_call(
            functools.partial(product_kernel, pairs, size, chunk, started, close),
            out_shape=outs,
            in_specs=[in_vmem] * len(inputs),
            out_specs=[in_vmem] * len(outs),
            cost_estimate=cost(flops, 0),
            compiler_params=params(),
            name="products",
        )(*inputs)
        for i, q in enumerate(queries):
            state[q] = out[i] if close else (out[2 * i], out[2 * i + 1])

    def swap_core(name, group):
        pack({"P": group})
        piece[name] = swap(piece["P"], 1)
        size[name] = size["P"]

    first, second = edge
    a, b = "%d" % first, "%d" % second
    for k in edge:
        piece["z%d" % k] = across(found[k], k)
    piece["T0"] = found[0]
    near("0")
    piece["N0"] = swap(piece["T0"], 1)
    for k in rest:
        piece["f%d" % k] = found[k]
    join(["z" + a] + ["f%d" % k for k in rest] + kinds(["T", "X", "N"] + far, ["0"]))

    for k in rest:
        piece["z%d" % k] = across(piece["f%d" % k], k)
    pack({"T" + a: ["z" + a]})
    near(a)
    piece["Z0"] = swap(piece["X0"], 1)
    keys = ["T0", "N0", "X0", "T" + a]
    before = ["T0"] + kinds(far, ["0"]) + ["T" + a]
    products([(q, keys) for q in before])
    join(["z" + b, "Z0"] + kinds(["T", "X"] + far, [a]))

    pack({"T" + b: ["z" + b]})
    near(b)
    new = ["X" + a, "T" + b, "Z0"]
    keys = keys + new
    late = kinds(far, [a]) + ["T" + b]
    products([(q, new) for q in before] + [(q, keys) for q in late])
    before = before + late
    join(["z%d" % k for k in rest] + kinds(["T", "X"] + far, [b]))

    pack({"Tb": ["z%d" % k for k in rest]})
    near("b")
    swap_core("Q", kinds(["T", "X"], [a, b]) + ["Tb"])
    new = ["X" + b, "Tb"]
    keys = keys + new
    late = kinds(far, [b]) + ["Tb"]
    products([(q, new) for q in before] + [(q, keys) for q in late])
    before = before + late
    products([(q, ["Q"]) for q in before])
    keys = keys + ["Q", "Xb"]
    join(["Tb", "Xb", "Q"] + kinds(far, ["b"]))

    piece["Zb"] = swap(piece["Xb"], 1)
    products([(q, ["Xb"]) for q in before] + [(q, keys) for q in kinds(far, ["b"])], close=True)

    order = []
    inputs = []
    for n in names:
        for m, kind in enumerate(["T"] + far):
            q = kind + n
            order.append((m, rest if n == "b" else [int(n)], size[q]))
            inputs += [piece[q], state[q]]
    send = pl.pallas_call(
        functools.partial(last_kernel, dims, order, size["Zb"]),
        out_shape=shape((n_gy, 1, n_query * 128), F32),
        in_specs=[in_vmem] * (1 + len(inputs)),
        out_specs=in_vmem,
        cost_estimate=cost(2 * width * size["Zb"] * n_query * rows, 0),
        compiler_params=params(),
        name="last",
    )(piece["Zb"], *inputs)

    back = lax.all_to_all(send, "gy", split_axis=0, concat_axis=0, tiled=True)
    out = pl.pallas_call(
        functools.partial(finish_kernel, dims),
        out_shape=shape((1, rows), F32),
        in_specs=[in_vmem, in_vmem],
        out_specs=in_vmem,
        compiler_params=params(),
        name="finish",
    )(home, back)
    return out.reshape(rows)


def solution(mesh):
    return jax.shard_map(
        per_device,
        mesh=mesh,
        in_specs=(P(("gx", "gy"), None), P(("gx", "gy")), P("gx", None)),
        out_specs=P(("gx", "gy")),
        check_vma=False,
    )
```

```python
import functools

import jax
import jax.numpy as jnp
from jax import lax
from jax.experimental import pallas as pl
from jax.experimental.pallas import tpu as pltpu
from jax.sharding import PartitionSpec as P

F32 = jnp.float32
BF16 = jnp.bfloat16
I32 = jnp.int32
SPARE = 8
KEYS = 4
VMEM = 24 * 1024 * 1024


def iota(shape, dim):
    return lax.broadcasted_iota(I32, shape, dim)


def dot_nt(a, b):
    return lax.dot_general(a, b, (((1,), (1,)), ((), ())), preferred_element_type=F32)


def dot_nn(a, b):
    return lax.dot_general(a, b, (((1,), (0,)), ((), ())), preferred_element_type=F32)


def one_hot(mask):
    return jnp.where(mask, 1.0, 0.0).astype(BF16)


def log2(value):
    assert value & (value - 1) == 0
    return value.bit_length() - 1


def params(limit=VMEM):
    return pltpu.CompilerParams(vmem_limit_bytes=limit)


def cost(flops, size):
    return pl.CostEstimate(flops=flops, bytes_accessed=size, transcendentals=0)


def request_kernel(dims, sizes_hbm, members_hbm, asked_ref, home_ref, sizes_ref, members_ref, sems):
    n_gx, n_gy, rows, quota = dims
    copies = [
        pltpu.make_async_copy(members_hbm, members_ref, sems.at[0]),
        pltpu.make_async_copy(sizes_hbm, sizes_ref, sems.at[1]),
    ]
    for copy in copies:
        copy.start()
    for copy in copies:
        copy.wait()
    owners = n_gx * n_gy
    member = members_ref[...]
    owner = lax.shift_right_logical(member, log2(rows))
    row = member & (rows - 1)
    slot = lax.axis_index("gy") * rows + iota((1, rows), 1)
    cluster = jnp.zeros((1, rows), I32)
    end = jnp.int32(0)
    for c in range(sizes_ref.shape[1]):
        end = end + sizes_ref[0, c]
        cluster = cluster + (slot >= end).astype(I32)
    mask = iota((owners, rows), 0) == owner
    hot = one_hot(mask)
    before = one_hot(iota((128, 128), 0) < iota((128, 128), 1))
    count = jnp.zeros((owners, 1), F32)
    ranks = []
    for b in range(rows // 128):
        part = hot[:, b * 128:(b + 1) * 128]
        rank = dot_nn(part, before) + count
        part32 = part.astype(F32)
        ranks.append(jnp.sum(part32 * rank, axis=0, keepdims=True))
        count = count + jnp.sum(part32, axis=1, keepdims=True)
    rank = jnp.concatenate(ranks, axis=1).astype(I32)
    place = one_hot(iota((quota, rows), 0) == rank)
    low = (row & 255).astype(F32)
    high = lax.shift_right_logical(row, 8).astype(F32)
    zero = jnp.zeros((owners, rows), F32)

    def pick(value):
        return dot_nt(jnp.where(mask, value, zero).astype(BF16), place)

    asked = pick(low) + 256.0 * pick(high) + float(rows) * pick(cluster.astype(F32))
    asked = asked.astype(I32)
    for o in range(owners):
        asked_ref[o] = asked[o:o + 1, :]
    plane = lax.shift_right_logical(owner, log2(n_gy))
    step = (lax.axis_index("gx") - plane) & (n_gx - 1)
    home_ref[0:1, :] = owner & (n_gy - 1)
    home_ref[1:2, :] = step * quota + rank


def select_kernel(dims, steps, asked_ref, unit_ref, *out_refs):
    n_gx, n_gy, rows, quota = dims
    chunk = n_gy * quota
    pick = one_hot((iota((chunk, quota), 0) & (quota - 1)) == iota((chunk, quota), 1))
    block = lax.shift_right_logical(iota((chunk, n_gy), 0), log2(quota))
    own_col = block == iota((chunk, n_gy), 1)
    block_row = lax.shift_right_logical(iota((n_gy, chunk), 1), log2(quota))
    own_row = block_row == iota((n_gy, chunk), 0)
    for step, ref in zip(steps, out_refs):
        plane = (lax.axis_index("gx") + step) & (n_gx - 1)
        wanted = jnp.concatenate([asked_ref[plane * n_gy + d] for d in range(n_gy)], axis=0)
        row = wanted & (rows - 1)
        cluster = lax.shift_right_logical(wanted, log2(rows)).astype(F32).astype(BF16)
        low = (row & 255).astype(F32).astype(BF16)
        high = lax.shift_right_logical(row, 8).astype(F32).astype(BF16)
        index = dot_nt(pick, low) + 256.0 * dot_nt(pick, high)
        index = jnp.sum(jnp.where(own_col, index, 0.0), axis=1, keepdims=True).astype(I32)
        flat = jnp.sum(jnp.where(own_row, dot_nt(cluster, pick), 0.0), axis=0, keepdims=True)
        hot = one_hot(iota((chunk, rows), 1) == index)
        ref[0:chunk, :] = dot_nn(hot, unit_ref[...]).astype(BF16)
        width = unit_ref.shape[1]
        line = jnp.concatenate([flat, jnp.zeros((1, width - chunk), F32)], axis=1)
        ref[chunk:chunk + SPARE, :] = jnp.where(iota((SPARE, width), 0) == 0, line, 0.0).astype(BF16)


def column(line):
    parts = []
    for b in range(line.shape[1] // 128):
        wide = jnp.broadcast_to(line[:, b * 128:(b + 1) * 128], (128, 128))
        parts.append(wide.T)
    return jnp.concatenate(parts, axis=0)


def wide(col, lanes):
    return jnp.concatenate([col] * (lanes // 128), axis=1)


def more(chunks):
    return -(-chunks // SPARE) * SPARE


def cluster_line(ref, size, chunk):
    block = ref[size:size + more(size // chunk), 0:chunk].astype(F32)
    return jnp.concatenate([block[r:r + 1, :] for r in range(size // chunk)], axis=1)


def pack_kernel(groups, sizes, chunk, *refs):
    refs = list(refs)
    outs = refs[sum(len(g) for g in groups):]
    for group, out_ref in zip(groups, outs):
        at = 0
        total = sum(sizes[n] for n in group)
        width = out_ref.shape[1]
        extra = more(total // chunk)
        meta = jnp.zeros((extra, width), F32)
        for name in group:
            ref, size = refs.pop(0), sizes[name]
            out_ref[at:at + size, :] = ref[0:size, :]
            lines = ref[size:size + more(size // chunk), :].astype(F32)
            for r in range(size // chunk):
                meta = jnp.where(iota((extra, width), 0) == at // chunk + r, lines[r:r + 1, :], meta)
            at += size
        out_ref[total:total + extra, :] = meta.astype(BF16)


def product_kernel(pairs, sizes, chunk, started, turned, close, *refs):
    names = sorted({n for q, ks in pairs for n in [q] + ks})
    queries = [q for q, _ in pairs]
    refs = list(refs)
    rows = {n: refs.pop(0) for n in names}
    state = {q: (refs.pop(0), refs.pop(0)) for q in queries if q in started}
    turns = {}
    for q, keys in pairs:
        n_q = sizes[q]
        if q in started:
            col = state[q][0][...]
            best = state[q][1][...]
        else:
            col = column(cluster_line(rows[q], n_q, chunk))
            best = jnp.full((n_q, 128), -1.0, F32)
            if not close:
                refs.pop(0)[...] = col
        out_ref = refs.pop(0)
        for k in keys:
            n_k = sizes[k]
            sims = dot_nt(rows[q][0:n_q, :], rows[k][0:n_k, :])
            keep = wide(col, n_k) == cluster_line(rows[k], n_k, chunk)
            if k == q:
                keep = keep & (iota((n_q, n_k), 0) != iota((n_q, n_k), 1))
            sims = jnp.where(keep, sims, -1.0)
            for v in range(n_k // 128):
                best = jnp.maximum(best, sims[:, v * 128:(v + 1) * 128])
            if (q, k) in turned:
                line = jnp.max(sims, axis=0, keepdims=True)
                turns[k] = jnp.maximum(turns[k], line) if k in turns else line
        if close:
            out_ref[...] = lined(best)
        else:
            out_ref[...] = best
    for k in sorted(turns):
        refs.pop(0)[...] = turns[k]


def lined(best):
    rows = best.shape[0]
    parts = [jnp.max(best[b * 128:(b + 1) * 128, :].T, axis=0, keepdims=True) for b in range(rows // 128)]
    return jnp.concatenate(parts, axis=1)


def last_kernel(dims, queries, stage, size, key_ref, turn_t_ref, turn_n_ref, turn_x_ref, *refs):
    n_gx, n_gy, rows, quota = dims
    chunk = n_gy * quota
    refs = list(refs)
    send_ref = refs.pop()
    keys = key_ref[0:size, :]
    col = column(cluster_line(key_ref, size, chunk))
    blocks = {}

    def spread(block, line, groups):
        for c, group in enumerate(groups):
            flat = line[:, c * chunk:(c + 1) * chunk]
            target = lax.shift_right_logical(iota((n_gy, chunk), 1), log2(quota))
            held = jnp.where(target == iota((n_gy, chunk), 0), flat, 0.0)
            fold = held[:, 0:128]
            for v in range(1, chunk // 128):
                fold = fold + held[:, v * 128:(v + 1) * 128]
            shift = 64
            while shift >= quota:
                fold = fold + pltpu.roll(fold, shift, 1)
                shift //= 2
            here = lax.shift_right_logical(iota((n_gy, 128), 1), log2(quota)) == group
            fold = jnp.where(here, fold, 0.0)
            blocks[block] = blocks[block] + fold if block in blocks else fold

    turn = jnp.full((size, 128), -1.0, F32)
    for (m, steps, n_q), row_ref, best_ref in zip(queries, refs[0::2], refs[1::2]):
        sims = dot_nt(keys, row_ref[0:n_q, :])
        keep = wide(col, n_q) == cluster_line(row_ref, n_q, chunk)
        sims = jnp.where(keep, sims, -1.0)
        line = jnp.maximum(jnp.max(sims, axis=0, keepdims=True), best_ref[...])
        if m and steps != stage:
            for v in range(n_q // 128):
                turn = jnp.maximum(turn, sims[:, v * 128:(v + 1) * 128])
        if not m and steps == stage:
            line = jnp.maximum(line, turn_t_ref[...])
        spread(m, line, steps)
    last = len(blocks)
    for t, line in enumerate([turn_n_ref[...], turn_x_ref[...], lined(turn)]):
        spread(last, line, range(t * len(stage), (t + 1) * len(stage)))
    whole = jnp.concatenate([blocks[b] for b in range(last + 1)], axis=1)
    for d in range(n_gy):
        send_ref[d] = whole[d:d + 1, :]


def finish_kernel(dims, stage, home_ref, back_ref, out_ref):
    n_gx, n_gy, rows, quota = dims
    n_query = n_gy // KEYS
    low, high = stage[0] * quota, (stage[-1] + 1) * quota
    lane = iota((n_gy, 128), 1)
    found = None
    for m in range(n_query):
        part = jnp.concatenate([back_ref[q ^ (KEYS * m)][:, m * 128:(m + 1) * 128] for q in range(n_gy)], axis=0)
        found = part if found is None else jnp.maximum(found, part)
    for t in range(1, KEYS):
        part = jnp.concatenate([back_ref[q ^ t][:, n_query * 128:] for q in range(n_gy)], axis=0)
        part = pltpu.roll(part, (low - (t - 1) * (high - low)) % 128, 1)
        found = jnp.where((lane >= low) & (lane < high), jnp.maximum(found, part), found)
    high = found.astype(BF16)
    rest = found - high.astype(F32)
    mid = rest.astype(BF16)
    low = (rest - mid.astype(F32)).astype(BF16)
    here = one_hot(iota((128, rows), 0) == home_ref[1:2, :])
    value = (dot_nn(high, here) + dot_nn(mid, here)) + dot_nn(low, here)
    own = iota((n_gy, rows), 0) == home_ref[0:1, :]
    out_ref[...] = jnp.sum(jnp.where(own, value, 0.0), axis=0, keepdims=True)


def shape(dims, dtype):
    return jax.ShapeDtypeStruct(dims, dtype)


def per_device(embeddings, members, sizes):
    rows = members.shape[0]
    width = embeddings.shape[1]
    n_gx = lax.axis_size("gx")
    n_gy = lax.axis_size("gy")
    owners = n_gx * n_gy
    quota = rows // owners
    chunk = n_gy * quota
    n_query = n_gy // KEYS
    dims = (n_gx, n_gy, rows, quota)
    in_vmem = pl.BlockSpec(memory_space=pltpu.VMEM)

    in_hbm = pl.BlockSpec(memory_space=pltpu.HBM)
    asked, home = pl.pallas_call(
        functools.partial(request_kernel, dims),
        out_shape=(shape((owners, 1, quota), I32), shape((2, rows), I32)),
        in_specs=[in_hbm, in_hbm],
        out_specs=(in_vmem, in_vmem),
        scratch_shapes=[
            pltpu.SMEM(sizes.shape, I32),
            pltpu.VMEM((1, rows), I32),
            pltpu.SemaphoreType.DMA((2,)),
        ],
        compiler_params=params(56 * 1024 * 1024),
        name="request",
    )(sizes, members.reshape(1, rows))
    asked = lax.all_to_all(asked, ("gx", "gy"), split_axis=0, concat_axis=0, tiled=True)

    values = embeddings.astype(F32)
    squared = jnp.sum(values * values, axis=1, keepdims=True)
    unit = (values * lax.rsqrt(squared + 1e-06)).astype(BF16)

    stages = [[0], [1, n_gx - 1], list(range(2, n_gx - 1))]

    def meet(*arrays):
        return lax.optimization_barrier(arrays)

    found = {}
    for steps in [stages[1][:1], stages[0], stages[1][1:] + stages[2]]:
        out = pl.pallas_call(
            functools.partial(select_kernel, dims, steps),
            out_shape=[shape((chunk + (2 if k else 1) * SPARE, width), BF16) for k in steps],
            in_specs=[in_vmem, in_vmem],
            out_specs=[in_vmem] * len(steps),
            cost_estimate=cost(2 * len(steps) * chunk * rows * width, rows * width),
            compiler_params=params(),
            name="select",
        )(asked, unit)
        unit, *out = meet(unit, *out)
        found.update(zip(steps, out))

    def across(array, step):
        return lax.ppermute(array, "gx", [(i, (i + step) % n_gx) for i in range(n_gx)])

    def swap(array, mask):
        return lax.ppermute(array, "gy", [(i, i ^ mask) for i in range(n_gy)])

    far = ["Y%d" % m for m in range(1, n_query)]
    edge = stages[1]
    rest = [k for k in stages[2]]
    names = ["%d" % k for k in stages[0] + stages[1]] + ["b"]
    piece = {}
    size = {}
    state = {}
    for n in names:
        for kind in ["T", "N", "X", "Z"] + far:
            size[kind + n] = chunk * (len(rest) if n == "b" else 1)
    for k in range(n_gx):
        size["z%d" % k] = chunk

    def pack(groups):
        flat = [n for g in groups.values() for n in g]
        for name, group in groups.items():
            size[name] = sum(size[n] for n in group)
        out = pl.pallas_call(
            functools.partial(pack_kernel, list(groups.values()), size, chunk),
            out_shape=[shape((size[n] + more(size[n] // chunk), width), BF16) for n in groups],
            in_specs=[in_vmem] * len(flat),
            out_specs=[in_vmem] * len(groups),
            cost_estimate=cost(0, 4 * sum(size[n] for n in flat) * width),
            compiler_params=params(),
            name="pack",
        )(*[piece[n] for n in flat])
        piece.update(zip(groups, out))

    def near(n):
        piece["X" + n] = swap(piece["T" + n], 2)
        for m, kind in enumerate(far):
            piece[kind + n] = swap(piece["T" + n], KEYS * (m + 1))

    def join(names):
        arrays = [piece[n] for n in names] + [a for q in state for a in state[q]]
        arrays = list(meet(*arrays))
        for name in names:
            piece[name] = arrays.pop(0)
        for q in state:
            state[q] = (arrays.pop(0), arrays.pop(0))

    def kinds(kinds, names):
        return [k + n for n in names for k in kinds]

    def products(pairs, turned=(), close=False):
        names = sorted({n for q, ks in pairs for n in [q] + ks})
        queries = [q for q, _ in pairs]
        started = [q for q in queries if q in state]
        inputs = [piece[n] for n in names] + [a for q in started for a in state[q]]
        outs = []
        for q in queries:
            if close:
                outs.append(shape((1, size[q]), F32))
            else:
                outs += [shape((size[q], 128), F32)] * (1 if q in started else 2)
        turned = {(q, k) for q, ks in pairs for k in ks if k in turned and q[0] == "Y" and q[1:] != "b"}
        outs += [shape((1, size[k]), F32) for k in sorted({k for _, k in turned})]
        flops = sum(2 * width * size[q] * size[k] for q, ks in pairs for k in ks)
        out = pl.pallas_call(
            functools.partial(product_kernel, pairs, size, chunk, started, turned, close),
            out_shape=outs,
            in_specs=[in_vmem] * len(inputs),
            out_specs=[in_vmem] * len(outs),
            cost_estimate=cost(flops, 0),
            compiler_params=params(),
            name="products",
        )(*inputs)
        out = list(out)
        for q in queries:
            if close:
                state[q] = out.pop(0)
            else:
                col = state[q][0] if q in started else out.pop(0)
                state[q] = (col, out.pop(0))
        return out

    def swap_core(name, group):
        pack({"P": group})
        piece[name] = swap(piece["P"], 1)
        size[name] = size["P"]

    first, second = edge
    a, b = "%d" % first, "%d" % second
    for k in edge:
        piece["z%d" % k] = across(found[k], k)
    piece["T0"] = found[0]
    near("0")
    piece["N0"] = swap(piece["T0"], 1)
    for k in rest:
        piece["f%d" % k] = found[k]
    join(["z" + a] + ["f%d" % k for k in rest] + kinds(["T", "X", "N"] + far, ["0"]))

    for k in rest:
        piece["z%d" % k] = across(piece["f%d" % k], k)
    pack({"T" + a: ["z" + a]})
    near(a)
    piece["Z0"] = swap(piece["X0"], 1)
    keys = ["T0", "N0", "X0", "T" + a]
    before = ["T0"] + kinds(far, ["0"]) + ["T" + a]
    products([(q, keys) for q in before])
    join(["z" + b, "Z0"] + kinds(["T", "X"] + far, [a]))

    pack({"T" + b: ["z" + b]})
    near(b)
    new = ["X" + a, "T" + b, "Z0"]
    keys = keys + new
    late = kinds(far, [a]) + ["T" + b]
    products([(q, new) for q in before] + [(q, keys) for q in late])
    before = before + late
    join(["z%d" % k for k in rest] + kinds(["T", "X"] + far, [b]))

    pack({"Tb": ["z%d" % k for k in rest]})
    near("b")
    piece["Nb"] = swap(piece["Tb"], 1)
    swap_core("Q", kinds(["T", "X"], [a, b]))
    new = ["X" + b, "Tb"]
    keys = keys + new
    late = kinds(far, [b]) + ["Tb"]
    turn_t = products([(q, new) for q in before] + [(q, keys) for q in late], ["Tb"])
    before = before + late
    turn_n = products([(q, ["Q", "Nb"]) for q in before], ["Nb"])
    join(["Tb", "Nb", "Xb"] + kinds(far, ["b"]))

    piece["Zb"] = swap(piece["Xb"], 1)
    turn_x = products([(q, ["Xb"]) for q in before] + [(q, ["Tb", "Nb", "Xb"]) for q in kinds(far, ["b"])], ["Xb"], close=True)

    order = []
    inputs = []
    for n in names:
        for m, kind in enumerate(["T"] + far):
            q = kind + n
            order.append((m, rest if n == "b" else [int(n)], size[q]))
            inputs += [piece[q], state[q]]
    inputs = [piece["Zb"]] + turn_t + turn_n + turn_x + inputs
    send = pl.pallas_call(
        functools.partial(last_kernel, dims, order, rest, size["Zb"]),
        out_shape=shape((n_gy, 1, (n_query + 1) * 128), F32),
        in_specs=[in_vmem] * len(inputs),
        out_specs=in_vmem,
        cost_estimate=cost(2 * width * size["Zb"] * n_query * rows, 0),
        compiler_params=params(),
        name="last",
    )(*inputs)

    back = lax.all_to_all(send, "gy", split_axis=0, concat_axis=0, tiled=True)
    out = pl.pallas_call(
        functools.partial(finish_kernel, dims, rest),
        out_shape=shape((1, rows), F32),
        in_specs=[in_vmem, in_vmem],
        out_specs=in_vmem,
        compiler_params=params(),
        name="finish",
    )(home, back)
    return out.reshape(rows)


def solution(mesh):
    return jax.shard_map(
        per_device,
        mesh=mesh,
        in_specs=(P(("gx", "gy"), None), P(("gx", "gy")), P("gx", None)),
        out_specs=P(("gx", "gy")),
        check_vma=False,
    )
```

```python
import functools

import jax
import jax.numpy as jnp
from jax import lax
from jax.experimental import pallas as pl
from jax.experimental.pallas import tpu as pltpu
from jax.sharding import PartitionSpec as P

F32 = jnp.float32
BF16 = jnp.bfloat16
I32 = jnp.int32
SPARE = 8
KEYS = 4
VMEM = 24 * 1024 * 1024


def iota(shape, dim):
    return lax.broadcasted_iota(I32, shape, dim)


def dot_nt(a, b):
    return lax.dot_general(a, b, (((1,), (1,)), ((), ())), preferred_element_type=F32)


def dot_nn(a, b):
    return lax.dot_general(a, b, (((1,), (0,)), ((), ())), preferred_element_type=F32)


def one_hot(mask):
    return jnp.where(mask, 1.0, 0.0).astype(BF16)


def log2(value):
    assert value & (value - 1) == 0
    return value.bit_length() - 1


def params(limit=VMEM):
    return pltpu.CompilerParams(vmem_limit_bytes=limit)


def cost(flops, size):
    return pl.CostEstimate(flops=flops, bytes_accessed=size, transcendentals=0)


def request_kernel(dims, sizes_hbm, members_hbm, asked_ref, home_ref, sizes_ref, members_ref, sems):
    n_gx, n_gy, rows, quota = dims
    copies = [
        pltpu.make_async_copy(members_hbm, members_ref, sems.at[0]),
        pltpu.make_async_copy(sizes_hbm, sizes_ref, sems.at[1]),
    ]
    for copy in copies:
        copy.start()
    for copy in copies:
        copy.wait()
    owners = n_gx * n_gy
    member = members_ref[...]
    owner = lax.shift_right_logical(member, log2(rows))
    row = member & (rows - 1)
    slot = lax.axis_index("gy") * rows + iota((1, rows), 1)
    cluster = jnp.zeros((1, rows), I32)
    end = jnp.int32(0)
    for c in range(sizes_ref.shape[1]):
        end = end + sizes_ref[0, c]
        cluster = cluster + (slot >= end).astype(I32)
    mask = iota((owners, rows), 0) == owner
    hot = one_hot(mask)
    before = one_hot(iota((128, 128), 0) < iota((128, 128), 1))
    count = jnp.zeros((owners, 1), F32)
    ranks = []
    for b in range(rows // 128):
        part = hot[:, b * 128:(b + 1) * 128]
        rank = dot_nn(part, before) + count
        part32 = part.astype(F32)
        ranks.append(jnp.sum(part32 * rank, axis=0, keepdims=True))
        count = count + jnp.sum(part32, axis=1, keepdims=True)
    rank = jnp.concatenate(ranks, axis=1).astype(I32)
    place = one_hot(iota((quota, rows), 0) == rank)
    low = (row & 255).astype(F32)
    high = lax.shift_right_logical(row, 8).astype(F32)
    zero = jnp.zeros((owners, rows), F32)

    def pick(value):
        return dot_nt(jnp.where(mask, value, zero).astype(BF16), place)

    asked = pick(low) + 256.0 * pick(high) + float(rows) * pick(cluster.astype(F32))
    asked = asked.astype(I32)
    for o in range(owners):
        asked_ref[o] = asked[o:o + 1, :]
    plane = lax.shift_right_logical(owner, log2(n_gy))
    step = (lax.axis_index("gx") - plane) & (n_gx - 1)
    home_ref[0:1, :] = owner & (n_gy - 1)
    home_ref[1:2, :] = step * quota + rank


def select_kernel(dims, steps, asked_ref, unit_ref, *out_refs):
    n_gx, n_gy, rows, quota = dims
    chunk = n_gy * quota
    pick = one_hot((iota((chunk, quota), 0) & (quota - 1)) == iota((chunk, quota), 1))
    block = lax.shift_right_logical(iota((chunk, n_gy), 0), log2(quota))
    own_col = block == iota((chunk, n_gy), 1)
    block_row = lax.shift_right_logical(iota((n_gy, chunk), 1), log2(quota))
    own_row = block_row == iota((n_gy, chunk), 0)
    for step, ref in zip(steps, out_refs):
        plane = (lax.axis_index("gx") + step) & (n_gx - 1)
        wanted = jnp.concatenate([asked_ref[plane * n_gy + d] for d in range(n_gy)], axis=0)
        row = wanted & (rows - 1)
        cluster = lax.shift_right_logical(wanted, log2(rows)).astype(F32).astype(BF16)
        low = (row & 255).astype(F32).astype(BF16)
        high = lax.shift_right_logical(row, 8).astype(F32).astype(BF16)
        index = dot_nt(pick, low) + 256.0 * dot_nt(pick, high)
        index = jnp.sum(jnp.where(own_col, index, 0.0), axis=1, keepdims=True).astype(I32)
        flat = jnp.sum(jnp.where(own_row, dot_nt(cluster, pick), 0.0), axis=0, keepdims=True)
        hot = one_hot(iota((chunk, rows), 1) == index)
        ref[0:chunk, :] = dot_nn(hot, unit_ref[...]).astype(BF16)
        width = unit_ref.shape[1]
        line = jnp.concatenate([flat, jnp.zeros((1, width - chunk), F32)], axis=1)
        ref[chunk:chunk + SPARE, :] = jnp.where(iota((SPARE, width), 0) == 0, line, 0.0).astype(BF16)


def column(line):
    parts = []
    for b in range(line.shape[1] // 128):
        wide = jnp.broadcast_to(line[:, b * 128:(b + 1) * 128], (128, 128))
        parts.append(wide.T)
    return jnp.concatenate(parts, axis=0)


def wide(col, lanes):
    return jnp.concatenate([col] * (lanes // 128), axis=1)


def more(chunks):
    return -(-chunks // SPARE) * SPARE


def cluster_line(ref, size, chunk):
    block = ref[size:size + more(size // chunk), 0:chunk].astype(F32)
    return jnp.concatenate([block[r:r + 1, :] for r in range(size // chunk)], axis=1)


def pack_kernel(groups, sizes, chunk, *refs):
    outs = refs[len(sizes):]
    for group, out_ref in zip(groups, outs):
        at = 0
        total = sum(count for _, _, count in group)
        width = out_ref.shape[1]
        extra = more(total // chunk)
        meta = jnp.zeros((extra, width), F32)
        for i, low, count in group:
            ref, size = refs[i], sizes[i]
            out_ref[at:at + count, :] = ref[low:low + count, :]
            lines = ref[size:size + more(size // chunk), :].astype(F32)
            for r in range(count // chunk):
                meta = jnp.where(iota((extra, width), 0) == at // chunk + r, lines[low // chunk + r:low // chunk + r + 1, :], meta)
            at += count
        out_ref[total:total + extra, :] = meta.astype(BF16)


def product_kernel(pairs, sizes, chunk, started, turned, close, *refs):
    names = sorted({n for q, ks in pairs for n in [q] + ks})
    queries = [q for q, _ in pairs]
    refs = list(refs)
    rows = {n: refs.pop(0) for n in names}
    state = {q: (refs.pop(0), refs.pop(0)) for q in queries if q in started}
    turns = {}
    for q, keys in pairs:
        n_q = sizes[q]
        if q in started:
            col = state[q][0][...]
            best = state[q][1][...]
        else:
            col = column(cluster_line(rows[q], n_q, chunk))
            best = jnp.full((n_q, 128), -1.0, F32)
            if q not in close:
                refs.pop(0)[...] = col
        out_ref = refs.pop(0)
        best = meet_keys(q, keys, rows, sizes, chunk, col, best, turned, turns)
        out_ref[...] = lined(best) if q in close else best
    for k in sorted(turns):
        refs.pop(0)[...] = turns[k]


def meet_keys(q, keys, rows, sizes, chunk, col, best, turned, turns):
    n_q = sizes[q]
    for k in keys:
        n_k = sizes[k]
        sims = dot_nt(rows[q][0:n_q, :], rows[k][0:n_k, :])
        keep = wide(col, n_k) == cluster_line(rows[k], n_k, chunk)
        if k == q:
            keep = keep & (iota((n_q, n_k), 0) != iota((n_q, n_k), 1))
        sims = jnp.where(keep, sims, -1.0)
        for v in range(n_k // 128):
            best = jnp.maximum(best, sims[:, v * 128:(v + 1) * 128])
        if (q, k) in turned:
            line = jnp.max(sims, axis=0, keepdims=True)
            turns[k] = jnp.maximum(turns[k], line) if k in turns else line
    return best


def lined(best):
    rows = best.shape[0]
    parts = [jnp.max(best[b * 128:(b + 1) * 128, :].T, axis=0, keepdims=True) for b in range(rows // 128)]
    return jnp.concatenate(parts, axis=1)


def final_kernel(dims, kinds, pairs, groups, sizes, turned, row_names, line_names, *refs):
    n_gx, n_gy, rows, quota = dims
    chunk = n_gy * quota
    refs = list(refs)
    row_refs = {n: refs.pop(0) for n in row_names}
    line_refs = {n: refs.pop(0) for n in line_names}
    col_ref, best_ref, send_ref = refs
    lines = {n: ref[...] for n, ref in line_refs.items()}
    for q, keys in pairs:
        n_q = sizes[q]
        if q == "Tb":
            col, best = col_ref[...], best_ref[...]
        else:
            col = column(cluster_line(row_refs[q], n_q, chunk))
            best = jnp.full((n_q, 128), -1.0, F32)
        line = lined(meet_keys(q, keys, row_refs, sizes, chunk, col, best, turned, lines))
        lines[q] = jnp.maximum(lines[q], line) if q in lines else line
    blocks = [jnp.full((n_gy, 128), -1.0, F32)] * len(kinds)
    own = lax.shift_right_logical(iota((n_gy, chunk), 1), log2(quota)) == iota((n_gy, chunk), 0)
    lane = lax.shift_right_logical(iota((n_gy, 128), 1), log2(quota))
    for name in sorted(lines):
        for c, (kind, group) in enumerate(groups[name]):
            held = jnp.where(own, lines[name][:, c * chunk:(c + 1) * chunk], 0.0)
            fold = held[:, 0:128]
            for v in range(1, chunk // 128):
                fold = fold + held[:, v * 128:(v + 1) * 128]
            shift = 64
            while shift >= quota:
                fold = fold + pltpu.roll(fold, shift, 1)
                shift //= 2
            at = kinds.index(kind)
            blocks[at] = jnp.where(lane == group, fold, blocks[at])
    whole = jnp.concatenate(blocks, axis=1)
    for d in range(n_gy):
        send_ref[d] = whole[d:d + 1, :]


def far_place(q, m):
    row = q // KEYS
    return q ^ (KEYS * m) ^ (1 if row < row ^ m else 0)


def finish_kernel(dims, stage, home_ref, back_ref, out_ref):
    n_gx, n_gy, rows, quota = dims
    n_query = n_gy // KEYS
    low, high = stage[0] * quota, (stage[-1] + 1) * quota
    lane = iota((n_gy, 128), 1)
    late = (lane >= low) & (lane < high)

    def taken(place, block):
        return jnp.concatenate([back_ref[place(q)][:, block * 128:(block + 1) * 128] for q in range(n_gy)], axis=0)

    found = taken(lambda q: q, 0)
    for m in range(1, n_query):
        part = taken(lambda q, m=m: q ^ (KEYS * m), m)
        last = taken(lambda q, m=m: far_place(q, m), m)
        found = jnp.maximum(found, jnp.where(late, last, part))
    for t in range(1, KEYS):
        found = jnp.maximum(found, taken(lambda q, t=t: q ^ t, n_query - 1 + t))
    high = found.astype(BF16)
    rest = found - high.astype(F32)
    mid = rest.astype(BF16)
    low = (rest - mid.astype(F32)).astype(BF16)
    here = one_hot(iota((128, rows), 0) == home_ref[1:2, :])
    value = (dot_nn(high, here) + dot_nn(mid, here)) + dot_nn(low, here)
    own = iota((n_gy, rows), 0) == home_ref[0:1, :]
    out_ref[...] = jnp.sum(jnp.where(own, value, 0.0), axis=0, keepdims=True)


def shape(dims, dtype):
    return jax.ShapeDtypeStruct(dims, dtype)


def per_device(embeddings, members, sizes):
    rows = members.shape[0]
    width = embeddings.shape[1]
    n_gx = lax.axis_size("gx")
    n_gy = lax.axis_size("gy")
    owners = n_gx * n_gy
    quota = rows // owners
    chunk = n_gy * quota
    n_query = n_gy // KEYS
    dims = (n_gx, n_gy, rows, quota)
    in_vmem = pl.BlockSpec(memory_space=pltpu.VMEM)

    in_hbm = pl.BlockSpec(memory_space=pltpu.HBM)
    asked, home = pl.pallas_call(
        functools.partial(request_kernel, dims),
        out_shape=(shape((owners, 1, quota), I32), shape((2, rows), I32)),
        in_specs=[in_hbm, in_hbm],
        out_specs=(in_vmem, in_vmem),
        scratch_shapes=[
            pltpu.SMEM(sizes.shape, I32),
            pltpu.VMEM((1, rows), I32),
            pltpu.SemaphoreType.DMA((2,)),
        ],
        compiler_params=params(56 * 1024 * 1024),
        name="request",
    )(sizes, members.reshape(1, rows))
    asked = lax.all_to_all(asked, ("gx", "gy"), split_axis=0, concat_axis=0, tiled=True)

    values = embeddings.astype(F32)
    squared = jnp.sum(values * values, axis=1, keepdims=True)
    unit = (values * lax.rsqrt(squared + 1e-06)).astype(BF16)

    stages = [[0], [1, n_gx - 1], list(range(2, n_gx - 1))]

    def meet(*arrays):
        return lax.optimization_barrier(arrays)

    found = {}
    for steps in [stages[1][:1], stages[0], stages[1][1:] + stages[2]]:
        out = pl.pallas_call(
            functools.partial(select_kernel, dims, steps),
            out_shape=[shape((chunk + (2 if k else 1) * SPARE, width), BF16) for k in steps],
            in_specs=[in_vmem, in_vmem],
            out_specs=[in_vmem] * len(steps),
            cost_estimate=cost(2 * len(steps) * chunk * rows * width, rows * width),
            compiler_params=params(),
            name="select",
        )(asked, unit)
        unit, *out = meet(unit, *out)
        found.update(zip(steps, out))

    def across(array, step):
        return lax.ppermute(array, "gx", [(i, (i + step) % n_gx) for i in range(n_gx)])

    def swap(array, mask):
        return lax.ppermute(array, "gy", [(i, i ^ mask) for i in range(n_gy)])

    far = ["Y%d" % m for m in range(1, n_query)]
    edge = stages[1]
    rest = [k for k in stages[2]]
    names = ["%d" % k for k in stages[0] + stages[1]] + ["b"]
    piece = {}
    size = {}
    state = {}
    lines = {}
    for n in names:
        for kind in ["T", "N", "X", "Z"] + far:
            size[kind + n] = chunk * (len(rest) if n == "b" else 1)
    for k in range(n_gx):
        size["z%d" % k] = chunk

    def pack(groups):
        groups = {name: [(g, 0, size[g]) if isinstance(g, str) else g for g in group] for name, group in groups.items()}
        flat = sorted({g[0] for group in groups.values() for g in group})
        for name, group in groups.items():
            size[name] = sum(count for _, _, count in group)
        stretches = [[(flat.index(n), low, count) for n, low, count in group] for group in groups.values()]
        out = pl.pallas_call(
            functools.partial(pack_kernel, stretches, [size[n] for n in flat], chunk),
            out_shape=[shape((size[n] + more(size[n] // chunk), width), BF16) for n in groups],
            in_specs=[in_vmem] * len(flat),
            out_specs=[in_vmem] * len(groups),
            cost_estimate=cost(0, 4 * sum(size[n] for n in groups) * width),
            compiler_params=params(),
            name="pack",
        )(*[piece[n] for n in flat])
        piece.update(zip(groups, out))

    def near(n):
        piece["X" + n] = swap(piece["T" + n], 2)
        for m, kind in enumerate(far):
            piece[kind + n] = swap(piece["T" + n], KEYS * (m + 1))

    def join(names):
        arrays = [piece[n] for n in names] + [a for q in state for a in state[q]]
        arrays = list(meet(*arrays))
        for name in names:
            piece[name] = arrays.pop(0)
        for q in state:
            state[q] = (arrays.pop(0), arrays.pop(0))

    def kinds(kinds, names):
        return [k + n for n in names for k in kinds]

    def products(pairs, turned=(), close=()):
        names = sorted({n for q, ks in pairs for n in [q] + ks})
        queries = [q for q, _ in pairs]
        started = [q for q in queries if q in state]
        inputs = [piece[n] for n in names] + [a for q in started for a in state[q]]
        outs = []
        for q in queries:
            if q in close:
                outs.append(shape((1, size[q]), F32))
            else:
                outs += [shape((size[q], 128), F32)] * (1 if q in started else 2)
        turns = sorted({k for _, k in turned})
        outs += [shape((1, size[k]), F32) for k in turns]
        flops = sum(2 * width * size[q] * size[k] for q, ks in pairs for k in ks)
        out = pl.pallas_call(
            functools.partial(product_kernel, pairs, size, chunk, started, set(turned), close),
            out_shape=outs,
            in_specs=[in_vmem] * len(inputs),
            out_specs=[in_vmem] * len(outs),
            cost_estimate=cost(flops, 0),
            compiler_params=params(),
            name="products",
        )(*inputs)
        out = list(out)
        for q in queries:
            if q in close:
                del state[q]
                lines[q] = out.pop(0)
            else:
                col = state[q][0] if q in started else out.pop(0)
                state[q] = (col, out.pop(0))
        for k, line in zip(turns, out):
            assert k not in lines
            lines[k] = line

    def swap_core(name, group):
        pack({"P": group})
        piece[name] = swap(piece["P"], 1)
        size[name] = size["P"]

    first, second = edge
    a, b = "%d" % first, "%d" % second
    one = ["0", a, b]
    for k in edge:
        piece["z%d" % k] = across(found[k], k)
    piece["T0"] = found[0]
    near("0")
    piece["N0"] = swap(piece["T0"], 1)
    for k in rest:
        piece["f%d" % k] = found[k]
    join(["z" + a] + ["f%d" % k for k in rest] + kinds(["T", "X", "N"] + far, ["0"]))

    for k in rest:
        piece["z%d" % k] = across(piece["f%d" % k], k)
    pack({"T" + a: ["z" + a]})
    near(a)
    piece["Z0"] = swap(piece["X0"], 1)
    keys = ["T0", "N0", "X0", "T" + a]
    before = ["T0"] + kinds(far, ["0"]) + ["T" + a]
    products([(q, keys) for q in before])
    join(["z" + b, "Z0"] + kinds(["T", "X"] + far, [a]))

    pack({"T" + b: ["z" + b]})
    near(b)
    new = ["X" + a, "T" + b, "Z0"]
    keys = keys + new
    late = kinds(far, [a]) + ["T" + b]
    products([(q, new) for q in before] + [(q, keys) for q in late])
    before = before + late
    join(["z%d" % k for k in rest] + kinds(["T", "X"] + far, [b]))

    pack({"Tb": ["z%d" % k for k in rest]})
    piece["Xb"] = swap(piece["Tb"], 2)
    for m, kind in enumerate(far):
        size[kind + "b"] = size["Tb"]
        piece[kind + "b"] = lax.ppermute(piece["Tb"], "gy", [(q, far_place(q, m + 1)) for q in range(n_gy)])
    swap_core("Q", kinds(["T", "X"], [a, b]) + ["Tb"])
    count = [size["T" + a], size["X" + a], size["T" + b], size["X" + b], size["Tb"]]
    start = [sum(count[:i]) for i in range(len(count))]
    take = [("Q", start[i], count[i]) for i in range(len(count))]
    pack({"Ns": [take[0], take[2]], "Zs": [take[1], take[3]], "Nb": [take[4]]})
    third = kinds(far, [b])
    keys = keys + ["X" + b]
    sides = kinds(["X"], one)
    products(
        [(q, ["X" + b, "Tb"]) for q in before]
        + [(q, keys + ["Tb"]) for q in third]
        + [("Tb", ["N0", "Z0"] + sides + ["Tb"])],
        [(q, "Tb") for q in before + third] + [("Tb", k) for k in sides + ["Z0"]],
    )
    before = before + third
    olds = kinds(far, one)
    products(
        [(q, ["Ns", "Zs", "Nb"]) for q in before + ["Tb"]],
        [(q, "Nb") for q in olds] + [("Tb", "Zs")],
        before,
    )
    join(["Tb", "Nb", "Xb"] + kinds(far, ["b"]))

    news = kinds(far, ["b"])
    pairs = [("Tb", ["Xb"]), ("Nb", ["Xb"])] + [(q, sides + ["Z0", "Zs", "Tb", "Nb", "Xb"]) for q in news]
    turned = {(q, k) for q in news for k in sides + ["Z0", "Zs", "Xb"]}
    groups = {}
    for n in one:
        for kind in ["T", "X", "Z"] + far:
            groups[kind + n] = [(kind, int(n))]
    for kind in ["T", "N", "X"] + far:
        groups[kind + "b"] = [(kind, k) for k in rest]
    groups["Zs"] = [("Z", first), ("Z", second)]
    row_names = sorted({n for q, ks in pairs for n in [q] + ks})
    line_names = sorted(lines)
    inputs = [piece[n] for n in row_names] + [lines[n] for n in line_names] + list(state["Tb"])
    shown = ["T"] + far + ["N", "X", "Z"]
    send = pl.pallas_call(
        functools.partial(final_kernel, dims, shown, pairs, groups, size, turned, row_names, line_names),
        out_shape=shape((n_gy, 1, len(shown) * 128), F32),
        in_specs=[in_vmem] * len(inputs),
        out_specs=in_vmem,
        cost_estimate=cost(sum(2 * width * size[q] * size[k] for q, ks in pairs for k in ks), 0),
        compiler_params=params(),
        name="final",
    )(*inputs)

    back = lax.all_to_all(send, "gy", split_axis=0, concat_axis=0, tiled=True)
    out = pl.pallas_call(
        functools.partial(finish_kernel, dims, rest),
        out_shape=shape((1, rows), F32),
        in_specs=[in_vmem, in_vmem],
        out_specs=in_vmem,
        compiler_params=params(),
        name="finish",
    )(home, back)
    return out.reshape(rows)


def solution(mesh):
    return jax.shard_map(
        per_device,
        mesh=mesh,
        in_specs=(P(("gx", "gy"), None), P(("gx", "gy")), P("gx", None)),
        out_specs=P(("gx", "gy")),
        check_vma=False,
    )
```

```python
import functools

import jax
import jax.numpy as jnp
from jax import lax
from jax.experimental import pallas as pl
from jax.experimental.pallas import tpu as pltpu
from jax.sharding import PartitionSpec as P

F32 = jnp.float32
BF16 = jnp.bfloat16
I32 = jnp.int32
SPARE = 8
KEYS = 4
VMEM = 24 * 1024 * 1024


def iota(shape, dim):
    return lax.broadcasted_iota(I32, shape, dim)


def dot_nt(a, b):
    return lax.dot_general(a, b, (((1,), (1,)), ((), ())), preferred_element_type=F32)


def dot_nn(a, b):
    return lax.dot_general(a, b, (((1,), (0,)), ((), ())), preferred_element_type=F32)


def one_hot(mask):
    return jnp.where(mask, 1.0, 0.0).astype(BF16)


def log2(value):
    assert value & (value - 1) == 0
    return value.bit_length() - 1


def params(limit=VMEM):
    return pltpu.CompilerParams(vmem_limit_bytes=limit)


def cost(flops, size):
    return pl.CostEstimate(flops=flops, bytes_accessed=size, transcendentals=0)


def request_kernel(dims, sizes_hbm, members_hbm, asked_ref, home_ref, sizes_ref, members_ref, sems):
    n_gx, n_gy, rows, quota = dims
    copies = [
        pltpu.make_async_copy(members_hbm, members_ref, sems.at[0]),
        pltpu.make_async_copy(sizes_hbm, sizes_ref, sems.at[1]),
    ]
    for copy in copies:
        copy.start()
    for copy in copies:
        copy.wait()
    owners = n_gx * n_gy
    member = members_ref[...]
    owner = lax.shift_right_logical(member, log2(rows))
    row = member & (rows - 1)
    slot = lax.axis_index("gy") * rows + iota((1, rows), 1)
    cluster = jnp.zeros((1, rows), I32)
    end = jnp.int32(0)
    for c in range(sizes_ref.shape[1]):
        end = end + sizes_ref[0, c]
        cluster = cluster + (slot >= end).astype(I32)
    mask = iota((owners, rows), 0) == owner
    hot = one_hot(mask)
    before = one_hot(iota((128, 128), 0) < iota((128, 128), 1))
    count = jnp.zeros((owners, 1), F32)
    ranks = []
    parts = [hot[:, b * 128:(b + 1) * 128] for b in range(rows // 128)]
    inner = dot_nn(jnp.concatenate(parts, axis=0), before)
    for b, part in enumerate(parts):
        rank = inner[b * owners:(b + 1) * owners, :] + count
        part32 = part.astype(F32)
        ranks.append(jnp.sum(part32 * rank, axis=0, keepdims=True))
        count = count + jnp.sum(part32, axis=1, keepdims=True)
    rank = jnp.concatenate(ranks, axis=1).astype(I32)
    place = one_hot(iota((quota, rows), 0) == rank)
    low = (row & 255).astype(F32)
    high = lax.shift_right_logical(row, 8).astype(F32)
    zero = jnp.zeros((owners, rows), F32)

    values = [jnp.where(mask, v, zero).astype(BF16) for v in (low, high, cluster.astype(F32))]
    picked = dot_nt(jnp.concatenate(values, axis=0), place)
    low, high, held = (picked[i * owners:(i + 1) * owners, :] for i in range(3))
    asked = (low + 256.0 * high + float(rows) * held).astype(I32)
    for o in range(owners):
        asked_ref[o] = asked[o:o + 1, :]
    plane = lax.shift_right_logical(owner, log2(n_gy))
    step = (lax.axis_index("gx") - plane) & (n_gx - 1)
    home_ref[0:1, :] = owner & (n_gy - 1)
    home_ref[1:2, :] = step * quota + rank


def select_kernel(dims, steps, asked_ref, unit_ref, *out_refs):
    n_gx, n_gy, rows, quota = dims
    chunk = n_gy * quota
    pick = one_hot((iota((chunk, quota), 0) & (quota - 1)) == iota((chunk, quota), 1))
    block = lax.shift_right_logical(iota((chunk, n_gy), 0), log2(quota))
    own_col = block == iota((chunk, n_gy), 1)
    block_row = lax.shift_right_logical(iota((n_gy, chunk), 1), log2(quota))
    own_row = block_row == iota((n_gy, chunk), 0)
    for step, ref in zip(steps, out_refs):
        plane = (lax.axis_index("gx") + step) & (n_gx - 1)
        wanted = jnp.concatenate([asked_ref[plane * n_gy + d] for d in range(n_gy)], axis=0)
        row = wanted & (rows - 1)
        cluster = lax.shift_right_logical(wanted, log2(rows)).astype(F32).astype(BF16)
        low = (row & 255).astype(F32).astype(BF16)
        high = lax.shift_right_logical(row, 8).astype(F32).astype(BF16)
        index = dot_nt(pick, low) + 256.0 * dot_nt(pick, high)
        index = jnp.sum(jnp.where(own_col, index, 0.0), axis=1, keepdims=True).astype(I32)
        flat = jnp.sum(jnp.where(own_row, dot_nt(cluster, pick), 0.0), axis=0, keepdims=True)
        hot = one_hot(iota((chunk, rows), 1) == index)
        ref[0:chunk, :] = dot_nn(hot, unit_ref[...]).astype(BF16)
        width = unit_ref.shape[1]
        line = jnp.concatenate([flat, jnp.zeros((1, width - chunk), F32)], axis=1)
        ref[chunk:chunk + 1, :] = line.astype(BF16)


def column(line):
    parts = []
    for b in range(line.shape[1] // 128):
        wide = jnp.broadcast_to(line[:, b * 128:(b + 1) * 128], (128, 128))
        parts.append(wide.T)
    return jnp.concatenate(parts, axis=0)


def wide(col, lanes):
    return jnp.concatenate([col] * (lanes // 128), axis=1)


def more(chunks):
    return chunks


def cluster_line(ref, size, chunk):
    block = ref[size:size + more(size // chunk), 0:chunk].astype(F32)
    return jnp.concatenate([block[r:r + 1, :] for r in range(size // chunk)], axis=1)


def pack_kernel(groups, sizes, chunk, *refs):
    outs = refs[len(sizes):]
    for group, out_ref in zip(groups, outs):
        at = 0
        total = sum(count for _, _, count in group)
        width = out_ref.shape[1]
        extra = more(total // chunk)
        meta = jnp.zeros((extra, width), F32)
        for i, low, count in group:
            ref, size = refs[i], sizes[i]
            out_ref[at:at + count, :] = ref[low:low + count, :]
            lines = ref[size:size + more(size // chunk), :].astype(F32)
            for r in range(count // chunk):
                meta = jnp.where(iota((extra, width), 0) == at // chunk + r, lines[low // chunk + r:low // chunk + r + 1, :], meta)
            at += count
        out_ref[total:total + extra, :] = meta.astype(BF16)


def product_kernel(pairs, sizes, chunk, started, turned, close, *refs):
    names = sorted({n for q, ks in pairs for n in [q] + ks})
    queries = [q for q, _ in pairs]
    refs = list(refs)
    rows = {n: refs.pop(0) for n in names}
    state = {q: (refs.pop(0), refs.pop(0)) for q in queries if q in started}
    turns = {}
    for q, keys in pairs:
        n_q = sizes[q]
        if q in started:
            col = state[q][0][...]
            best = state[q][1][...]
        else:
            col = column(cluster_line(rows[q], n_q, chunk))
            best = jnp.full((n_q, 128), -1.0, F32)
            if q not in close:
                refs.pop(0)[...] = col
        out_ref = refs.pop(0)
        best = meet_keys(q, keys, rows, sizes, chunk, col, best, turned, turns)
        out_ref[...] = lined(best) if q in close else best
    for k in sorted(turns):
        refs.pop(0)[...] = turns[k]


def meet_keys(q, keys, rows, sizes, chunk, col, best, turned, turns):
    n_q = sizes[q]
    for k in keys:
        n_k = sizes[k]
        sims = dot_nt(rows[q][0:n_q, :], rows[k][0:n_k, :])
        keep = wide(col, n_k) == cluster_line(rows[k], n_k, chunk)
        if k == q:
            keep = keep & (iota((n_q, n_k), 0) != iota((n_q, n_k), 1))
        sims = jnp.where(keep, sims, -1.0)
        for v in range(n_k // 128):
            best = jnp.maximum(best, sims[:, v * 128:(v + 1) * 128])
        if (q, k) in turned:
            line = jnp.max(sims, axis=0, keepdims=True)
            turns[k] = jnp.maximum(turns[k], line) if k in turns else line
    return best


def lined(best):
    rows = best.shape[0]
    parts = [jnp.max(best[b * 128:(b + 1) * 128, :].T, axis=0, keepdims=True) for b in range(rows // 128)]
    return jnp.concatenate(parts, axis=1)


def final_kernel(dims, kinds, pairs, groups, sizes, turned, row_names, line_names, *refs):
    n_gx, n_gy, rows, quota = dims
    chunk = n_gy * quota
    refs = list(refs)
    row_refs = {n: refs.pop(0) for n in row_names}
    line_refs = {n: refs.pop(0) for n in line_names}
    col_ref, best_ref, send_ref = refs
    lines = {n: ref[...] for n, ref in line_refs.items()}
    for q, keys in pairs:
        n_q = sizes[q]
        if q == "Tb":
            col, best = col_ref[...], best_ref[...]
        else:
            col = column(cluster_line(row_refs[q], n_q, chunk))
            best = jnp.full((n_q, 128), -1.0, F32)
        line = lined(meet_keys(q, keys, row_refs, sizes, chunk, col, best, turned, lines))
        lines[q] = jnp.maximum(lines[q], line) if q in lines else line
    blocks = [jnp.full((n_gy, 128), -1.0, F32)] * len(kinds)
    own = lax.shift_right_logical(iota((n_gy, chunk), 1), log2(quota)) == iota((n_gy, chunk), 0)
    lane = lax.shift_right_logical(iota((n_gy, 128), 1), log2(quota))
    for name in sorted(lines):
        for c, (kind, group) in enumerate(groups[name]):
            held = jnp.where(own, lines[name][:, c * chunk:(c + 1) * chunk], 0.0)
            fold = held[:, 0:128]
            for v in range(1, chunk // 128):
                fold = fold + held[:, v * 128:(v + 1) * 128]
            shift = 64
            while shift >= quota:
                fold = fold + pltpu.roll(fold, shift, 1)
                shift //= 2
            at = kinds.index(kind)
            blocks[at] = jnp.where(lane == group, fold, blocks[at])
    whole = jnp.concatenate(blocks, axis=1)
    for d in range(n_gy):
        send_ref[d] = whole[d:d + 1, :]


def far_place(q, m):
    row = q // KEYS
    return q ^ (KEYS * m) ^ (1 if row < row ^ m else 0)


def finish_kernel(dims, stage, home_ref, back_ref, out_ref):
    n_gx, n_gy, rows, quota = dims
    n_query = n_gy // KEYS
    low, high = stage[0] * quota, (stage[-1] + 1) * quota
    lane = iota((n_gy, 128), 1)
    late = (lane >= low) & (lane < high)

    def taken(place, block):
        return jnp.concatenate([back_ref[place(q)][:, block * 128:(block + 1) * 128] for q in range(n_gy)], axis=0)

    found = taken(lambda q: q, 0)
    for m in range(1, n_query):
        part = taken(lambda q, m=m: q ^ (KEYS * m), m)
        last = taken(lambda q, m=m: far_place(q, m), m)
        found = jnp.maximum(found, jnp.where(late, last, part))
    for t in range(1, KEYS):
        found = jnp.maximum(found, taken(lambda q, t=t: q ^ t, n_query - 1 + t))
    high = found.astype(BF16)
    rest = found - high.astype(F32)
    mid = rest.astype(BF16)
    low = (rest - mid.astype(F32)).astype(BF16)
    here = one_hot(iota((128, rows), 0) == home_ref[1:2, :])
    value = dot_nn(jnp.concatenate([high.astype(F32), mid.astype(F32), low.astype(F32)], axis=0).astype(BF16), here)
    value = (value[0:n_gy] + value[n_gy:2 * n_gy]) + value[2 * n_gy:3 * n_gy]
    own = iota((n_gy, rows), 0) == home_ref[0:1, :]
    out_ref[...] = jnp.sum(jnp.where(own, value, 0.0), axis=0, keepdims=True)


def shape(dims, dtype):
    return jax.ShapeDtypeStruct(dims, dtype)


def per_device(embeddings, members, sizes):
    rows = members.shape[0]
    width = embeddings.shape[1]
    n_gx = lax.axis_size("gx")
    n_gy = lax.axis_size("gy")
    owners = n_gx * n_gy
    quota = rows // owners
    chunk = n_gy * quota
    n_query = n_gy // KEYS
    dims = (n_gx, n_gy, rows, quota)
    in_vmem = pl.BlockSpec(memory_space=pltpu.VMEM)

    in_hbm = pl.BlockSpec(memory_space=pltpu.HBM)
    asked, home = pl.pallas_call(
        functools.partial(request_kernel, dims),
        out_shape=(shape((owners, 1, quota), I32), shape((2, rows), I32)),
        in_specs=[in_hbm, in_hbm],
        out_specs=(in_vmem, in_vmem),
        scratch_shapes=[
            pltpu.SMEM(sizes.shape, I32),
            pltpu.VMEM((1, rows), I32),
            pltpu.SemaphoreType.DMA((2,)),
        ],
        compiler_params=params(56 * 1024 * 1024),
        name="request",
    )(sizes, members.reshape(1, rows))
    asked = lax.all_to_all(asked, ("gx", "gy"), split_axis=0, concat_axis=0, tiled=True)

    values = embeddings.astype(F32)
    squared = jnp.sum(values * values, axis=1, keepdims=True)
    unit = (values * lax.rsqrt(squared + 1e-06)).astype(BF16)

    stages = [[0], [1, n_gx - 1], list(range(2, n_gx - 1))]

    def meet(*arrays):
        return lax.optimization_barrier(arrays)

    found = {}
    for steps in [stages[1][:1], stages[0], stages[1][1:] + stages[2]]:
        out = pl.pallas_call(
            functools.partial(select_kernel, dims, steps),
            out_shape=[shape((chunk + (SPARE if k else 1), width), BF16) for k in steps],
            in_specs=[in_vmem, in_vmem],
            out_specs=[in_vmem] * len(steps),
            cost_estimate=cost(2 * len(steps) * chunk * rows * width, rows * width),
            compiler_params=params(),
            name="select",
        )(asked, unit)
        unit, *out = meet(unit, *out)
        found.update(zip(steps, out))

    def across(array, step):
        return lax.ppermute(array, "gx", [(i, (i + step) % n_gx) for i in range(n_gx)])

    def swap(array, mask):
        return lax.ppermute(array, "gy", [(i, i ^ mask) for i in range(n_gy)])

    far = ["Y%d" % m for m in range(1, n_query)]
    edge = stages[1]
    rest = [k for k in stages[2]]
    names = ["%d" % k for k in stages[0] + stages[1]] + ["b"]
    piece = {}
    size = {}
    state = {}
    lines = {}
    for n in names:
        for kind in ["T", "N", "X", "Z"] + far:
            size[kind + n] = chunk * (len(rest) if n == "b" else 1)
    for k in range(n_gx):
        size["z%d" % k] = chunk

    def pack(groups):
        groups = {name: [(g, 0, size[g]) if isinstance(g, str) else g for g in group] for name, group in groups.items()}
        flat = sorted({g[0] for group in groups.values() for g in group})
        for name, group in groups.items():
            size[name] = sum(count for _, _, count in group)
        stretches = [[(flat.index(n), low, count) for n, low, count in group] for group in groups.values()]
        out = pl.pallas_call(
            functools.partial(pack_kernel, stretches, [size[n] for n in flat], chunk),
            out_shape=[shape((size[n] + more(size[n] // chunk), width), BF16) for n in groups],
            in_specs=[in_vmem] * len(flat),
            out_specs=[in_vmem] * len(groups),
            cost_estimate=cost(0, 4 * sum(size[n] for n in groups) * width),
            compiler_params=params(),
            name="pack",
        )(*[piece[n] for n in flat])
        piece.update(zip(groups, out))

    def near(n):
        piece["X" + n] = swap(piece["T" + n], 2)
        for m, kind in enumerate(far):
            piece[kind + n] = swap(piece["T" + n], KEYS * (m + 1))

    def join(names):
        arrays = [piece[n] for n in names] + [a for q in state for a in state[q]]
        arrays = list(meet(*arrays))
        for name in names:
            piece[name] = arrays.pop(0)
        for q in state:
            state[q] = (arrays.pop(0), arrays.pop(0))

    def kinds(kinds, names):
        return [k + n for n in names for k in kinds]

    def products(pairs, turned=(), close=()):
        names = sorted({n for q, ks in pairs for n in [q] + ks})
        queries = [q for q, _ in pairs]
        started = [q for q in queries if q in state]
        inputs = [piece[n] for n in names] + [a for q in started for a in state[q]]
        outs = []
        for q in queries:
            if q in close:
                outs.append(shape((1, size[q]), F32))
            else:
                outs += [shape((size[q], 128), F32)] * (1 if q in started else 2)
        turns = sorted({k for _, k in turned})
        outs += [shape((1, size[k]), F32) for k in turns]
        flops = sum(2 * width * size[q] * size[k] for q, ks in pairs for k in ks)
        out = pl.pallas_call(
            functools.partial(product_kernel, pairs, size, chunk, started, set(turned), close),
            out_shape=outs,
            in_specs=[in_vmem] * len(inputs),
            out_specs=[in_vmem] * len(outs),
            cost_estimate=cost(flops, 0),
            compiler_params=params(),
            name="products",
        )(*inputs)
        out = list(out)
        for q in queries:
            if q in close:
                del state[q]
                lines[q] = out.pop(0)
            else:
                col = state[q][0] if q in started else out.pop(0)
                state[q] = (col, out.pop(0))
        for k, line in zip(turns, out):
            assert k not in lines
            lines[k] = line

    def swap_core(name, group):
        pack({"P": group})
        piece[name] = swap(piece["P"], 1)
        size[name] = size["P"]

    first, second = edge
    a, b = "%d" % first, "%d" % second
    one = ["0", a, b]
    for k in edge:
        piece["z%d" % k] = across(found[k], k)
    piece["T0"] = found[0]
    near("0")
    piece["N0"] = swap(piece["T0"], 1)
    for k in rest:
        piece["f%d" % k] = found[k]
    join(["z" + a] + ["f%d" % k for k in rest] + kinds(["T", "X", "N"] + far, ["0"]))

    for k in rest:
        piece["z%d" % k] = across(piece["f%d" % k], k)
    pack({"T" + a: ["z" + a]})
    near(a)
    piece["Z0"] = swap(piece["X0"], 1)
    keys = ["T0", "N0", "X0", "T" + a]
    before = ["T0"] + kinds(far, ["0"]) + ["T" + a]
    products([(q, keys) for q in before])
    join(["z" + b, "Z0"] + kinds(["T", "X"] + far, [a]))

    pack({"T" + b: ["z" + b]})
    near(b)
    new = ["X" + a, "T" + b, "Z0"]
    keys = keys + new
    late = kinds(far, [a]) + ["T" + b]
    products([(q, new) for q in before] + [(q, keys) for q in late])
    before = before + late
    join(["z%d" % k for k in rest] + kinds(["T", "X"] + far, [b]))

    pack({"Tb": ["z%d" % k for k in rest]})
    piece["Xb"] = swap(piece["Tb"], 2)
    for m, kind in enumerate(far):
        size[kind + "b"] = size["Tb"]
        piece[kind + "b"] = lax.ppermute(piece["Tb"], "gy", [(q, far_place(q, m + 1)) for q in range(n_gy)])
    swap_core("Q", kinds(["T", "X"], [a, b]) + ["Tb"])
    count = [size["T" + a], size["X" + a], size["T" + b], size["X" + b], size["Tb"]]
    start = [sum(count[:i]) for i in range(len(count))]
    take = [("Q", start[i], count[i]) for i in range(len(count))]
    pack({"Ns": [take[0], take[2]], "Zs": [take[1], take[3]], "Nb": [take[4]]})
    third = kinds(far, [b])
    keys = keys + ["X" + b]
    sides = kinds(["X"], one)
    products(
        [(q, ["X" + b, "Tb"]) for q in before]
        + [(q, keys + ["Tb"]) for q in third]
        + [("Tb", ["N0", "Z0"] + sides + ["Tb"])],
        [(q, "Tb") for q in before + third] + [("Tb", k) for k in sides + ["Z0"]],
    )
    before = before + third
    olds = kinds(far, one)
    products(
        [(q, ["Ns", "Zs", "Nb"]) for q in before + ["Tb"]],
        [(q, "Nb") for q in olds] + [("Tb", "Zs")],
        before,
    )
    join(["Tb", "Nb", "Xb"] + kinds(far, ["b"]))

    news = kinds(far, ["b"])
    pairs = [("Tb", ["Xb"]), ("Nb", ["Xb"])] + [(q, sides + ["Z0", "Zs", "Tb", "Nb", "Xb"]) for q in news]
    turned = {(q, k) for q in news for k in sides + ["Z0", "Zs", "Xb"]}
    groups = {}
    for n in one:
        for kind in ["T", "X", "Z"] + far:
            groups[kind + n] = [(kind, int(n))]
    for kind in ["T", "N", "X"] + far:
        groups[kind + "b"] = [(kind, k) for k in rest]
    groups["Zs"] = [("Z", first), ("Z", second)]
    row_names = sorted({n for q, ks in pairs for n in [q] + ks})
    line_names = sorted(lines)
    inputs = [piece[n] for n in row_names] + [lines[n] for n in line_names] + list(state["Tb"])
    shown = ["T"] + far + ["N", "X", "Z"]
    send = pl.pallas_call(
        functools.partial(final_kernel, dims, shown, pairs, groups, size, turned, row_names, line_names),
        out_shape=shape((n_gy, 1, len(shown) * 128), F32),
        in_specs=[in_vmem] * len(inputs),
        out_specs=in_vmem,
        cost_estimate=cost(sum(2 * width * size[q] * size[k] for q, ks in pairs for k in ks), 0),
        compiler_params=params(),
        name="final",
    )(*inputs)

    back = lax.all_to_all(send, "gy", split_axis=0, concat_axis=0, tiled=True)
    out = pl.pallas_call(
        functools.partial(finish_kernel, dims, rest),
        out_shape=shape((1, rows), F32),
        in_specs=[in_vmem, in_vmem],
        out_specs=in_vmem,
        compiler_params=params(),
        name="finish",
    )(home, back)
    return out.reshape(rows)


def solution(mesh):
    return jax.shard_map(
        per_device,
        mesh=mesh,
        in_specs=(P(("gx", "gy"), None), P(("gx", "gy")), P("gx", None)),
        out_specs=P(("gx", "gy")),
        check_vma=False,
    )
```

```python
import functools

import jax
import jax.numpy as jnp
from jax import lax
from jax.experimental import pallas as pl
from jax.experimental.pallas import tpu as pltpu
from jax.sharding import PartitionSpec as P

F32 = jnp.float32
BF16 = jnp.bfloat16
I32 = jnp.int32
SPARE = 8
KEYS = 4
VMEM = 24 * 1024 * 1024
LAST = 4
WEIGHT = 20.0


def iota(shape, dim):
    return lax.broadcasted_iota(I32, shape, dim)


def dot_nt(a, b):
    return lax.dot_general(a, b, (((1,), (1,)), ((), ())), preferred_element_type=F32)


def dot_nn(a, b):
    return lax.dot_general(a, b, (((1,), (0,)), ((), ())), preferred_element_type=F32)


def one_hot(mask):
    return jnp.where(mask, 1.0, 0.0).astype(BF16)


def log2(value):
    assert value & (value - 1) == 0
    return value.bit_length() - 1


def params(limit=VMEM):
    return pltpu.CompilerParams(vmem_limit_bytes=limit)


def cost(flops, size):
    return pl.CostEstimate(flops=flops, bytes_accessed=size, transcendentals=0)


def request_kernel(dims, sizes_hbm, members_hbm, asked_ref, home_ref, sizes_ref, members_ref, sems):
    n_gx, n_gy, rows, quota = dims
    copies = [
        pltpu.make_async_copy(members_hbm, members_ref, sems.at[0]),
        pltpu.make_async_copy(sizes_hbm, sizes_ref, sems.at[1]),
    ]
    for copy in copies:
        copy.start()
    for copy in copies:
        copy.wait()
    owners = n_gx * n_gy
    member = members_ref[...]
    owner = lax.shift_right_logical(member, log2(rows))
    row = member & (rows - 1)
    slot = lax.axis_index("gy") * rows + iota((1, rows), 1)
    cluster = jnp.zeros((1, rows), I32)
    end = jnp.int32(0)
    for c in range(sizes_ref.shape[1]):
        end = end + sizes_ref[0, c]
        cluster = cluster + (slot >= end).astype(I32)
    mask = iota((owners, rows), 0) == owner
    hot = one_hot(mask)
    before = one_hot(iota((128, 128), 0) < iota((128, 128), 1))
    count = jnp.zeros((owners, 1), F32)
    ranks = []
    parts = [hot[:, b * 128:(b + 1) * 128] for b in range(rows // 128)]
    inner = dot_nn(jnp.concatenate(parts, axis=0), before)
    for b, part in enumerate(parts):
        rank = inner[b * owners:(b + 1) * owners, :] + count
        part32 = part.astype(F32)
        ranks.append(jnp.sum(part32 * rank, axis=0, keepdims=True))
        count = count + jnp.sum(part32, axis=1, keepdims=True)
    rank = jnp.concatenate(ranks, axis=1).astype(I32)
    place = one_hot(iota((quota, rows), 0) == rank)
    low = (row & 255).astype(F32)
    high = lax.shift_right_logical(row, 8).astype(F32)
    zero = jnp.zeros((owners, rows), F32)

    values = [jnp.where(mask, v, zero).astype(BF16) for v in (low, high, cluster.astype(F32))]
    picked = dot_nt(jnp.concatenate(values, axis=0), place)
    low, high, held = (picked[i * owners:(i + 1) * owners, :] for i in range(3))
    asked = (low + 256.0 * high + float(rows) * held).astype(I32)
    for o in range(owners):
        asked_ref[o] = asked[o:o + 1, :]
    plane = lax.shift_right_logical(owner, log2(n_gy))
    step = (lax.axis_index("gx") - plane) & (n_gx - 1)
    home_ref[0:1, :] = owner & (n_gy - 1)
    home_ref[1:2, :] = step * quota + rank


def select_kernel(dims, parts, asked_ref, unit_ref, *out_refs):
    n_gx, n_gy, rows, quota = dims
    chunk = n_gy * quota
    pick = one_hot((iota((chunk, quota), 0) & (quota - 1)) == iota((chunk, quota), 1))
    block = lax.shift_right_logical(iota((chunk, n_gy), 0), log2(quota))
    own_col = block == iota((chunk, n_gy), 1)
    block_row = lax.shift_right_logical(iota((n_gy, chunk), 1), log2(quota))
    own_row = block_row == iota((n_gy, chunk), 0)
    refs = list(out_refs)
    width = unit_ref.shape[1]
    for step in sorted({k for k, _, _ in parts}):
        plane = (lax.axis_index("gx") + step) & (n_gx - 1)
        wanted = jnp.concatenate([asked_ref[plane * n_gy + d] for d in range(n_gy)], axis=0)
        row = wanted & (rows - 1)
        cluster = lax.shift_right_logical(wanted, log2(rows)).astype(F32).astype(BF16)
        low = (row & 255).astype(F32).astype(BF16)
        high = lax.shift_right_logical(row, 8).astype(F32).astype(BF16)
        index = dot_nt(pick, low) + 256.0 * dot_nt(pick, high)
        index = jnp.sum(jnp.where(own_col, index, 0.0), axis=1, keepdims=True).astype(I32)
        flat = jnp.sum(jnp.where(own_row, dot_nt(cluster, pick), 0.0), axis=0, keepdims=True)
        hot = one_hot(iota((chunk, rows), 1) == index)
        found = dot_nn(hot, unit_ref[...]).astype(BF16)
        for ref, (k, first, count) in zip(out_refs, parts):
            if k == step:
                ref[0:count, :] = found[first:first + count, :]
                line = [flat[:, first:first + count], jnp.zeros((1, width - count), F32)]
                ref[count:count + 1, :] = jnp.concatenate(line, axis=1).astype(BF16)


def column(line):
    parts = []
    for b in range(line.shape[1] // 128):
        wide = jnp.broadcast_to(line[:, b * 128:(b + 1) * 128], (128, 128))
        parts.append(wide.T)
    return jnp.concatenate(parts, axis=0)


def wide(col, lanes):
    return jnp.concatenate([col] * (lanes // 128), axis=1)


def length(parts):
    return sum(count for _, _, count in parts)


def cluster_line(ref, parts):
    size = length(parts)
    block = ref[size:size + len(parts), :].astype(F32)
    return jnp.concatenate([block[r:r + 1, 0:part[2]] for r, part in enumerate(parts)], axis=1)


def pack_kernel(groups, *refs):
    refs = list(refs)
    outs = refs[sum(len(g) for g in groups):]
    for group, out_ref in zip(groups, outs):
        at = 0
        total = sum(length(parts) for parts in group)
        width = out_ref.shape[1]
        lines = []
        for parts in group:
            ref, size = refs.pop(0), length(parts)
            out_ref[at:at + size, :] = ref[0:size, :]
            lines.append(ref[size:size + len(parts), :].astype(F32))
            at += size
        count = sum(len(parts) for parts in group)
        out_ref[total:total + count, :] = jnp.concatenate(lines, axis=0).astype(BF16)


def split_kernel(pieces, ref, *outs):
    total = sum(length(parts) for parts in pieces)
    at = 0
    row = total
    for parts, out_ref in zip(pieces, outs):
        size = length(parts)
        out_ref[0:size, :] = ref[at:at + size, :]
        out_ref[size:size + len(parts), :] = ref[row:row + len(parts), :]
        at += size
        row += len(parts)


def needed(one, two):
    (a, s), (b, t) = sorted([(n[0], int(n[-1])) for n in (one, two)], key=lambda n: "TNXY".index(n[0]))
    if a + b in ("TN", "TX"):
        return s >= t
    if a + b == "NX":
        return s == t or s < t < LAST or s == LAST
    if a + b == "TY":
        return s == LAST or t < LAST
    if a + b == "NY":
        return s == LAST and t < LAST
    return a + b in ("TT", "XY")


def cross(stack, held, inner, parts, refs, stack_ref, col_ref, best_ref):
    at = {}
    size = 0
    for n in stack:
        at[n] = size
        stack_ref[size:size + length(parts[n]), :] = refs[n][0:length(parts[n]), :]
        size += length(parts[n])
    col_ref[...] = column(jnp.concatenate([cluster_line(refs[n], parts[n]) for n in stack], axis=1))
    best_ref[...] = jnp.full((size, 128), -1.0, F32)
    lines = {}
    for k in held + (stack if inner else []):
        near = [n for n in stack if needed(n, k)]
        low = min(at[n] for n in near)
        high = max(at[n] + length(parts[n]) for n in near)
        n_k = length(parts[k])
        sims = dot_nt(stack_ref[low:high, :], refs[k][0:n_k, :])
        keep = wide(col_ref[low:high, :], n_k) == cluster_line(refs[k], parts[k])
        if k in stack:
            keep = keep & (iota((high - low, n_k), 0) + (low - at[k]) != iota((high - low, n_k), 1))
        sims = jnp.where(keep, sims, -1.0)
        best = best_ref[low:high, :]
        for v in range(n_k // 128):
            best = jnp.maximum(best, sims[:, v * 128:(v + 1) * 128])
        best_ref[low:high, :] = best
        if k not in stack:
            lines[k] = jnp.max(sims, axis=0, keepdims=True)
    for n in stack:
        lines[n] = lined(best_ref[at[n]:at[n] + length(parts[n]), :])
    return lines


def product_kernel(stack, held, inner, parts, *refs):
    names = stack + held
    refs = list(refs)
    rows = {n: refs.pop(0) for n in names}
    outs = {n: refs.pop(0) for n in names}
    for n, line in cross(stack, held, inner, parts, rows, *refs).items():
        outs[n][...] = line


def lined(best):
    rows = best.shape[0]
    parts = [jnp.max(best[b * 128:(b + 1) * 128, :].T, axis=0, keepdims=True) for b in range(rows // 128)]
    return jnp.concatenate(parts, axis=1)


def final_kernel(dims, kinds, stack, held, parts, known, *refs):
    n_gx, n_gy, rows, quota = dims
    chunk = n_gy * quota
    refs = list(refs)
    row_refs = {n: refs.pop(0) for n in stack + held}
    lines = {}
    for n in known:
        line = refs.pop(0)[...]
        lines[n] = jnp.maximum(lines[n], line) if n in lines else line
    send_ref = refs.pop(0)
    for n, line in cross(stack, held, True, parts, row_refs, *refs).items():
        lines[n] = jnp.maximum(lines[n], line) if n in lines else line
    whole = {}
    for n in sorted(lines):
        at = 0
        for k, first, count in parts[n]:
            whole.setdefault((n[:-1], k), {})[first] = lines[n][:, at:at + count]
            at += count
    blocks = [jnp.full((n_gy, 128), -1.0, F32)] * len(kinds)
    own = lax.shift_right_logical(iota((n_gy, chunk), 1), log2(quota)) == iota((n_gy, chunk), 0)
    lane = lax.shift_right_logical(iota((n_gy, 128), 1), log2(quota))
    for (kind, k), found in sorted(whole.items()):
        line = jnp.concatenate([found[first] for first in sorted(found)], axis=1)
        held_here = jnp.where(own, line, 0.0)
        fold = held_here[:, 0:128]
        for v in range(1, chunk // 128):
            fold = fold + held_here[:, v * 128:(v + 1) * 128]
        shift = 64
        while shift >= quota:
            fold = fold + pltpu.roll(fold, shift, 1)
            shift //= 2
        at = kinds.index(kind)
        blocks[at] = jnp.where(lane == k, fold, blocks[at])
    everything = jnp.concatenate(blocks, axis=1)
    for d in range(n_gy):
        send_ref[d] = everything[d:d + 1, :]


def far_place(q, m):
    row = q // KEYS
    return q ^ (KEYS * m) ^ (1 if row < row ^ m else 0)


def finish_kernel(dims, home_ref, back_ref, out_ref):
    n_gx, n_gy, rows, quota = dims
    n_query = n_gy // KEYS

    def taken(place, block):
        return jnp.concatenate([back_ref[place(q)][:, block * 128:(block + 1) * 128] for q in range(n_gy)], axis=0)

    found = taken(lambda q: q, 0)
    for m in range(1, n_query):
        found = jnp.maximum(found, taken(lambda q, m=m: far_place(q, m), m))
    for t in (1, 2):
        found = jnp.maximum(found, taken(lambda q, t=t: q ^ t, n_query - 1 + t))
    high = found.astype(BF16)
    rest = found - high.astype(F32)
    mid = rest.astype(BF16)
    low = (rest - mid.astype(F32)).astype(BF16)
    here = one_hot(iota((128, rows), 0) == home_ref[1:2, :])
    value = dot_nn(jnp.concatenate([high.astype(F32), mid.astype(F32), low.astype(F32)], axis=0).astype(BF16), here)
    value = (value[0:n_gy] + value[n_gy:2 * n_gy]) + value[2 * n_gy:3 * n_gy]
    own = iota((n_gy, rows), 0) == home_ref[0:1, :]
    out_ref[...] = jnp.sum(jnp.where(own, value, 0.0), axis=0, keepdims=True)


def shape(dims, dtype):
    return jax.ShapeDtypeStruct(dims, dtype)


def per_device(embeddings, members, sizes):
    rows = members.shape[0]
    width = embeddings.shape[1]
    n_gx = lax.axis_size("gx")
    n_gy = lax.axis_size("gy")
    owners = n_gx * n_gy
    quota = rows // owners
    chunk = n_gy * quota
    n_query = n_gy // KEYS
    dims = (n_gx, n_gy, rows, quota)
    in_vmem = pl.BlockSpec(memory_space=pltpu.VMEM)

    in_hbm = pl.BlockSpec(memory_space=pltpu.HBM)
    asked, home = pl.pallas_call(
        functools.partial(request_kernel, dims),
        out_shape=(shape((owners, 1, quota), I32), shape((2, rows), I32)),
        in_specs=[in_hbm, in_hbm],
        out_specs=(in_vmem, in_vmem),
        scratch_shapes=[
            pltpu.SMEM(sizes.shape, I32),
            pltpu.VMEM((1, rows), I32),
            pltpu.SemaphoreType.DMA((2,)),
        ],
        compiler_params=params(56 * 1024 * 1024),
        name="request",
    )(sizes, members.reshape(1, rows))
    asked = lax.all_to_all(asked, ("gx", "gy"), split_axis=0, concat_axis=0, tiled=True)

    values = embeddings.astype(F32)
    squared = jnp.sum(values * values, axis=1, keepdims=True)
    unit = (values * lax.rsqrt(squared + 1e-06)).astype(BF16)

    full = [(k, 0, chunk) for k in range(n_gx)]
    if n_gx == 4:
        rest = [[(2, 0, chunk // 2)], [(2, chunk // 2, chunk // 2)]]
    else:
        rest = [full[2:-3], full[-3:-1]]
    stages = [[full[0]], [full[1]], [full[-1]]] + rest
    far = ["Y%d" % m for m in range(1, n_query)]
    parts = {kind + str(s): stage for s, stage in enumerate(stages) for kind in ["T", "N", "X"] + far}
    piece = {}
    lines = []

    def meet(*arrays):
        return lax.optimization_barrier(arrays)

    found = {}
    for wanted in [stages[1], stages[0], stages[2] + stages[3] + stages[4]]:
        out = pl.pallas_call(
            functools.partial(select_kernel, dims, wanted),
            out_shape=[shape((count + (SPARE if k else 1), width), BF16) for k, _, count in wanted],
            in_specs=[in_vmem, in_vmem],
            out_specs=[in_vmem] * len(wanted),
            cost_estimate=cost(2 * len(wanted) * chunk * rows * width, rows * width),
            compiler_params=params(),
            name="select",
        )(asked, unit)
        unit, *out = meet(unit, *out)
        found.update(zip(wanted, out))

    def across(part):
        step = part[0]
        return lax.ppermute(found[part], "gx", [(i, (i + step) % n_gx) for i in range(n_gx)])

    def swap(array, mask):
        return lax.ppermute(array, "gy", [(i, i ^ mask) for i in range(n_gy)])

    def pack(arrays, groups):
        out_parts = sum(groups, [])
        return pl.pallas_call(
            functools.partial(pack_kernel, [groups]),
            out_shape=shape((length(out_parts) + len(out_parts), width), BF16),
            in_specs=[in_vmem] * len(arrays),
            out_specs=in_vmem,
            cost_estimate=cost(0, 4 * length(out_parts) * width),
            compiler_params=params(),
            name="pack",
        )(*arrays)

    def land(s, arrays):
        name = "T" + str(s)
        piece[name] = pack(arrays, [[part] for part in stages[s]])
        return name

    def near(s):
        own = piece["T" + str(s)]
        piece["X" + str(s)] = swap(own, 2)
        for m, kind in enumerate(far):
            piece[kind + str(s)] = lax.ppermute(own, "gy", [(q, far_place(q, m + 1)) for q in range(n_gy)])

    def join(names, arrays):
        out = list(meet(*[piece[n] for n in names], *arrays, *[line for _, line in lines]))
        for n in names:
            piece[n] = out.pop(0)
        arrays = [out.pop(0) for _ in arrays]
        lines[:] = [(n, out.pop(0)) for n, _ in lines]
        return arrays

    def scratch(stack):
        rows_in = sum(length(parts[n]) for n in stack)
        return [pltpu.VMEM((rows_in, width), BF16), pltpu.VMEM((rows_in, 128), F32), pltpu.VMEM((rows_in, 128), F32)]

    def products(stack, held, inner=True, weight=0.0):
        names = stack + held
        flops = 2 * width * sum(length(parts[n]) for n in stack) * sum(length(parts[n]) for n in names)
        out = pl.pallas_call(
            functools.partial(product_kernel, stack, held, inner, parts),
            out_shape=[shape((1, length(parts[n])), F32) for n in names],
            in_specs=[in_vmem] * len(names),
            out_specs=[in_vmem] * len(names),
            scratch_shapes=scratch(stack),
            cost_estimate=cost(int(weight * flops), 0),
            compiler_params=params(),
            name="products",
        )(*[piece[n] for n in names])
        lines.extend(zip(names, out))

    def kinds(letters, *numbers):
        out = []
        for n in numbers:
            for letter in letters:
                out += [kind + str(n) for kind in (far if letter == "Y" else [letter])]
        return out

    z1 = [across(part) for part in stages[1]]
    z2 = [across(part) for part in stages[2]]
    piece["T0"] = found[full[0]]
    near(0)
    piece["N0"] = swap(piece["T0"], 1)
    late = stages[3] + stages[4]
    *z1, = join(kinds("TNXY", 0), z1 + [found[part] for part in late])
    for part, array in zip(late, z1[1:]):
        found[part] = array
    z3 = [across(part) for part in stages[3]]
    z4 = [across(part) for part in stages[4]]
    land(1, z1[:1])
    near(1)
    piece["N1"] = swap(piece["T1"], 1)
    products(kinds("NY", 0) + ["T0", "T1", "X0"], [])
    z2 = join(kinds("TNXY", 1), z2)
    land(2, z2)
    near(2)
    products(kinds("NY", 1) + ["T2", "X1"], kinds("TNXY", 0) + ["T1"])
    z3 = join([], z3)
    land(3, z3)
    near(3)
    products(["T3"], kinds("TNXY", 0, 1) + ["T2"])
    products(kinds("YX", 2), kinds("TNXY", 0, 1) + ["T2", "T3"])
    z4 = join(["T2", "T3"], z4)
    land(4, z4)
    near(4)
    group = ["T2", "T3", "T4"]
    both = swap(pack([piece[n] for n in group], [parts[n] for n in group]), 1)
    cores = ["N2", "N3", "N4"]
    out = pl.pallas_call(
        functools.partial(split_kernel, [parts[n] for n in cores]),
        out_shape=[shape((length(parts[n]) + len(parts[n]), width), BF16) for n in cores],
        in_specs=[in_vmem],
        out_specs=[in_vmem] * len(cores),
        cost_estimate=cost(0, 0),
        compiler_params=params(),
        name="split",
    )(both)
    piece.update(zip(cores, out))
    products(kinds("Y", 3) + ["T4", "X3"], kinds("TNXY", 0, 1) + kinds("TXY", 2) + ["T3"], weight=WEIGHT)
    products(cores, kinds("XY", 0, 1, 2, 3) + ["T2", "T3", "T4"], inner=False)
    join(kinds("TNXY", 4), [])
    stack = kinds("YX", 4)
    held = kinds("XY", 0, 1, 2, 3) + ["T4", "N4"]
    shown = ["T"] + far + ["N", "X"]
    names = stack + held
    send = pl.pallas_call(
        functools.partial(final_kernel, dims, shown, stack, held, parts, [n for n, _ in lines]),
        out_shape=shape((n_gy, 1, len(shown) * 128), F32),
        in_specs=[in_vmem] * (len(names) + len(lines)),
        out_specs=in_vmem,
        scratch_shapes=scratch(stack),
        cost_estimate=cost(2 * width * chunk * 8 * chunk, 0),
        compiler_params=params(),
        name="final",
    )(*[piece[n] for n in names], *[line for _, line in lines])

    back = lax.all_to_all(send, "gy", split_axis=0, concat_axis=0, tiled=True)
    out = pl.pallas_call(
        functools.partial(finish_kernel, dims),
        out_shape=shape((1, rows), F32),
        in_specs=[in_vmem, in_vmem],
        out_specs=in_vmem,
        compiler_params=params(),
        name="finish",
    )(home, back)
    return out.reshape(rows)


def solution(mesh):
    return jax.shard_map(
        per_device,
        mesh=mesh,
        in_specs=(P(("gx", "gy"), None), P(("gx", "gy")), P("gx", None)),
        out_specs=P(("gx", "gy")),
        check_vma=False,
    )
```

```python
import functools

import jax
import jax.numpy as jnp
from jax import lax
from jax.experimental import pallas as pl
from jax.experimental.pallas import tpu as pltpu
from jax.sharding import PartitionSpec as P

F32 = jnp.float32
BF16 = jnp.bfloat16
I32 = jnp.int32
SPARE = 8
KEYS = 4
VMEM = 24 * 1024 * 1024
LAST = 4
WEIGHT = 20.0


def iota(shape, dim):
    return lax.broadcasted_iota(I32, shape, dim)


def dot_nt(a, b):
    return lax.dot_general(a, b, (((1,), (1,)), ((), ())), preferred_element_type=F32)


def dot_nn(a, b):
    return lax.dot_general(a, b, (((1,), (0,)), ((), ())), preferred_element_type=F32)


def one_hot(mask):
    return jnp.where(mask, 1.0, 0.0).astype(BF16)


def log2(value):
    assert value & (value - 1) == 0
    return value.bit_length() - 1


def params(limit=VMEM):
    return pltpu.CompilerParams(vmem_limit_bytes=limit)


def cost(flops, size):
    return pl.CostEstimate(flops=flops, bytes_accessed=size, transcendentals=0)


def request_kernel(dims, sizes_hbm, members_hbm, asked_ref, home_ref, sizes_ref, members_ref, sems):
    n_gx, n_gy, rows, quota = dims
    copies = [
        pltpu.make_async_copy(members_hbm, members_ref, sems.at[0]),
        pltpu.make_async_copy(sizes_hbm, sizes_ref, sems.at[1]),
    ]
    for copy in copies:
        copy.start()
    for copy in copies:
        copy.wait()
    owners = n_gx * n_gy
    member = members_ref[...]
    owner = lax.shift_right_logical(member, log2(rows))
    row = member & (rows - 1)
    slot = lax.axis_index("gy") * rows + iota((1, rows), 1)
    cluster = jnp.zeros((1, rows), I32)
    end = jnp.int32(0)
    for c in range(sizes_ref.shape[1]):
        end = end + sizes_ref[0, c]
        cluster = cluster + (slot >= end).astype(I32)
    mask = iota((owners, rows), 0) == owner
    hot = one_hot(mask)
    before = one_hot(iota((128, 128), 0) < iota((128, 128), 1))
    count = jnp.zeros((owners, 1), F32)
    ranks = []
    parts = [hot[:, b * 128:(b + 1) * 128] for b in range(rows // 128)]
    inner = dot_nn(jnp.concatenate(parts, axis=0), before)
    for b, part in enumerate(parts):
        rank = inner[b * owners:(b + 1) * owners, :] + count
        part32 = part.astype(F32)
        ranks.append(jnp.sum(part32 * rank, axis=0, keepdims=True))
        count = count + jnp.sum(part32, axis=1, keepdims=True)
    rank = jnp.concatenate(ranks, axis=1).astype(I32)
    place = one_hot(iota((quota, rows), 0) == rank)
    low = (row & 255).astype(F32)
    high = lax.shift_right_logical(row, 8).astype(F32)
    zero = jnp.zeros((owners, rows), F32)

    values = [jnp.where(mask, v, zero).astype(BF16) for v in (low, high, cluster.astype(F32))]
    picked = dot_nt(jnp.concatenate(values, axis=0), place)
    low, high, held = (picked[i * owners:(i + 1) * owners, :] for i in range(3))
    asked = (low + 256.0 * high + float(rows) * held).astype(I32)
    for o in range(owners):
        asked_ref[o] = asked[o:o + 1, :]
    plane = lax.shift_right_logical(owner, log2(n_gy))
    step = (lax.axis_index("gx") - plane) & (n_gx - 1)
    home_ref[0:1, :] = owner & (n_gy - 1)
    home_ref[1:2, :] = step * quota + rank


def select_kernel(dims, parts, asked_ref, unit_ref, *out_refs):
    n_gx, n_gy, rows, quota = dims
    chunk = n_gy * quota
    pick = one_hot((iota((chunk, quota), 0) & (quota - 1)) == iota((chunk, quota), 1))
    block = lax.shift_right_logical(iota((chunk, n_gy), 0), log2(quota))
    own_col = block == iota((chunk, n_gy), 1)
    block_row = lax.shift_right_logical(iota((n_gy, chunk), 1), log2(quota))
    own_row = block_row == iota((n_gy, chunk), 0)
    refs = list(out_refs)
    width = unit_ref.shape[1]
    for step in sorted({k for k, _, _ in parts}):
        plane = (lax.axis_index("gx") + step) & (n_gx - 1)
        wanted = jnp.concatenate([asked_ref[plane * n_gy + d] for d in range(n_gy)], axis=0)
        row = wanted & (rows - 1)
        cluster = lax.shift_right_logical(wanted, log2(rows)).astype(F32).astype(BF16)
        low = (row & 255).astype(F32).astype(BF16)
        high = lax.shift_right_logical(row, 8).astype(F32).astype(BF16)
        index = dot_nt(pick, low) + 256.0 * dot_nt(pick, high)
        index = jnp.sum(jnp.where(own_col, index, 0.0), axis=1, keepdims=True).astype(I32)
        flat = jnp.sum(jnp.where(own_row, dot_nt(cluster, pick), 0.0), axis=0, keepdims=True)
        hot = one_hot(iota((chunk, rows), 1) == index)
        found = dot_nn(hot, unit_ref[...]).astype(BF16)
        for ref, (k, first, count) in zip(out_refs, parts):
            if k == step:
                ref[0:count, :] = found[first:first + count, :]
                line = [flat[:, first:first + count], jnp.zeros((1, width - count), F32)]
                ref[count:count + 1, :] = jnp.concatenate(line, axis=1).astype(BF16)


def column(line):
    parts = []
    for b in range(line.shape[1] // 128):
        wide = jnp.broadcast_to(line[:, b * 128:(b + 1) * 128], (128, 128))
        parts.append(wide.T)
    return jnp.concatenate(parts, axis=0)


def wide(col, lanes):
    return jnp.concatenate([col] * (lanes // 128), axis=1)


def length(parts):
    return sum(count for _, _, count in parts)


def cluster_line(ref, parts):
    size = length(parts)
    block = ref[size:size + len(parts), :].astype(F32)
    return jnp.concatenate([block[r:r + 1, 0:part[2]] for r, part in enumerate(parts)], axis=1)


def pack_kernel(groups, *refs):
    refs = list(refs)
    outs = refs[sum(len(g) for g in groups):]
    for group, out_ref in zip(groups, outs):
        at = 0
        total = sum(length(parts) for parts in group)
        width = out_ref.shape[1]
        lines = []
        for parts in group:
            ref, size = refs.pop(0), length(parts)
            out_ref[at:at + size, :] = ref[0:size, :]
            lines.append(ref[size:size + len(parts), :].astype(F32))
            at += size
        count = sum(len(parts) for parts in group)
        out_ref[total:total + count, :] = jnp.concatenate(lines, axis=0).astype(BF16)


def split_kernel(pieces, ref, *outs):
    total = sum(length(parts) for parts in pieces)
    at = 0
    row = total
    for parts, out_ref in zip(pieces, outs):
        size = length(parts)
        out_ref[0:size, :] = ref[at:at + size, :]
        out_ref[size:size + len(parts), :] = ref[row:row + len(parts), :]
        at += size
        row += len(parts)


def needed(one, two):
    (a, s), (b, t) = sorted([(n[0], int(n[-1])) for n in (one, two)], key=lambda n: "TNXY".index(n[0]))
    if a + b in ("TN", "TX"):
        return s >= t
    if a + b == "NX":
        return s == t or s < t < LAST or s == LAST
    if a + b == "TY":
        return s == LAST or t < LAST
    if a + b == "NY":
        return s == LAST and t < LAST
    return a + b in ("TT", "XY")


def cross(stack, held, inner, parts, refs, stack_ref, col_ref, best_ref):
    at = {}
    size = 0
    for n in stack:
        at[n] = size
        stack_ref[size:size + length(parts[n]), :] = refs[n][0:length(parts[n]), :]
        size += length(parts[n])
    col_ref[...] = column(jnp.concatenate([cluster_line(refs[n], parts[n]) for n in stack], axis=1))
    best_ref[...] = jnp.full((size, 128), -1.0, F32)
    lines = {}
    for k in held + (stack if inner else []):
        near = [n for n in stack if needed(n, k)]
        low = min(at[n] for n in near)
        high = max(at[n] + length(parts[n]) for n in near)
        n_k = length(parts[k])
        sims = dot_nt(stack_ref[low:high, :], refs[k][0:n_k, :])
        keep = wide(col_ref[low:high, :], n_k) == cluster_line(refs[k], parts[k])
        if k in stack:
            keep = keep & (iota((high - low, n_k), 0) + (low - at[k]) != iota((high - low, n_k), 1))
        sims = jnp.where(keep, sims, -1.0)
        best = best_ref[low:high, :]
        for v in range(n_k // 128):
            best = jnp.maximum(best, sims[:, v * 128:(v + 1) * 128])
        best_ref[low:high, :] = best
        if k not in stack:
            lines[k] = jnp.max(sims, axis=0, keepdims=True)
    for n in stack:
        lines[n] = lined(best_ref[at[n]:at[n] + length(parts[n]), :])
    return lines


def product_kernel(stack, held, inner, parts, *refs):
    names = stack + held
    refs = list(refs)
    rows = {n: refs.pop(0) for n in names}
    outs = {n: refs.pop(0) for n in names}
    for n, line in cross(stack, held, inner, parts, rows, *refs).items():
        outs[n][...] = line


def lined(best):
    rows = best.shape[0]
    parts = [jnp.max(best[b * 128:(b + 1) * 128, :].T, axis=0, keepdims=True) for b in range(rows // 128)]
    return jnp.concatenate(parts, axis=1)


def final_kernel(dims, kinds, stack, held, parts, known, *refs):
    n_gx, n_gy, rows, quota = dims
    chunk = n_gy * quota
    refs = list(refs)
    row_refs = {n: refs.pop(0) for n in stack + held}
    lines = {}
    for n in known:
        line = refs.pop(0)[...]
        lines[n] = jnp.maximum(lines[n], line) if n in lines else line
    send_ref = refs.pop(0)
    for n, line in cross(stack, held, True, parts, row_refs, *refs).items():
        lines[n] = jnp.maximum(lines[n], line) if n in lines else line
    whole = {}
    for n in sorted(lines):
        at = 0
        for k, first, count in parts[n]:
            whole.setdefault((n[:-1], k), {})[first] = lines[n][:, at:at + count]
            at += count
    blocks = [jnp.full((n_gy, 128), -1.0, F32)] * len(kinds)
    own = lax.shift_right_logical(iota((n_gy, chunk), 1), log2(quota)) == iota((n_gy, chunk), 0)
    lane = lax.shift_right_logical(iota((n_gy, 128), 1), log2(quota))
    for (kind, k), found in sorted(whole.items()):
        line = jnp.concatenate([found[first] for first in sorted(found)], axis=1)
        held_here = jnp.where(own, line, 0.0)
        fold = held_here[:, 0:128]
        for v in range(1, chunk // 128):
            fold = fold + held_here[:, v * 128:(v + 1) * 128]
        shift = 64
        while shift >= quota:
            fold = fold + pltpu.roll(fold, shift, 1)
            shift //= 2
        at = kinds.index(kind)
        blocks[at] = jnp.where(lane == k, fold, blocks[at])
    everything = jnp.concatenate(blocks, axis=1)
    for d in range(n_gy):
        send_ref[d] = everything[d:d + 1, :]


def far_place(q, m):
    row = q // KEYS
    return q ^ (KEYS * m) ^ (1 if row < row ^ m else 0)


def finish_kernel(dims, home_ref, back_ref, out_ref):
    n_gx, n_gy, rows, quota = dims
    n_query = n_gy // KEYS

    def taken(place, block):
        return jnp.concatenate([back_ref[place(q)][:, block * 128:(block + 1) * 128] for q in range(n_gy)], axis=0)

    found = taken(lambda q: q, 0)
    for m in range(1, n_query):
        found = jnp.maximum(found, taken(lambda q, m=m: far_place(q, m), m))
    for t in (1, 2):
        found = jnp.maximum(found, taken(lambda q, t=t: q ^ t, n_query - 1 + t))
    high = found.astype(BF16)
    rest = found - high.astype(F32)
    mid = rest.astype(BF16)
    low = (rest - mid.astype(F32)).astype(BF16)
    here = one_hot(iota((128, rows), 0) == home_ref[1:2, :])
    value = dot_nn(jnp.concatenate([high.astype(F32), mid.astype(F32), low.astype(F32)], axis=0).astype(BF16), here)
    value = (value[0:n_gy] + value[n_gy:2 * n_gy]) + value[2 * n_gy:3 * n_gy]
    own = iota((n_gy, rows), 0) == home_ref[0:1, :]
    out_ref[...] = jnp.sum(jnp.where(own, value, 0.0), axis=0, keepdims=True)


def shape(dims, dtype):
    return jax.ShapeDtypeStruct(dims, dtype)


def per_device(embeddings, members, sizes):
    rows = members.shape[0]
    width = embeddings.shape[1]
    n_gx = lax.axis_size("gx")
    n_gy = lax.axis_size("gy")
    owners = n_gx * n_gy
    quota = rows // owners
    chunk = n_gy * quota
    n_query = n_gy // KEYS
    dims = (n_gx, n_gy, rows, quota)
    in_vmem = pl.BlockSpec(memory_space=pltpu.VMEM)

    in_hbm = pl.BlockSpec(memory_space=pltpu.HBM)
    asked, home = pl.pallas_call(
        functools.partial(request_kernel, dims),
        out_shape=(shape((owners, 1, quota), I32), shape((2, rows), I32)),
        in_specs=[in_hbm, in_hbm],
        out_specs=(in_vmem, in_vmem),
        scratch_shapes=[
            pltpu.SMEM(sizes.shape, I32),
            pltpu.VMEM((1, rows), I32),
            pltpu.SemaphoreType.DMA((2,)),
        ],
        compiler_params=params(56 * 1024 * 1024),
        name="request",
    )(sizes, members.reshape(1, rows))
    asked = lax.all_to_all(asked, ("gx", "gy"), split_axis=0, concat_axis=0, tiled=True)

    values = embeddings.astype(F32)
    squared = jnp.sum(values * values, axis=1, keepdims=True)
    unit = (values * lax.rsqrt(squared + 1e-06)).astype(BF16)

    full = [(k, 0, chunk) for k in range(n_gx)]
    if n_gx == 4:
        rest = [[(2, 0, chunk // 2)], [(2, chunk // 2, chunk // 2)]]
    else:
        rest = [full[2:-3], full[-3:-1]]
    stages = [[full[0]], [full[1]], [full[-1]]] + rest
    far = ["Y%d" % m for m in range(1, n_query)]
    parts = {kind + str(s): stage for s, stage in enumerate(stages) for kind in ["T", "N", "X"] + far}
    piece = {}
    lines = []

    def meet(*arrays):
        return lax.optimization_barrier(arrays)

    found = {}
    for wanted in [stages[1], stages[0], stages[2] + stages[3] + stages[4]]:
        out = pl.pallas_call(
            functools.partial(select_kernel, dims, wanted),
            out_shape=[shape((count + (SPARE if k else 1), width), BF16) for k, _, count in wanted],
            in_specs=[in_vmem, in_vmem],
            out_specs=[in_vmem] * len(wanted),
            cost_estimate=cost(2 * len(wanted) * chunk * rows * width, rows * width),
            compiler_params=params(),
            name="select",
        )(asked, unit)
        unit, *out = meet(unit, *out)
        found.update(zip(wanted, out))

    def across(part):
        step = part[0]
        return lax.ppermute(found[part], "gx", [(i, (i + step) % n_gx) for i in range(n_gx)])

    def swap(array, mask):
        return lax.ppermute(array, "gy", [(i, i ^ mask) for i in range(n_gy)])

    def pack(arrays, groups):
        out_parts = sum(groups, [])
        return pl.pallas_call(
            functools.partial(pack_kernel, [groups]),
            out_shape=shape((length(out_parts) + len(out_parts), width), BF16),
            in_specs=[in_vmem] * len(arrays),
            out_specs=in_vmem,
            cost_estimate=cost(0, 4 * length(out_parts) * width),
            compiler_params=params(),
            name="pack",
        )(*arrays)

    def land(s, arrays):
        name = "T" + str(s)
        piece[name] = pack(arrays, [[part] for part in stages[s]])
        return name

    def near(s):
        own = piece["T" + str(s)]
        piece["X" + str(s)] = swap(own, 2)
        for m, kind in enumerate(far):
            piece[kind + str(s)] = lax.ppermute(own, "gy", [(q, far_place(q, m + 1)) for q in range(n_gy)])

    def join(names, arrays):
        out = list(meet(*[piece[n] for n in names], *arrays, *[line for _, line in lines]))
        for n in names:
            piece[n] = out.pop(0)
        arrays = [out.pop(0) for _ in arrays]
        lines[:] = [(n, out.pop(0)) for n, _ in lines]
        return arrays

    def scratch(stack):
        rows_in = sum(length(parts[n]) for n in stack)
        return [pltpu.VMEM((rows_in, width), BF16), pltpu.VMEM((rows_in, 128), F32), pltpu.VMEM((rows_in, 128), F32)]

    def products(stack, held, inner=True, weight=0.0):
        names = stack + held
        flops = 2 * width * sum(length(parts[n]) for n in stack) * sum(length(parts[n]) for n in names)
        out = pl.pallas_call(
            functools.partial(product_kernel, stack, held, inner, parts),
            out_shape=[shape((1, length(parts[n])), F32) for n in names],
            in_specs=[in_vmem] * len(names),
            out_specs=[in_vmem] * len(names),
            scratch_shapes=scratch(stack),
            cost_estimate=cost(int(weight * flops), 0),
            compiler_params=params(),
            name="products",
        )(*[piece[n] for n in names])
        lines.extend(zip(names, out))

    def kinds(letters, *numbers):
        out = []
        for n in numbers:
            for letter in letters:
                out += [kind + str(n) for kind in (far if letter == "Y" else [letter])]
        return out

    z1 = [across(part) for part in stages[1]]
    z2 = [across(part) for part in stages[2]]
    piece["T0"] = found[full[0]]
    near(0)
    piece["N0"] = swap(piece["T0"], 1)
    late = stages[3] + stages[4]
    *z1, = join(kinds("TNXY", 0), z1 + [found[part] for part in late])
    for part, array in zip(late, z1[1:]):
        found[part] = array
    z3 = [across(part) for part in stages[3]]
    z4 = [across(part) for part in stages[4]]
    land(1, z1[:1])
    near(1)
    piece["N1"] = swap(piece["T1"], 1)
    products(kinds("NY", 0) + ["T0", "T1", "X0"], [])
    z2 = join(kinds("TN", 1), z2)
    land(2, z2)
    near(2)
    products(kinds("NY", 1) + ["T2", "X1"], kinds("TNXY", 0) + ["T1"])
    z3 = join([], z3)
    land(3, z3)
    near(3)
    products(["T3"], kinds("TNXY", 0, 1) + ["T2"])
    products(kinds("YX", 2), kinds("TNXY", 0, 1) + ["T2", "T3"])
    z4 = join(["T2", "T3"], z4)
    land(4, z4)
    near(4)
    group = ["T2", "T3", "T4"]
    both = swap(pack([piece[n] for n in group], [parts[n] for n in group]), 1)
    cores = ["N2", "N3", "N4"]
    out = pl.pallas_call(
        functools.partial(split_kernel, [parts[n] for n in cores]),
        out_shape=[shape((length(parts[n]) + len(parts[n]), width), BF16) for n in cores],
        in_specs=[in_vmem],
        out_specs=[in_vmem] * len(cores),
        cost_estimate=cost(0, 0),
        compiler_params=params(),
        name="split",
    )(both)
    piece.update(zip(cores, out))
    products(kinds("Y", 3) + ["T4", "X3"], kinds("TNXY", 0, 1) + kinds("TXY", 2) + ["T3"], weight=WEIGHT)
    products(cores, kinds("XY", 0, 1, 2, 3) + ["T2", "T3", "T4"], inner=False)
    join(kinds("TNXY", 4), [])
    stack = kinds("YX", 4)
    held = kinds("XY", 0, 1, 2, 3) + ["T4", "N4"]
    shown = ["T"] + far + ["N", "X"]
    names = stack + held
    send = pl.pallas_call(
        functools.partial(final_kernel, dims, shown, stack, held, parts, [n for n, _ in lines]),
        out_shape=shape((n_gy, 1, len(shown) * 128), F32),
        in_specs=[in_vmem] * (len(names) + len(lines)),
        out_specs=in_vmem,
        scratch_shapes=scratch(stack),
        cost_estimate=cost(2 * width * chunk * 8 * chunk, 0),
        compiler_params=params(),
        name="final",
    )(*[piece[n] for n in names], *[line for _, line in lines])

    back = lax.all_to_all(send, "gy", split_axis=0, concat_axis=0, tiled=True)
    out = pl.pallas_call(
        functools.partial(finish_kernel, dims),
        out_shape=shape((1, rows), F32),
        in_specs=[in_vmem, in_vmem],
        out_specs=in_vmem,
        compiler_params=params(),
        name="finish",
    )(home, back)
    return out.reshape(rows)


def solution(mesh):
    return jax.shard_map(
        per_device,
        mesh=mesh,
        in_specs=(P(("gx", "gy"), None), P(("gx", "gy")), P("gx", None)),
        out_specs=P(("gx", "gy")),
        check_vma=False,
    )
```

```python
import functools

import jax
import jax.numpy as jnp
from jax import lax
from jax.experimental import pallas as pl
from jax.experimental.pallas import tpu as pltpu
from jax.sharding import PartitionSpec as P

F32 = jnp.float32
BF16 = jnp.bfloat16
I32 = jnp.int32
SPARE = 8
KEYS = 4
VMEM = 24 * 1024 * 1024
LAST = 4
WEIGHT = 20.0


def iota(shape, dim):
    return lax.broadcasted_iota(I32, shape, dim)


def dot_nt(a, b):
    return lax.dot_general(a, b, (((1,), (1,)), ((), ())), preferred_element_type=F32)


def dot_nn(a, b):
    return lax.dot_general(a, b, (((1,), (0,)), ((), ())), preferred_element_type=F32)


def one_hot(mask):
    return jnp.where(mask, 1.0, 0.0).astype(BF16)


def log2(value):
    assert value & (value - 1) == 0
    return value.bit_length() - 1


def params(limit=VMEM):
    return pltpu.CompilerParams(vmem_limit_bytes=limit)


def cost(flops, size):
    return pl.CostEstimate(flops=flops, bytes_accessed=size, transcendentals=0)


def request_kernel(dims, sizes_hbm, members_hbm, asked_ref, home_ref, sizes_ref, members_ref, sems):
    n_gx, n_gy, rows, quota = dims
    copies = [
        pltpu.make_async_copy(members_hbm, members_ref, sems.at[0]),
        pltpu.make_async_copy(sizes_hbm, sizes_ref, sems.at[1]),
    ]
    for copy in copies:
        copy.start()
    for copy in copies:
        copy.wait()
    owners = n_gx * n_gy
    member = members_ref[...]
    owner = lax.shift_right_logical(member, log2(rows))
    row = member & (rows - 1)
    slot = lax.axis_index("gy") * rows + iota((1, rows), 1)
    cluster = jnp.zeros((1, rows), I32)
    end = jnp.int32(0)
    for c in range(sizes_ref.shape[1]):
        end = end + sizes_ref[0, c]
        cluster = cluster + (slot >= end).astype(I32)
    mask = iota((owners, rows), 0) == owner
    hot = one_hot(mask)
    before = one_hot(iota((128, 128), 0) < iota((128, 128), 1))
    count = jnp.zeros((owners, 1), F32)
    ranks = []
    parts = [hot[:, b * 128:(b + 1) * 128] for b in range(rows // 128)]
    inner = dot_nn(jnp.concatenate(parts, axis=0), before)
    for b, part in enumerate(parts):
        rank = inner[b * owners:(b + 1) * owners, :] + count
        part32 = part.astype(F32)
        ranks.append(jnp.sum(part32 * rank, axis=0, keepdims=True))
        count = count + jnp.sum(part32, axis=1, keepdims=True)
    rank = jnp.concatenate(ranks, axis=1).astype(I32)
    place = one_hot(iota((quota, rows), 0) == rank)
    low = (row & 255).astype(F32)
    high = lax.shift_right_logical(row, 8).astype(F32)
    zero = jnp.zeros((owners, rows), F32)

    values = [jnp.where(mask, v, zero).astype(BF16) for v in (low, high, cluster.astype(F32))]
    picked = dot_nt(jnp.concatenate(values, axis=0), place)
    low, high, held = (picked[i * owners:(i + 1) * owners, :] for i in range(3))
    asked = (low + 256.0 * high + float(rows) * held).astype(I32)
    for o in range(owners):
        asked_ref[o] = asked[o:o + 1, :]
    plane = lax.shift_right_logical(owner, log2(n_gy))
    step = (lax.axis_index("gx") - plane) & (n_gx - 1)
    home_ref[0:1, :] = owner & (n_gy - 1)
    home_ref[1:2, :] = step * quota + rank


def select_kernel(dims, parts, asked_ref, unit_ref, *out_refs):
    n_gx, n_gy, rows, quota = dims
    chunk = n_gy * quota
    pick = one_hot((iota((chunk, quota), 0) & (quota - 1)) == iota((chunk, quota), 1))
    block = lax.shift_right_logical(iota((chunk, n_gy), 0), log2(quota))
    own_col = block == iota((chunk, n_gy), 1)
    block_row = lax.shift_right_logical(iota((n_gy, chunk), 1), log2(quota))
    own_row = block_row == iota((n_gy, chunk), 0)
    refs = list(out_refs)
    width = unit_ref.shape[1]
    for step in sorted({k for k, _, _ in parts}):
        plane = (lax.axis_index("gx") + step) & (n_gx - 1)
        wanted = jnp.concatenate([asked_ref[plane * n_gy + d] for d in range(n_gy)], axis=0)
        row = wanted & (rows - 1)
        cluster = lax.shift_right_logical(wanted, log2(rows)).astype(F32).astype(BF16)
        low = (row & 255).astype(F32).astype(BF16)
        high = lax.shift_right_logical(row, 8).astype(F32).astype(BF16)
        index = dot_nt(pick, low) + 256.0 * dot_nt(pick, high)
        index = jnp.sum(jnp.where(own_col, index, 0.0), axis=1, keepdims=True).astype(I32)
        flat = jnp.sum(jnp.where(own_row, dot_nt(cluster, pick), 0.0), axis=0, keepdims=True)
        hot = one_hot(iota((chunk, rows), 1) == index)
        found = dot_nn(hot, unit_ref[...]).astype(BF16)
        for ref, (k, first, count) in zip(out_refs, parts):
            if k == step:
                ref[0:count, :] = found[first:first + count, :]
                line = [flat[:, first:first + count], jnp.zeros((1, width - count), F32)]
                ref[count:count + 1, :] = jnp.concatenate(line, axis=1).astype(BF16)


def column(line):
    parts = []
    for b in range(line.shape[1] // 128):
        wide = jnp.broadcast_to(line[:, b * 128:(b + 1) * 128], (128, 128))
        parts.append(wide.T)
    return jnp.concatenate(parts, axis=0)


def wide(col, lanes):
    return jnp.concatenate([col] * (lanes // 128), axis=1)


def length(parts):
    return sum(count for _, _, count in parts)


def cluster_line(ref, parts):
    size = length(parts)
    block = ref[size:size + len(parts), :].astype(F32)
    return jnp.concatenate([block[r:r + 1, 0:part[2]] for r, part in enumerate(parts)], axis=1)


def pack_kernel(groups, *refs):
    refs = list(refs)
    outs = refs[sum(len(g) for g in groups):]
    for group, out_ref in zip(groups, outs):
        at = 0
        total = sum(length(parts) for parts in group)
        width = out_ref.shape[1]
        lines = []
        for parts in group:
            ref, size = refs.pop(0), length(parts)
            out_ref[at:at + size, :] = ref[0:size, :]
            lines.append(ref[size:size + len(parts), :].astype(F32))
            at += size
        count = sum(len(parts) for parts in group)
        out_ref[total:total + count, :] = jnp.concatenate(lines, axis=0).astype(BF16)


def split_kernel(pieces, ref, *outs):
    total = sum(length(parts) for parts in pieces)
    at = 0
    row = total
    for parts, out_ref in zip(pieces, outs):
        size = length(parts)
        out_ref[0:size, :] = ref[at:at + size, :]
        out_ref[size:size + len(parts), :] = ref[row:row + len(parts), :]
        at += size
        row += len(parts)


def needed(one, two):
    (a, s), (b, t) = sorted([(n[0], int(n[-1])) for n in (one, two)], key=lambda n: "TNXY".index(n[0]))
    if a + b in ("TN", "TX"):
        return s >= t
    if a + b == "NX":
        return s == t or s < t < LAST or s == LAST
    if a + b == "TY":
        return s == LAST or t < LAST
    if a + b == "NY":
        return s == LAST and t < LAST
    return a + b in ("TT", "XY")


def cross(stack, held, inner, parts, refs, stack_ref, col_ref, best_ref):
    at = {}
    size = 0
    for n in stack:
        at[n] = size
        stack_ref[size:size + length(parts[n]), :] = refs[n][0:length(parts[n]), :]
        size += length(parts[n])
    col_ref[...] = column(jnp.concatenate([cluster_line(refs[n], parts[n]) for n in stack], axis=1))
    best_ref[...] = jnp.full((size, 128), -1.0, F32)
    lines = {}
    for k in held + (stack if inner else []):
        near = [n for n in stack if needed(n, k)]
        low = min(at[n] for n in near)
        high = max(at[n] + length(parts[n]) for n in near)
        n_k = length(parts[k])
        sims = dot_nt(stack_ref[low:high, :], refs[k][0:n_k, :])
        keep = wide(col_ref[low:high, :], n_k) == cluster_line(refs[k], parts[k])
        if k in stack:
            keep = keep & (iota((high - low, n_k), 0) + (low - at[k]) != iota((high - low, n_k), 1))
        sims = jnp.where(keep, sims, -1.0)
        best = best_ref[low:high, :]
        for v in range(n_k // 128):
            best = jnp.maximum(best, sims[:, v * 128:(v + 1) * 128])
        best_ref[low:high, :] = best
        if k not in stack:
            lines[k] = jnp.max(sims, axis=0, keepdims=True)
    for n in stack:
        lines[n] = lined(best_ref[at[n]:at[n] + length(parts[n]), :])
    return lines


def product_kernel(stack, held, inner, parts, *refs):
    names = stack + held
    refs = list(refs)
    rows = {n: refs.pop(0) for n in names}
    outs = {n: refs.pop(0) for n in names}
    for n, line in cross(stack, held, inner, parts, rows, *refs).items():
        outs[n][...] = line


def lined(best):
    rows = best.shape[0]
    parts = [jnp.max(best[b * 128:(b + 1) * 128, :].T, axis=0, keepdims=True) for b in range(rows // 128)]
    return jnp.concatenate(parts, axis=1)


def final_kernel(dims, kinds, stack, held, parts, known, *refs):
    n_gx, n_gy, rows, quota = dims
    chunk = n_gy * quota
    refs = list(refs)
    row_refs = {n: refs.pop(0) for n in stack + held}
    lines = {}
    for n in known:
        line = refs.pop(0)[...]
        lines[n] = jnp.maximum(lines[n], line) if n in lines else line
    send_ref = refs.pop(0)
    for n, line in cross(stack, held, True, parts, row_refs, *refs).items():
        lines[n] = jnp.maximum(lines[n], line) if n in lines else line
    whole = {}
    for n in sorted(lines):
        at = 0
        for k, first, count in parts[n]:
            whole.setdefault((n[:-1], k), {})[first] = lines[n][:, at:at + count]
            at += count
    blocks = [jnp.full((n_gy, 128), -1.0, F32)] * len(kinds)
    own = lax.shift_right_logical(iota((n_gy, chunk), 1), log2(quota)) == iota((n_gy, chunk), 0)
    lane = lax.shift_right_logical(iota((n_gy, 128), 1), log2(quota))
    for (kind, k), found in sorted(whole.items()):
        line = jnp.concatenate([found[first] for first in sorted(found)], axis=1)
        held_here = jnp.where(own, line, 0.0)
        fold = held_here[:, 0:128]
        for v in range(1, chunk // 128):
            fold = fold + held_here[:, v * 128:(v + 1) * 128]
        shift = 64
        while shift >= quota:
            fold = fold + pltpu.roll(fold, shift, 1)
            shift //= 2
        at = kinds.index(kind)
        blocks[at] = jnp.where(lane == k, fold, blocks[at])
    everything = jnp.concatenate(blocks, axis=1)
    for d in range(n_gy):
        send_ref[d] = everything[d:d + 1, :]


def far_place(q, m):
    row = q // KEYS
    return q ^ (KEYS * m) ^ (1 if row < row ^ m else 0)


def finish_kernel(dims, home_ref, back_ref, out_ref):
    n_gx, n_gy, rows, quota = dims
    n_query = n_gy // KEYS

    def taken(place, block):
        return jnp.concatenate([back_ref[place(q)][:, block * 128:(block + 1) * 128] for q in range(n_gy)], axis=0)

    found = taken(lambda q: q, 0)
    for m in range(1, n_query):
        found = jnp.maximum(found, taken(lambda q, m=m: far_place(q, m), m))
    for t in (1, 2):
        found = jnp.maximum(found, taken(lambda q, t=t: q ^ t, n_query - 1 + t))
    high = found.astype(BF16)
    rest = found - high.astype(F32)
    mid = rest.astype(BF16)
    low = (rest - mid.astype(F32)).astype(BF16)
    here = one_hot(iota((128, rows), 0) == home_ref[1:2, :])
    value = dot_nn(jnp.concatenate([high.astype(F32), mid.astype(F32), low.astype(F32)], axis=0).astype(BF16), here)
    value = (value[0:n_gy] + value[n_gy:2 * n_gy]) + value[2 * n_gy:3 * n_gy]
    own = iota((n_gy, rows), 0) == home_ref[0:1, :]
    out_ref[...] = jnp.sum(jnp.where(own, value, 0.0), axis=0, keepdims=True)


def shape(dims, dtype):
    return jax.ShapeDtypeStruct(dims, dtype)


def per_device(embeddings, members, sizes):
    rows = members.shape[0]
    width = embeddings.shape[1]
    n_gx = lax.axis_size("gx")
    n_gy = lax.axis_size("gy")
    owners = n_gx * n_gy
    quota = rows // owners
    chunk = n_gy * quota
    n_query = n_gy // KEYS
    dims = (n_gx, n_gy, rows, quota)
    in_vmem = pl.BlockSpec(memory_space=pltpu.VMEM)

    in_hbm = pl.BlockSpec(memory_space=pltpu.HBM)
    asked, home = pl.pallas_call(
        functools.partial(request_kernel, dims),
        out_shape=(shape((owners, 1, quota), I32), shape((2, rows), I32)),
        in_specs=[in_hbm, in_hbm],
        out_specs=(in_vmem, in_vmem),
        scratch_shapes=[
            pltpu.SMEM(sizes.shape, I32),
            pltpu.VMEM((1, rows), I32),
            pltpu.SemaphoreType.DMA((2,)),
        ],
        compiler_params=params(56 * 1024 * 1024),
        name="request",
    )(sizes, members.reshape(1, rows))
    asked = lax.all_to_all(asked, ("gx", "gy"), split_axis=0, concat_axis=0, tiled=True)

    values = embeddings.astype(F32)
    squared = jnp.sum(values * values, axis=1, keepdims=True)
    unit = (values * lax.rsqrt(squared + 1e-06)).astype(BF16)

    full = [(k, 0, chunk) for k in range(n_gx)]
    if n_gx == 4:
        rest = [[(2, 0, chunk // 2)], [(2, chunk // 2, chunk // 2)]]
    else:
        rest = [full[2:-3], full[-3:-1]]
    stages = [[full[0]], [full[1]], [full[-1]]] + rest
    far = ["Y%d" % m for m in range(1, n_query)]
    parts = {kind + str(s): stage for s, stage in enumerate(stages) for kind in ["T", "N", "X"] + far}
    piece = {}
    lines = []

    def meet(*arrays):
        return lax.optimization_barrier(arrays)

    found = {}
    for wanted in [stages[1], stages[0], stages[2] + stages[3] + stages[4]]:
        out = pl.pallas_call(
            functools.partial(select_kernel, dims, wanted),
            out_shape=[shape((count + (SPARE if k else 1), width), BF16) for k, _, count in wanted],
            in_specs=[in_vmem, in_vmem],
            out_specs=[in_vmem] * len(wanted),
            cost_estimate=cost(2 * len(wanted) * chunk * rows * width, rows * width),
            compiler_params=params(),
            name="select",
        )(asked, unit)
        unit, *out = meet(unit, *out)
        found.update(zip(wanted, out))

    def across(part):
        step = part[0]
        return lax.ppermute(found[part], "gx", [(i, (i + step) % n_gx) for i in range(n_gx)])

    def swap(array, mask):
        return lax.ppermute(array, "gy", [(i, i ^ mask) for i in range(n_gy)])

    def pack(arrays, groups):
        out_parts = sum(groups, [])
        return pl.pallas_call(
            functools.partial(pack_kernel, [groups]),
            out_shape=shape((length(out_parts) + len(out_parts), width), BF16),
            in_specs=[in_vmem] * len(arrays),
            out_specs=in_vmem,
            cost_estimate=cost(0, 4 * length(out_parts) * width),
            compiler_params=params(),
            name="pack",
        )(*arrays)

    def land(s, arrays):
        name = "T" + str(s)
        piece[name] = pack(arrays, [[part] for part in stages[s]])
        return name

    def near(s):
        own = piece["T" + str(s)]
        piece["X" + str(s)] = swap(own, 2)
        for m, kind in enumerate(far):
            piece[kind + str(s)] = lax.ppermute(own, "gy", [(q, far_place(q, m + 1)) for q in range(n_gy)])

    def join(names, arrays):
        out = list(meet(*[piece[n] for n in names], *arrays, *[line for _, line in lines]))
        for n in names:
            piece[n] = out.pop(0)
        arrays = [out.pop(0) for _ in arrays]
        lines[:] = [(n, out.pop(0)) for n, _ in lines]
        return arrays

    def scratch(stack):
        rows_in = sum(length(parts[n]) for n in stack)
        return [pltpu.VMEM((rows_in, width), BF16), pltpu.VMEM((rows_in, 128), F32), pltpu.VMEM((rows_in, 128), F32)]

    def products(stack, held, inner=True, weight=0.0):
        names = stack + held
        flops = 2 * width * sum(length(parts[n]) for n in stack) * sum(length(parts[n]) for n in names)
        out = pl.pallas_call(
            functools.partial(product_kernel, stack, held, inner, parts),
            out_shape=[shape((1, length(parts[n])), F32) for n in names],
            in_specs=[in_vmem] * len(names),
            out_specs=[in_vmem] * len(names),
            scratch_shapes=scratch(stack),
            cost_estimate=cost(int(weight * flops), 0),
            compiler_params=params(),
            name="products",
        )(*[piece[n] for n in names])
        lines.extend(zip(names, out))

    def kinds(letters, *numbers):
        out = []
        for n in numbers:
            for letter in letters:
                out += [kind + str(n) for kind in (far if letter == "Y" else [letter])]
        return out

    z1 = [across(part) for part in stages[1]]
    z2 = [across(part) for part in stages[2]]
    piece["T0"] = found[full[0]]
    near(0)
    piece["N0"] = swap(piece["T0"], 1)
    late = stages[3] + stages[4]
    *z1, = join(kinds("TNXY", 0), z1 + [found[part] for part in late])
    for part, array in zip(late, z1[1:]):
        found[part] = array
    z3 = [across(part) for part in stages[3]]
    z4 = [across(part) for part in stages[4]]
    land(1, z1[:1])
    near(1)
    piece["N1"] = swap(piece["T1"], 1)
    products(kinds("NY", 0) + ["T0", "T1", "X0"], [])
    z2 = join(kinds("TN", 1), z2)
    land(2, z2)
    near(2)
    products(kinds("NY", 1) + ["T2", "X1"], kinds("TNXY", 0) + ["T1"])
    z3 = join([], z3)
    land(3, z3)
    near(3)
    products(["T3"], kinds("TNXY", 0, 1) + ["T2"])
    products(kinds("YX", 2), kinds("TNXY", 0, 1) + ["T2", "T3"])
    z4 = join(["T2", "T3"], z4)
    land(4, z4)
    near(4)
    group = ["T2", "T3", "T4"]
    both = swap(pack([piece[n] for n in group], [parts[n] for n in group]), 1)
    cores = ["N2", "N3", "N4"]
    out = pl.pallas_call(
        functools.partial(split_kernel, [parts[n] for n in cores]),
        out_shape=[shape((length(parts[n]) + len(parts[n]), width), BF16) for n in cores],
        in_specs=[in_vmem],
        out_specs=[in_vmem] * len(cores),
        cost_estimate=cost(0, 0),
        compiler_params=params(),
        name="split",
    )(both)
    piece.update(zip(cores, out))
    products(kinds("Y", 3) + ["T4", "X3"], kinds("TNXY", 0, 1) + kinds("TXY", 2) + ["T3"], weight=WEIGHT)
    products(cores, kinds("XY", 0, 1, 2, 3) + ["T2", "T3", "T4"], inner=False)
    join(kinds("Y", 4), [])
    products(kinds("Y", 4), kinds("X", 0, 1, 2, 3) + ["T4"], inner=False)
    stack = kinds("YX", 4)
    held = kinds("Y", 0, 1, 2, 3) + ["T4", "N4"]
    shown = ["T"] + far + ["N", "X"]
    names = stack + held
    send = pl.pallas_call(
        functools.partial(final_kernel, dims, shown, stack, held, parts, [n for n, _ in lines]),
        out_shape=shape((n_gy, 1, len(shown) * 128), F32),
        in_specs=[in_vmem] * (len(names) + len(lines)),
        out_specs=in_vmem,
        scratch_shapes=scratch(stack),
        cost_estimate=cost(2 * width * chunk * 8 * chunk, 0),
        compiler_params=params(),
        name="final",
    )(*[piece[n] for n in names], *[line for _, line in lines])

    back = lax.all_to_all(send, "gy", split_axis=0, concat_axis=0, tiled=True)
    out = pl.pallas_call(
        functools.partial(finish_kernel, dims),
        out_shape=shape((1, rows), F32),
        in_specs=[in_vmem, in_vmem],
        out_specs=in_vmem,
        compiler_params=params(),
        name="finish",
    )(home, back)
    return out.reshape(rows)


def solution(mesh):
    return jax.shard_map(
        per_device,
        mesh=mesh,
        in_specs=(P(("gx", "gy"), None), P(("gx", "gy")), P("gx", None)),
        out_specs=P(("gx", "gy")),
        check_vma=False,
    )
```

```python
import functools

import jax
import jax.numpy as jnp
from jax import lax
from jax.experimental import pallas as pl
from jax.experimental.pallas import tpu as pltpu
from jax.sharding import PartitionSpec as P

F32 = jnp.float32
BF16 = jnp.bfloat16
I32 = jnp.int32
SPARE = 8
KEYS = 4
VMEM = 24 * 1024 * 1024
LAST = 4
WEIGHT = 20.0


def iota(shape, dim):
    return lax.broadcasted_iota(I32, shape, dim)


def dot_nt(a, b):
    return lax.dot_general(a, b, (((1,), (1,)), ((), ())), preferred_element_type=F32)


def dot_nn(a, b):
    return lax.dot_general(a, b, (((1,), (0,)), ((), ())), preferred_element_type=F32)


def one_hot(mask):
    return jnp.where(mask, 1.0, 0.0).astype(BF16)


def log2(value):
    assert value & (value - 1) == 0
    return value.bit_length() - 1


def params(limit=VMEM):
    return pltpu.CompilerParams(vmem_limit_bytes=limit)


def cost(flops, size):
    return pl.CostEstimate(flops=flops, bytes_accessed=size, transcendentals=0)


def request_kernel(dims, sizes_hbm, members_hbm, asked_ref, home_ref, sizes_ref, members_ref, sems):
    n_gx, n_gy, rows, quota = dims
    copies = [
        pltpu.make_async_copy(members_hbm, members_ref, sems.at[0]),
        pltpu.make_async_copy(sizes_hbm, sizes_ref, sems.at[1]),
    ]
    for copy in copies:
        copy.start()
    for copy in copies:
        copy.wait()
    owners = n_gx * n_gy
    member = members_ref[...]
    owner = lax.shift_right_logical(member, log2(rows))
    row = member & (rows - 1)
    slot = lax.axis_index("gy") * rows + iota((1, rows), 1)
    cluster = jnp.zeros((1, rows), I32)
    end = jnp.int32(0)
    for c in range(sizes_ref.shape[1]):
        end = end + sizes_ref[0, c]
        cluster = cluster + (slot >= end).astype(I32)
    mask = iota((owners, rows), 0) == owner
    hot = one_hot(mask)
    before = one_hot(iota((128, 128), 0) < iota((128, 128), 1))
    count = jnp.zeros((owners, 1), F32)
    ranks = []
    parts = [hot[:, b * 128:(b + 1) * 128] for b in range(rows // 128)]
    inner = dot_nn(jnp.concatenate(parts, axis=0), before)
    for b, part in enumerate(parts):
        rank = inner[b * owners:(b + 1) * owners, :] + count
        part32 = part.astype(F32)
        ranks.append(jnp.sum(part32 * rank, axis=0, keepdims=True))
        count = count + jnp.sum(part32, axis=1, keepdims=True)
    rank = jnp.concatenate(ranks, axis=1).astype(I32)
    place = one_hot(iota((quota, rows), 0) == rank)
    low = (row & 255).astype(F32)
    high = lax.shift_right_logical(row, 8).astype(F32)
    zero = jnp.zeros((owners, rows), F32)

    values = [jnp.where(mask, v, zero).astype(BF16) for v in (low, high, cluster.astype(F32))]
    picked = dot_nt(jnp.concatenate(values, axis=0), place)
    low, high, held = (picked[i * owners:(i + 1) * owners, :] for i in range(3))
    asked = (low + 256.0 * high).astype(I32)
    held = held.astype(I32)
    for o in range(owners):
        asked_ref[o] = jnp.concatenate([asked[o:o + 1, :], held[o:o + 1, :]], axis=0)
    plane = lax.shift_right_logical(owner, log2(n_gy))
    step = (lax.axis_index("gx") - plane) & (n_gx - 1)
    home_ref[0:1, :] = owner & (n_gy - 1)
    home_ref[1:2, :] = step * quota + rank


def select_kernel(dims, parts, asked_ref, unit_ref, *out_refs):
    n_gx, n_gy, rows, quota = dims
    chunk = n_gy * quota
    pick = one_hot((iota((chunk, quota), 0) & (quota - 1)) == iota((chunk, quota), 1))
    block = lax.shift_right_logical(iota((chunk, n_gy), 0), log2(quota))
    own_col = block == iota((chunk, n_gy), 1)
    block_row = lax.shift_right_logical(iota((n_gy, chunk), 1), log2(quota))
    own_row = block_row == iota((n_gy, chunk), 0)
    refs = list(out_refs)
    width = unit_ref.shape[1]
    for step in sorted({k for k, _, _ in parts}):
        plane = (lax.axis_index("gx") + step) & (n_gx - 1)
        row = jnp.concatenate([asked_ref[plane * n_gy + d, 0:1, :] for d in range(n_gy)], axis=0)
        cluster = jnp.concatenate([asked_ref[plane * n_gy + d, 1:2, :] for d in range(n_gy)], axis=0).astype(F32).astype(BF16)
        low = (row & 255).astype(F32).astype(BF16)
        high = lax.shift_right_logical(row, 8).astype(F32).astype(BF16)
        index = dot_nt(pick, low) + 256.0 * dot_nt(pick, high)
        index = jnp.sum(jnp.where(own_col, index, 0.0), axis=1, keepdims=True).astype(I32)
        flat = jnp.sum(jnp.where(own_row, dot_nt(cluster, pick), 0.0), axis=0, keepdims=True)
        hot = one_hot(iota((chunk, rows), 1) == index)
        found = dot_nn(hot, unit_ref[...]).astype(BF16)
        for ref, (k, first, count) in zip(out_refs, parts):
            if k == step:
                ref[0:count, :] = found[first:first + count, :]
                line = [flat[:, first:first + count], jnp.zeros((1, width - count), F32)]
                ref[count:count + 1, :] = jnp.concatenate(line, axis=1).astype(BF16)


def column(line):
    parts = []
    for b in range(line.shape[1] // 128):
        wide = jnp.broadcast_to(line[:, b * 128:(b + 1) * 128], (128, 128))
        parts.append(wide.T)
    return jnp.concatenate(parts, axis=0)


def wide(col, lanes):
    return jnp.concatenate([col] * (lanes // 128), axis=1)


def length(parts):
    return sum(count for _, _, count in parts)


def cluster_line(ref, parts):
    size = length(parts)
    block = ref[size:size + len(parts), :].astype(F32)
    return jnp.concatenate([block[r:r + 1, 0:part[2]] for r, part in enumerate(parts)], axis=1)


def pack_kernel(groups, *refs):
    refs = list(refs)
    outs = refs[sum(len(g) for g in groups):]
    for group, out_ref in zip(groups, outs):
        at = 0
        total = sum(length(parts) for parts in group)
        width = out_ref.shape[1]
        lines = []
        for parts in group:
            ref, size = refs.pop(0), length(parts)
            out_ref[at:at + size, :] = ref[0:size, :]
            lines.append(ref[size:size + len(parts), :].astype(F32))
            at += size
        count = sum(len(parts) for parts in group)
        out_ref[total:total + count, :] = jnp.concatenate(lines, axis=0).astype(BF16)


def split_kernel(pieces, ref, *outs):
    total = sum(length(parts) for parts in pieces)
    at = 0
    row = total
    for parts, out_ref in zip(pieces, outs):
        size = length(parts)
        out_ref[0:size, :] = ref[at:at + size, :]
        out_ref[size:size + len(parts), :] = ref[row:row + len(parts), :]
        at += size
        row += len(parts)


def needed(one, two):
    (a, s), (b, t) = sorted([(n[0], int(n[-1])) for n in (one, two)], key=lambda n: "TNXY".index(n[0]))
    if a + b in ("TN", "TX"):
        return s >= t
    if a + b == "NX":
        return s == t or s < t < LAST or s == LAST
    if a + b == "TY":
        return s == LAST or t < LAST
    if a + b == "NY":
        return s == LAST and t < LAST
    return a + b in ("TT", "XY")


def cross(stack, held, inner, parts, refs, stack_ref, col_ref, best_ref):
    at = {}
    size = 0
    for n in stack:
        at[n] = size
        stack_ref[size:size + length(parts[n]), :] = refs[n][0:length(parts[n]), :]
        size += length(parts[n])
    col_ref[...] = column(jnp.concatenate([cluster_line(refs[n], parts[n]) for n in stack], axis=1))
    best_ref[...] = jnp.full((size, 128), -1.0, F32)
    lines = {}
    for k in held + (stack if inner else []):
        near = [n for n in stack if needed(n, k)]
        low = min(at[n] for n in near)
        high = max(at[n] + length(parts[n]) for n in near)
        n_k = length(parts[k])
        sims = dot_nt(stack_ref[low:high, :], refs[k][0:n_k, :])
        keep = wide(col_ref[low:high, :], n_k) == cluster_line(refs[k], parts[k])
        if k in stack:
            keep = keep & (iota((high - low, n_k), 0) + (low - at[k]) != iota((high - low, n_k), 1))
        sims = jnp.where(keep, sims, -1.0)
        best = best_ref[low:high, :]
        for v in range(n_k // 128):
            best = jnp.maximum(best, sims[:, v * 128:(v + 1) * 128])
        best_ref[low:high, :] = best
        if k not in stack:
            lines[k] = jnp.max(sims, axis=0, keepdims=True)
    for n in stack:
        lines[n] = lined(best_ref[at[n]:at[n] + length(parts[n]), :])
    return lines


def product_kernel(stack, held, inner, parts, *refs):
    names = stack + held
    refs = list(refs)
    rows = {n: refs.pop(0) for n in names}
    outs = {n: refs.pop(0) for n in names}
    for n, line in cross(stack, held, inner, parts, rows, *refs).items():
        outs[n][...] = line


def lined(best):
    rows = best.shape[0]
    parts = [jnp.max(best[b * 128:(b + 1) * 128, :].T, axis=0, keepdims=True) for b in range(rows // 128)]
    return jnp.concatenate(parts, axis=1)


def final_kernel(dims, kinds, stack, held, parts, known, *refs):
    n_gx, n_gy, rows, quota = dims
    chunk = n_gy * quota
    refs = list(refs)
    row_refs = {n: refs.pop(0) for n in stack + held}
    lines = {}
    for n in known:
        line = refs.pop(0)[...]
        lines[n] = jnp.maximum(lines[n], line) if n in lines else line
    send_ref = refs.pop(0)
    for n, line in cross(stack, held, True, parts, row_refs, *refs).items():
        lines[n] = jnp.maximum(lines[n], line) if n in lines else line
    whole = {}
    for n in sorted(lines):
        at = 0
        for k, first, count in parts[n]:
            whole.setdefault((n[:-1], k), {})[first] = lines[n][:, at:at + count]
            at += count
    blocks = [jnp.full((n_gy, 128), -1.0, F32)] * len(kinds)
    own = lax.shift_right_logical(iota((n_gy, chunk), 1), log2(quota)) == iota((n_gy, chunk), 0)
    lane = lax.shift_right_logical(iota((n_gy, 128), 1), log2(quota))
    for (kind, k), found in sorted(whole.items()):
        line = jnp.concatenate([found[first] for first in sorted(found)], axis=1)
        held_here = jnp.where(own, line, 0.0)
        fold = held_here[:, 0:128]
        for v in range(1, chunk // 128):
            fold = fold + held_here[:, v * 128:(v + 1) * 128]
        shift = 64
        while shift >= quota:
            fold = fold + pltpu.roll(fold, shift, 1)
            shift //= 2
        at = kinds.index(kind)
        blocks[at] = jnp.where(lane == k, fold, blocks[at])
    everything = jnp.concatenate(blocks, axis=1)
    for d in range(n_gy):
        send_ref[d] = everything[d:d + 1, :]


def far_place(q, m):
    row = q // KEYS
    return q ^ (KEYS * m) ^ (1 if row < row ^ m else 0)


def finish_kernel(dims, home_ref, back_ref, out_ref):
    n_gx, n_gy, rows, quota = dims
    n_query = n_gy // KEYS

    def taken(place, block):
        return jnp.concatenate([back_ref[place(q)][:, block * 128:(block + 1) * 128] for q in range(n_gy)], axis=0)

    found = taken(lambda q: q, 0)
    for m in range(1, n_query):
        found = jnp.maximum(found, taken(lambda q, m=m: far_place(q, m), m))
    for t in (1, 2):
        found = jnp.maximum(found, taken(lambda q, t=t: q ^ t, n_query - 1 + t))
    high = found.astype(BF16)
    rest = found - high.astype(F32)
    mid = rest.astype(BF16)
    low = (rest - mid.astype(F32)).astype(BF16)
    here = one_hot(iota((128, rows), 0) == home_ref[1:2, :])
    value = dot_nn(jnp.concatenate([high.astype(F32), mid.astype(F32), low.astype(F32)], axis=0).astype(BF16), here)
    value = (value[0:n_gy] + value[n_gy:2 * n_gy]) + value[2 * n_gy:3 * n_gy]
    own = iota((n_gy, rows), 0) == home_ref[0:1, :]
    out_ref[...] = jnp.sum(jnp.where(own, value, 0.0), axis=0, keepdims=True)


def shape(dims, dtype):
    return jax.ShapeDtypeStruct(dims, dtype)


def per_device(embeddings, members, sizes):
    rows = members.shape[0]
    width = embeddings.shape[1]
    n_gx = lax.axis_size("gx")
    n_gy = lax.axis_size("gy")
    owners = n_gx * n_gy
    quota = rows // owners
    chunk = n_gy * quota
    n_query = n_gy // KEYS
    dims = (n_gx, n_gy, rows, quota)
    in_vmem = pl.BlockSpec(memory_space=pltpu.VMEM)

    in_hbm = pl.BlockSpec(memory_space=pltpu.HBM)
    asked, home = pl.pallas_call(
        functools.partial(request_kernel, dims),
        out_shape=(shape((owners, 2, quota), I32), shape((2, rows), I32)),
        in_specs=[in_hbm, in_hbm],
        out_specs=(in_vmem, in_vmem),
        scratch_shapes=[
            pltpu.SMEM(sizes.shape, I32),
            pltpu.VMEM((1, rows), I32),
            pltpu.SemaphoreType.DMA((2,)),
        ],
        compiler_params=params(56 * 1024 * 1024),
        name="request",
    )(sizes, members.reshape(1, rows))
    asked = lax.all_to_all(asked, ("gx", "gy"), split_axis=0, concat_axis=0, tiled=True)

    values = embeddings.astype(F32)
    squared = jnp.sum(values * values, axis=1, keepdims=True)
    unit = (values * lax.rsqrt(squared + 1e-06)).astype(BF16)

    full = [(k, 0, chunk) for k in range(n_gx)]
    if n_gx == 4:
        rest = [[(2, 0, chunk // 2)], [(2, chunk // 2, chunk // 2)]]
    else:
        rest = [full[2:-3], full[-3:-1]]
    stages = [[full[0]], [full[1]], [full[-1]]] + rest
    far = ["Y%d" % m for m in range(1, n_query)]
    parts = {kind + str(s): stage for s, stage in enumerate(stages) for kind in ["T", "N", "X"] + far}
    piece = {}
    lines = []

    def meet(*arrays):
        return lax.optimization_barrier(arrays)

    found = {}
    for wanted in [stages[1], stages[0], stages[2] + stages[3] + stages[4]]:
        out = pl.pallas_call(
            functools.partial(select_kernel, dims, wanted),
            out_shape=[shape((count + (SPARE if k else 1), width), BF16) for k, _, count in wanted],
            in_specs=[in_vmem, in_vmem],
            out_specs=[in_vmem] * len(wanted),
            cost_estimate=cost(2 * len(wanted) * chunk * rows * width, rows * width),
            compiler_params=params(),
            name="select",
        )(asked, unit)
        unit, *out = meet(unit, *out)
        found.update(zip(wanted, out))

    def across(part):
        step = part[0]
        return lax.ppermute(found[part], "gx", [(i, (i + step) % n_gx) for i in range(n_gx)])

    def swap(array, mask):
        return lax.ppermute(array, "gy", [(i, i ^ mask) for i in range(n_gy)])

    def pack(arrays, groups):
        out_parts = sum(groups, [])
        return pl.pallas_call(
            functools.partial(pack_kernel, [groups]),
            out_shape=shape((length(out_parts) + len(out_parts), width), BF16),
            in_specs=[in_vmem] * len(arrays),
            out_specs=in_vmem,
            cost_estimate=cost(0, 4 * length(out_parts) * width),
            compiler_params=params(),
            name="pack",
        )(*arrays)

    def land(s, arrays):
        name = "T" + str(s)
        piece[name] = pack(arrays, [[part] for part in stages[s]])
        return name

    def near(s):
        own = piece["T" + str(s)]
        piece["X" + str(s)] = swap(own, 2)
        for m, kind in enumerate(far):
            piece[kind + str(s)] = lax.ppermute(own, "gy", [(q, far_place(q, m + 1)) for q in range(n_gy)])

    def join(names, arrays):
        out = list(meet(*[piece[n] for n in names], *arrays, *[line for _, line in lines]))
        for n in names:
            piece[n] = out.pop(0)
        arrays = [out.pop(0) for _ in arrays]
        lines[:] = [(n, out.pop(0)) for n, _ in lines]
        return arrays

    def scratch(stack):
        rows_in = sum(length(parts[n]) for n in stack)
        return [pltpu.VMEM((rows_in, width), BF16), pltpu.VMEM((rows_in, 128), F32), pltpu.VMEM((rows_in, 128), F32)]

    def products(stack, held, inner=True, weight=0.0):
        names = stack + held
        flops = 2 * width * sum(length(parts[n]) for n in stack) * sum(length(parts[n]) for n in names)
        out = pl.pallas_call(
            functools.partial(product_kernel, stack, held, inner, parts),
            out_shape=[shape((1, length(parts[n])), F32) for n in names],
            in_specs=[in_vmem] * len(names),
            out_specs=[in_vmem] * len(names),
            scratch_shapes=scratch(stack),
            cost_estimate=cost(int(weight * flops), 0),
            compiler_params=params(),
            name="products",
        )(*[piece[n] for n in names])
        lines.extend(zip(names, out))

    def kinds(letters, *numbers):
        out = []
        for n in numbers:
            for letter in letters:
                out += [kind + str(n) for kind in (far if letter == "Y" else [letter])]
        return out

    z1 = [across(part) for part in stages[1]]
    z2 = [across(part) for part in stages[2]]
    piece["T0"] = found[full[0]]
    near(0)
    piece["N0"] = swap(piece["T0"], 1)
    late = stages[3] + stages[4]
    *z1, = join(kinds("TNXY", 0), z1 + [found[part] for part in late])
    for part, array in zip(late, z1[1:]):
        found[part] = array
    z3 = [across(part) for part in stages[3]]
    z4 = [across(part) for part in stages[4]]
    land(1, z1[:1])
    near(1)
    piece["N1"] = swap(piece["T1"], 1)
    products(kinds("NY", 0) + ["T0", "T1", "X0"], [])
    z2 = join(kinds("TN", 1), z2)
    land(2, z2)
    near(2)
    products(kinds("NY", 1) + ["T2", "X1"], kinds("TNXY", 0) + ["T1"])
    z3 = join([], z3)
    land(3, z3)
    near(3)
    products(["T3"], kinds("TNXY", 0, 1) + ["T2"])
    products(kinds("YX", 2), kinds("TNXY", 0, 1) + ["T2", "T3"])
    z4 = join(["T2", "T3"], z4)
    land(4, z4)
    near(4)
    group = ["T2", "T3", "T4"]
    both = swap(pack([piece[n] for n in group], [parts[n] for n in group]), 1)
    cores = ["N2", "N3", "N4"]
    out = pl.pallas_call(
        functools.partial(split_kernel, [parts[n] for n in cores]),
        out_shape=[shape((length(parts[n]) + len(parts[n]), width), BF16) for n in cores],
        in_specs=[in_vmem],
        out_specs=[in_vmem] * len(cores),
        cost_estimate=cost(0, 0),
        compiler_params=params(),
        name="split",
    )(both)
    piece.update(zip(cores, out))
    products(kinds("Y", 3) + ["T4", "X3"], kinds("TNXY", 0, 1) + kinds("TXY", 2) + ["T3"], weight=WEIGHT)
    products(cores, kinds("XY", 0, 1, 2, 3) + ["T2", "T3", "T4"], inner=False)
    join(kinds("Y", 4), [])
    products(kinds("Y", 4), kinds("X", 0, 1, 2, 3) + ["T4"], inner=False)
    stack = kinds("YX", 4)
    held = kinds("Y", 0, 1, 2, 3) + ["T4", "N4"]
    shown = ["T"] + far + ["N", "X"]
    names = stack + held
    send = pl.pallas_call(
        functools.partial(final_kernel, dims, shown, stack, held, parts, [n for n, _ in lines]),
        out_shape=shape((n_gy, 1, len(shown) * 128), F32),
        in_specs=[in_vmem] * (len(names) + len(lines)),
        out_specs=in_vmem,
        scratch_shapes=scratch(stack),
        cost_estimate=cost(2 * width * chunk * 8 * chunk, 0),
        compiler_params=params(),
        name="final",
    )(*[piece[n] for n in names], *[line for _, line in lines])

    back = lax.all_to_all(send, "gy", split_axis=0, concat_axis=0, tiled=True)
    out = pl.pallas_call(
        functools.partial(finish_kernel, dims),
        out_shape=shape((1, rows), F32),
        in_specs=[in_vmem, in_vmem],
        out_specs=in_vmem,
        compiler_params=params(),
        name="finish",
    )(home, back)
    return out.reshape(rows)


def solution(mesh):
    return jax.shard_map(
        per_device,
        mesh=mesh,
        in_specs=(P(("gx", "gy"), None), P(("gx", "gy")), P("gx", None)),
        out_specs=P(("gx", "gy")),
        check_vma=False,
    )
```
